32 devices in a mesh: groups: 2 (over x), blk: 16 (over z, y, core).
Axes of the slice: x: 2, y: 2, z: 4, core: 2. Of those that a mesh axis runs over, the one named last changes fastest.
Arguments:
- features: float32 [64, 16384], P(None, ('groups', 'blk')), parts along dimension 1, may hold values from -6 to 6
- solves: float32 [16, 16384], P(None, ('groups', 'blk')), parts along dimension 1, may hold values from -6 to 6
- probes: float32 [16, 16384], P(None, ('groups', 'blk')), parts along dimension 1, may hold values from -6 to 6
Outputs:
- feature_grad: float32 [64, 16384], P(None, ('groups', 'blk')), parts along dimension 1
The draws below stay inside these ranges and needn't reach their ends.
There are 2 independent parts, one for each index of `groups`. The reference program is written for one: setup_inputs(seed, part) draws one part's arguments, and reference() takes and returns one part's arrays. A program takes and returns all parts, laid end to end along the dimension named above; each array names one. Nothing has to cross between parts.
All inputs are finite; a program needn't handle non-finite values.
Results may differ from the reference program's by a relative error of at most 0.0003.
Values sent between devices are 32-bit elements; how exact they have to be, the bound alone decides.
No kernel may reach another device: no remote copies, remote signals or barrier semaphores. Data moves between devices by JAX's collectives and lax.ppermute only.
A program may use at most 64 MiB of HBM per device.

```python
import jax
import jax.numpy as jnp
from jax import lax

DF = 64
PROBES = 16
R = 512
N = 8192
N_BLK = 16


def block_scale(key, extent, cuts, low, high):
    level = 1.0
    for dim, parts in cuts:
        draws = jax.random.uniform(jax.random.fold_in(jax.random.fold_in(key, 6), dim), (parts,), jnp.float32, low / len(cuts), high / len(cuts))
        level = level * jnp.repeat(jnp.exp(draws), extent[dim] // parts).reshape((-1,) + (1,) * (len(extent) - 1 - dim))
    return level


def gaussian(key, extent, scale, reach, shards=(), held_as=jnp.bfloat16):
    drawn = scale * jax.random.normal(key, extent, jnp.float32)
    if shards:
        drawn = drawn * block_scale(key, extent, shards, -0.22, 0.18)
    return jnp.clip(drawn, -reach, reach).astype(held_as)


def setup_inputs(seed: int = 0, part: int = 0) -> dict:
    seeds = jax.random.split(jax.random.key(seed), 4)
    part_splits = jax.random.split(jax.random.fold_in(seeds[3], part), 4)
    features = gaussian(part_splits[0], (DF, N), 1.0, 6.0, ((1, 16),), jnp.float32)
    solves = gaussian(part_splits[1], (PROBES, N), 1.0, 6.0, ((1, 16),), jnp.float32)
    probes = gaussian(part_splits[2], (PROBES, N), 1.0, 6.0, ((1, 16),), jnp.float32)
    return {"features": features, "solves": solves, "probes": probes}


def term_weights(vectors):
    position = jnp.arange(vectors)
    return jnp.where(position == 0, 0.5, -0.5 / (vectors - 1)).astype(jnp.float32)


def reference(features, solves, probes):
    weights = term_weights(PROBES)[:, None]
    squares = jnp.sum(features * features, axis=0)
    lefthand = jnp.concatenate([solves, probes], 0)
    righthand = jnp.concatenate([weights * probes, weights * solves], 0)
    highest = lax.Precision.HIGHEST

    def one_block(block):
        start = (block * R).astype(jnp.int32)
        feat_block = lax.dynamic_slice_in_dim(features, start, R, 1)
        left_block = lax.dynamic_slice_in_dim(lefthand, start, R, 1)
        square_block = lax.dynamic_slice_in_dim(squares, start, R, 0)
        inner = lax.dot_general(feat_block, features, (((0,), (0,)), ((), ())), precision=highest)
        distance = square_block[:, None] + squares[None, :] - 2.0 * inner
        kernel = jnp.exp(-distance / (2.0 * DF))
        coupling = lax.dot_general(left_block, righthand, (((0,), (0,)), ((), ())), precision=highest) * kernel
        pulled = lax.dot_general(features, coupling, (((1,), (1,)), ((), ())), precision=highest)
        return -(feat_block * jnp.sum(coupling, axis=1)[None, :] - pulled) / DF

    stacked = lax.map(one_block, jnp.arange(N_BLK, dtype=jnp.int32))
    return jnp.transpose(stacked, (1, 0, 2)).reshape(DF, N)
```

```python
import functools

import jax
import jax.numpy as jnp
from jax import lax
from jax.experimental import pallas as pl
from jax.experimental.pallas import tpu as pltpu
from jax.sharding import PartitionSpec as P

LOG2E = 1.4426950408889634
NORM_ROWS = 16


def split2(value):
    high = value.astype(jnp.bfloat16)
    low = (value - high.astype(jnp.float32)).astype(jnp.bfloat16)
    return high, low


def split3(value):
    high = value.astype(jnp.bfloat16).astype(jnp.float32)
    rest = value - high
    mid = rest.astype(jnp.bfloat16).astype(jnp.float32)
    return high, mid, rest - mid


def term_weights(vectors):
    position = lax.broadcasted_iota(jnp.int32, (2 * vectors, 1), 0)
    first = (position == 0) | (position == vectors)
    return jnp.where(first, 0.5, -0.5 / (vectors - 1)).astype(jnp.float32)


def norm_rows(norms, first):
    parts = split3(norms)
    points = norms.shape[1]
    row = lax.broadcasted_iota(jnp.int32, (NORM_ROWS, points), 0)
    at, ones = (0, 3) if first else (3, 0)
    rows = jnp.where((row >= ones) & (row < ones + 3), 1.0, 0.0)
    for place, part in enumerate(parts):
        rows = jnp.where(row == at + place, part, rows)
    return rows


def prepare_mine(mine, width, vectors, dist_ref, pair_ref):
    feat = mine[:width]
    scale = LOG2E / (2.0 * width)
    norms = jnp.sum(feat * feat, axis=0, keepdims=True) * -scale
    scaled = feat * (2.0 * scale)
    high = scaled.astype(jnp.bfloat16).astype(jnp.float32)
    low = scaled - high
    dist = jnp.concatenate([high, low, high, norm_rows(norms, True)], 0)
    dist_ref[...] = dist.T.astype(jnp.bfloat16)
    vecs = mine[width:] * term_weights(vectors)
    high = vecs.astype(jnp.bfloat16).astype(jnp.float32)
    low = vecs - high
    pair_ref[...] = jnp.concatenate([high, low, high], 0).T.astype(jnp.bfloat16)


def prepare_theirs(theirs, width, vectors):
    feat = theirs[:width]
    scale = LOG2E / (2.0 * width)
    points = feat.shape[1]
    norms = jnp.sum(feat * feat, axis=0, keepdims=True) * -scale
    high, low = split2(feat)
    norms = norm_rows(norms, False).astype(jnp.bfloat16)
    dist = jnp.concatenate([high, high, low, norms], 0)
    vecs = jnp.concatenate([theirs[width + vectors :], theirs[width : width + vectors]], 0)
    vec_high, vec_low = split2(vecs)
    pair = jnp.concatenate([vec_high, vec_high, vec_low], 0)
    pull = jnp.concatenate([high, low, jnp.ones((2 * width, points), jnp.bfloat16)], 0)
    return dist, pair, pull


def kernel(width, vectors, chunk, mine_ref, theirs_ref, out_ref, dist_ref, pair_ref, acc_ref):
    step = pl.program_id(0)

    @pl.when(step == 0)
    def _():
        prepare_mine(mine_ref[...], width, vectors, dist_ref, pair_ref)
        acc_ref[...] = jnp.zeros_like(acc_ref)

    dist, pair, pull = prepare_theirs(theirs_ref[0], width, vectors)
    points = mine_ref.shape[1]
    for start in range(0, points, chunk):
        rows = pl.ds(start, chunk)
        power = jnp.dot(dist_ref[rows], dist, preferred_element_type=jnp.float32)
        bilinear = jnp.dot(pair_ref[rows], pair, preferred_element_type=jnp.float32)
        coupling = jnp.exp2(power) * bilinear
        high, low = split2(coupling)
        across = (((1,), (1,)), ((), ()))
        acc_ref[rows] += lax.dot_general(
            high, pull, across, preferred_element_type=jnp.float32
        ) + lax.dot_general(low, pull, across, preferred_element_type=jnp.float32)

    @pl.when(step == pl.num_programs(0) - 1)
    def _():
        total = acc_ref[...].T
        pulled = total[:width] + total[width : 2 * width]
        sums = total[2 * width : 2 * width + 1]
        out_ref[...] = -(mine_ref[:width] * sums - pulled) / width


def pair_terms(mine, gathered, width, vectors):
    points = mine.shape[1]
    depth = mine.shape[0]
    blocks = gathered.shape[0]
    pairs = points * points * blocks
    return pl.pallas_call(
        functools.partial(kernel, width, vectors, min(256, points)),
        grid=(blocks,),
        in_specs=[
            pl.BlockSpec((depth, points), lambda b: (0, 0)),
            pl.BlockSpec((1, depth, points), lambda b: (b, 0, 0)),
        ],
        out_specs=pl.BlockSpec((width, points), lambda b: (0, 0)),
        out_shape=jax.ShapeDtypeStruct((width, points), jnp.float32),
        scratch_shapes=[
            pltpu.VMEM((points, 3 * width + NORM_ROWS), jnp.bfloat16),
            pltpu.VMEM((points, 6 * vectors), jnp.bfloat16),
            pltpu.VMEM((points, 4 * width), jnp.float32),
        ],
        compiler_params=pltpu.CompilerParams(vmem_limit_bytes=32 << 20),
        cost_estimate=pl.CostEstimate(
            flops=2 * pairs * 1024, bytes_accessed=4 * depth * points * blocks, transcendentals=pairs
        ),
    )(mine, gathered)


def local(features, solves, probes):
    width = features.shape[0]
    vectors = solves.shape[0]
    mine = jnp.concatenate([features, solves, probes], 0)
    gathered = lax.all_gather(mine, "blk")
    return pair_terms(mine, gathered, width, vectors)


def solution(mesh):
    in_specs = (P(None, ("groups", "blk")), P(None, ("groups", "blk")), P(None, ("groups", "blk")))
    out_specs = P(None, ("groups", "blk"))
    return jax.shard_map(local, mesh=mesh, in_specs=in_specs, out_specs=out_specs, check_vma=False)
```

```python
import functools

import jax
import jax.numpy as jnp
from jax import lax
from jax.experimental import pallas as pl
from jax.experimental.pallas import tpu as pltpu
from jax.sharding import PartitionSpec as P

LOG2E = 1.4426950408889634
NORM_ROWS = 16
VMEM_LIMIT = 40 << 20


def swapped(value, axis, bit):
    count = lax.axis_size(axis)
    return lax.ppermute(value, axis, [(source, source ^ bit) for source in range(count)])


def split2(value):
    high = value.astype(jnp.bfloat16)
    low = (value - high.astype(jnp.float32)).astype(jnp.bfloat16)
    return high, low


def term_weights(vectors):
    position = lax.broadcasted_iota(jnp.int32, (2 * vectors, 1), 0)
    first = (position == 0) | (position == vectors)
    return jnp.where(first, 0.5, -0.5 / (vectors - 1)).astype(jnp.float32)


def norm_rows(norms, first):
    high = norms.astype(jnp.bfloat16).astype(jnp.float32)
    rest = norms - high
    mid = rest.astype(jnp.bfloat16).astype(jnp.float32)
    row = lax.broadcasted_iota(jnp.int32, (NORM_ROWS, norms.shape[1]), 0)
    at, ones = (0, 3) if first else (3, 0)
    rows = jnp.where((row >= ones) & (row < ones + 3), 1.0, 0.0)
    for place, part in enumerate((high, mid, rest - mid)):
        rows = jnp.where(row == at + place, part, rows)
    return rows.astype(jnp.bfloat16)


def prepared_rows(block, width, vectors):
    feat = block[:width]
    scale = LOG2E / (2.0 * width)
    norms = jnp.sum(feat * feat, axis=0, keepdims=True) * -scale
    high, low = split2(feat * (2.0 * scale))
    dist = jnp.concatenate([high, low, high, norm_rows(norms, True)], 0)
    high, low = split2(block[width:] * term_weights(vectors))
    pair = jnp.concatenate([high, low, high], 0)
    return dist.T, pair.T


def prepared_columns(block, width, vectors):
    feat = block[:width]
    scale = LOG2E / (2.0 * width)
    norms = jnp.sum(feat * feat, axis=0, keepdims=True) * -scale
    high, low = split2(feat)
    dist = jnp.concatenate([high, high, low, norm_rows(norms, False)], 0)
    vecs = jnp.concatenate([block[width + vectors :], block[width : width + vectors]], 0)
    vec_high, vec_low = split2(vecs)
    pair = jnp.concatenate([vec_high, vec_high, vec_low], 0)
    ones = jnp.ones((2 * width, block.shape[1]), jnp.bfloat16)
    pull = jnp.concatenate([high, low, ones], 0)
    return dist, pair, pull


def block_terms(dist_rows, pair_rows, columns):
    across = (((1,), (1,)), ((), ()))
    total = None
    for dist, pair, pull in columns:
        power = jnp.dot(dist_rows, dist, preferred_element_type=jnp.float32)
        bilinear = jnp.dot(pair_rows, pair, preferred_element_type=jnp.float32)
        high, low = split2(jnp.exp2(power) * bilinear)
        for half in (high, low):
            term = lax.dot_general(half, pull, across, preferred_element_type=jnp.float32)
            total = term if total is None else total + term
    return total


def kernel(width, vectors, chunk, rows, columns, fresh, started, *refs):
    refs = list(refs)
    take = lambda count: [refs.pop(0) for _ in range(count)]
    row_refs = take(rows)
    column_refs = take(columns)
    ready = [] if fresh else take(2 * rows)
    before = take(rows) if started else []
    out = take(rows)
    made = take(2 * rows) if fresh else ready
    prepared = [prepared_columns(ref[...], width, vectors) for ref in column_refs]
    for place in range(rows):
        dist_ref, pair_ref = made[2 * place : 2 * place + 2]
        if fresh:
            dist_ref[...], pair_ref[...] = prepared_rows(row_refs[place][...], width, vectors)
        points = row_refs[place].shape[1]
        for start in range(0, points, chunk):
            span = pl.ds(start, chunk)
            total = block_terms(dist_ref[span], pair_ref[span], prepared).T
            pulled = total[:width] + total[width : 2 * width]
            sums = total[2 * width : 2 * width + 1]
            value = (pulled - row_refs[place][:width, span] * sums) / width
            if started:
                value += before[place][:, span]
            out[place][:, span] = value


def pair_terms(row_blocks, column_blocks, width, vectors, ready=None, before=None):
    points = row_blocks[0].shape[1]
    rows, columns = len(row_blocks), len(column_blocks)
    fresh, started = ready is None, before is not None
    shape = jax.ShapeDtypeStruct
    out_shape = [shape((width, points), jnp.float32)] * rows
    if fresh:
        out_shape += [
            shape((points, 3 * width + NORM_ROWS), jnp.bfloat16),
            shape((points, 6 * vectors), jnp.bfloat16),
        ] * rows
    operands = list(row_blocks) + list(column_blocks) + (ready or []) + (before or [])
    pairs = points * points * rows * columns
    results = pl.pallas_call(
        functools.partial(
            kernel, width, vectors, min(512, points), rows, columns, fresh, started
        ),
        out_shape=out_shape,
        in_specs=[pl.BlockSpec(memory_space=pltpu.VMEM)] * len(operands),
        out_specs=[pl.BlockSpec(memory_space=pltpu.VMEM)] * len(out_shape),
        compiler_params=pltpu.CompilerParams(vmem_limit_bytes=VMEM_LIMIT),
        cost_estimate=pl.CostEstimate(
            flops=2 * pairs * 1024,
            bytes_accessed=4 * points * 96 * (rows + columns),
            transcendentals=pairs,
        ),
    )(*operands)
    results = list(results)
    return results[:rows], results[rows:] if fresh else ready


def packed(features, solves, probes):
    width, points = features.shape
    vectors = solves.shape[0]

    def body(features_ref, solves_ref, probes_ref, out_ref):
        out_ref[:width] = features_ref[...]
        out_ref[width : width + vectors] = solves_ref[...]
        out_ref[width + vectors :] = probes_ref[...]

    return pl.pallas_call(
        body, out_shape=jax.ShapeDtypeStruct((width + 2 * vectors, points), jnp.float32)
    )(features, solves, probes)


def local(features, solves, probes):
    width = features.shape[0]
    vectors = solves.shape[0]
    count = lax.axis_size("blk")
    terms = functools.partial(pair_terms, width=width, vectors=vectors)
    swap = lambda value, bit: swapped(value, "blk", bit)

    mine = packed(features, solves, probes)
    sibling = swap(mine, 1)
    bits = [bit for bit in (1 << place for place in range(2, count.bit_length())) if bit < count]
    far = swap(mine, bits[-1])
    near = swap(mine, 2)
    direct = {bit: swap(mine, bit) for bit in bits[:-1]}

    here, ready_here = terms([mine, sibling], [mine])
    near, here = lax.optimization_barrier((near, here))
    near_sibling = swap(near, 1)
    there, ready_there = terms([near, near_sibling], [mine])
    far, there = lax.optimization_barrier((far, there))
    columns = [mine, far]
    for bit in reversed(bits[:-1]):
        columns += [direct[bit]] + [swap(block, bit) for block in columns[1:]]
    middle, last = columns[1:-1], columns[-1:]
    for start in range(0, len(middle), 2):
        both, _ = terms(
            [mine, sibling, near, near_sibling],
            middle[start : start + 2],
            ready=ready_here + ready_there,
            before=here + there,
        )
        here, there = both[:2], both[2:]
    there, _ = terms([near, near_sibling], last, ready=ready_there, before=there)
    here, _ = terms([mine, sibling], last, ready=ready_here, before=here)

    toward_near = there[0] + swap(there[1], 1)
    from_near = swap(toward_near, 2)
    return here[0] + swap(here[1], 1) + from_near


def solution(mesh):
    in_specs = (P(None, ("groups", "blk")), P(None, ("groups", "blk")), P(None, ("groups", "blk")))
    out_specs = P(None, ("groups", "blk"))
    return jax.shard_map(local, mesh=mesh, in_specs=in_specs, out_specs=out_specs, check_vma=False)
```

```python
import functools

import jax
import jax.numpy as jnp
from jax import lax
from jax.experimental import pallas as pl
from jax.experimental.pallas import tpu as pltpu
from jax.sharding import PartitionSpec as P

LOG2E = 1.4426950408889634
NORM_ROWS = 16
VMEM_LIMIT = 40 << 20


def swapped(value, axis, bit):
    count = lax.axis_size(axis)
    return lax.ppermute(value, axis, [(source, source ^ bit) for source in range(count)])


def split2(value):
    high = value.astype(jnp.bfloat16)
    low = (value - high.astype(jnp.float32)).astype(jnp.bfloat16)
    return high, low


def term_weights(vectors):
    position = lax.broadcasted_iota(jnp.int32, (2 * vectors, 1), 0)
    first = (position == 0) | (position == vectors)
    return jnp.where(first, 0.5, -0.5 / (vectors - 1)).astype(jnp.float32)


def norm_rows(norms, first):
    high = norms.astype(jnp.bfloat16).astype(jnp.float32)
    rest = norms - high
    mid = rest.astype(jnp.bfloat16).astype(jnp.float32)
    row = lax.broadcasted_iota(jnp.int32, (NORM_ROWS, norms.shape[1]), 0)
    at, ones = (0, 3) if first else (3, 0)
    rows = jnp.where((row >= ones) & (row < ones + 3), 1.0, 0.0)
    for place, part in enumerate((high, mid, rest - mid)):
        rows = jnp.where(row == at + place, part, rows)
    return rows.astype(jnp.bfloat16)


def prepared_rows(block, width, vectors):
    feat = block[:width]
    scale = LOG2E / (2.0 * width)
    norms = jnp.sum(feat * feat, axis=0, keepdims=True) * -scale
    high, low = split2(feat * (2.0 * scale))
    dist = jnp.concatenate([high, low, high, norm_rows(norms, True)], 0)
    high, low = split2(block[width:] * term_weights(vectors))
    pair = jnp.concatenate([high, low, high], 0)
    return dist.T, pair.T


def prepared_columns(block, width, vectors):
    feat = block[:width]
    scale = LOG2E / (2.0 * width)
    norms = jnp.sum(feat * feat, axis=0, keepdims=True) * -scale
    high, low = split2(feat)
    dist = jnp.concatenate([high, high, low, norm_rows(norms, False)], 0)
    vecs = jnp.concatenate([block[width + vectors :], block[width : width + vectors]], 0)
    vec_high, vec_low = split2(vecs)
    pair = jnp.concatenate([vec_high, vec_high, vec_low], 0)
    ones = jnp.ones((2 * width, block.shape[1]), jnp.bfloat16)
    pull = jnp.concatenate([high, low, ones], 0)
    return dist, pair, pull


def block_terms(dist_rows, pair_rows, columns):
    across = (((1,), (1,)), ((), ()))
    total = None
    for dist, pair, pull in columns:
        power = jnp.dot(dist_rows, dist, preferred_element_type=jnp.float32)
        bilinear = jnp.dot(pair_rows, pair, preferred_element_type=jnp.float32)
        high, low = split2(jnp.exp2(power) * bilinear)
        for half in (high, low):
            term = lax.dot_general(half, pull, across, preferred_element_type=jnp.float32)
            total = term if total is None else total + term
    return total


def kernel(width, vectors, chunk, rows, columns, fresh, started, *refs):
    refs = list(refs)
    take = lambda count: [refs.pop(0) for _ in range(count)]
    row_refs = take(rows)
    column_refs = take(columns)
    ready = [] if fresh else take(2 * rows)
    before = take(rows) if started else []
    out = take(rows)
    made = take(2 * rows) if fresh else ready
    prepared = [prepared_columns(ref[...], width, vectors) for ref in column_refs]
    for place in range(rows):
        dist_ref, pair_ref = made[2 * place : 2 * place + 2]
        if fresh:
            dist_ref[...], pair_ref[...] = prepared_rows(row_refs[place][...], width, vectors)
        points = row_refs[place].shape[1]
        for start in range(0, points, chunk):
            span = pl.ds(start, chunk)
            total = block_terms(dist_ref[span], pair_ref[span], prepared).T
            pulled = total[:width] + total[width : 2 * width]
            sums = total[2 * width : 2 * width + 1]
            value = (pulled - row_refs[place][:width, span] * sums) / width
            if started:
                value += before[place][:, span]
            out[place][:, span] = value


def pair_terms(row_blocks, column_blocks, width, vectors, ready=None, before=None):
    points = row_blocks[0].shape[1]
    rows, columns = len(row_blocks), len(column_blocks)
    fresh, started = ready is None, before is not None
    shape = jax.ShapeDtypeStruct
    out_shape = [shape((width, points), jnp.float32)] * rows
    if fresh:
        out_shape += [
            shape((points, 3 * width + NORM_ROWS), jnp.bfloat16),
            shape((points, 6 * vectors), jnp.bfloat16),
        ] * rows
    operands = list(row_blocks) + list(column_blocks) + (ready or []) + (before or [])
    results = pl.pallas_call(
        functools.partial(
            kernel, width, vectors, min(512, points), rows, columns, fresh, started
        ),
        out_shape=out_shape,
        in_specs=[pl.BlockSpec(memory_space=pltpu.VMEM)] * len(operands),
        out_specs=[pl.BlockSpec(memory_space=pltpu.VMEM)] * len(out_shape),
        compiler_params=pltpu.CompilerParams(vmem_limit_bytes=VMEM_LIMIT),
        cost_estimate=pl.CostEstimate(flops=1, bytes_accessed=1, transcendentals=1),
    )(*operands)
    results = list(results)
    return results[:rows], results[rows:] if fresh else ready


def packed(features, solves, probes):
    width, points = features.shape
    vectors = solves.shape[0]
    half = points // 2

    def body(features_ref, solves_ref, probes_ref, out_ref, first_ref, second_ref):
        rows = ((0, features_ref), (width, solves_ref), (width + vectors, probes_ref))
        for start, ref in rows:
            span = pl.ds(start, ref.shape[0])
            out_ref[span] = ref[...]
            first_ref[span] = ref[:, :half]
            second_ref[span] = ref[:, half:]

    depth = width + 2 * vectors
    return pl.pallas_call(
        body,
        out_shape=[jax.ShapeDtypeStruct((depth, n), jnp.float32) for n in (points, half, half)],
    )(features, solves, probes)


def local(features, solves, probes):
    width = features.shape[0]
    vectors = solves.shape[0]
    count = lax.axis_size("blk")
    terms = functools.partial(pair_terms, width=width, vectors=vectors)
    swap = lambda value, bit: swapped(value, "blk", bit)
    tied = lax.optimization_barrier

    top = count // 2
    beside = [1 << place for place in range(1, count.bit_length() - 2) if place != 2]
    mine, first, second = packed(features, solves, probes)
    far_first = swap(first, top)
    near = swap(mine, 4)
    direct = [swap(mine, bit) for bit in beside]
    sibling = swap(mine, 1)

    def spread(block):
        blocks = [block]
        for bit in beside:
            blocks += [swap(other, bit) for other in blocks]
        return blocks

    here, ready_here = terms([mine, sibling], [mine])
    far_first, here = tied((far_first, here))
    early = direct + [far_first]
    here, _ = terms([mine, sibling], early, ready=ready_here, before=here)
    first_columns = spread(far_first)
    far_second = swap(second, top)
    near, here = tied((near, here))
    near_sibling = swap(near, 1)
    there, ready_there = terms([near, near_sibling], [mine] + early)
    all_rows = [mine, sibling, near, near_sibling]
    ready = ready_here + ready_there
    far_second, there = tied((far_second, there))
    second_columns = spread(far_second)
    middle = [*first_columns[1:], far_second]
    both, _ = terms(all_rows, middle, ready=ready, before=here + there)
    here, there = both[:2], both[2:]
    last = second_columns[1:]
    there, _ = terms([near, near_sibling], last, ready=ready_there, before=there)
    here, _ = terms([mine, sibling], last, ready=ready_here, before=here)

    toward_near = there[0] + swap(there[1], 1)
    from_near = swap(toward_near, 4)
    return here[0] + swap(here[1], 1) + from_near


def solution(mesh):
    in_specs = (P(None, ("groups", "blk")), P(None, ("groups", "blk")), P(None, ("groups", "blk")))
    out_specs = P(None, ("groups", "blk"))
    return jax.shard_map(local, mesh=mesh, in_specs=in_specs, out_specs=out_specs, check_vma=False)
```

```python
import functools

import jax
import jax.numpy as jnp
from jax import lax
from jax.experimental import pallas as pl
from jax.experimental.pallas import tpu as pltpu
from jax.sharding import PartitionSpec as P

LOG2E = 1.4426950408889634
NORM_ROWS = 16
VMEM_LIMIT = 24 << 20


def swapped(value, axis, bit):
    count = lax.axis_size(axis)
    return lax.ppermute(value, axis, [(source, source ^ bit) for source in range(count)])


def split2(value):
    high = value.astype(jnp.bfloat16)
    low = (value - high.astype(jnp.float32)).astype(jnp.bfloat16)
    return high, low


def term_weights(vectors):
    position = lax.broadcasted_iota(jnp.int32, (2 * vectors, 1), 0)
    first = (position == 0) | (position == vectors)
    return jnp.where(first, 0.5, -0.5 / (vectors - 1)).astype(jnp.float32)


def norm_rows(norms, first):
    high = norms.astype(jnp.bfloat16).astype(jnp.float32)
    rest = norms - high
    mid = rest.astype(jnp.bfloat16).astype(jnp.float32)
    row = lax.broadcasted_iota(jnp.int32, (NORM_ROWS, norms.shape[1]), 0)
    at, ones = (0, 3) if first else (3, 0)
    rows = jnp.where((row >= ones) & (row < ones + 3), 1.0, 0.0)
    for place, part in enumerate((high, mid, rest - mid)):
        rows = jnp.where(row == at + place, part, rows)
    return rows.astype(jnp.bfloat16)


def prepared_rows(block, width, vectors):
    feat = block[:width]
    scale = LOG2E / (2.0 * width)
    norms = jnp.sum(feat * feat, axis=0, keepdims=True) * -scale
    high, low = split2(feat * (2.0 * scale))
    dist = jnp.concatenate([high, low, high, norm_rows(norms, True)], 0)
    high, low = split2(block[width:] * term_weights(vectors))
    pair = jnp.concatenate([high, low, high], 0)
    return dist.T, pair.T


def prepared_columns(block, width, vectors):
    feat = block[:width]
    scale = LOG2E / (2.0 * width)
    norms = jnp.sum(feat * feat, axis=0, keepdims=True) * -scale
    high, low = split2(feat)
    dist = jnp.concatenate([high, high, low, norm_rows(norms, False)], 0)
    vecs = jnp.concatenate([block[width + vectors :], block[width : width + vectors]], 0)
    vec_high, vec_low = split2(vecs)
    pair = jnp.concatenate([vec_high, vec_high, vec_low], 0)
    ones = jnp.ones((2 * width, block.shape[1]), jnp.bfloat16)
    pull = jnp.concatenate([high, low, ones], 0)
    return dist, pair, pull


def block_terms(dist_rows, pair_rows, columns):
    across = (((1,), (1,)), ((), ()))
    total = None
    for dist, pair, pull in columns:
        power = jnp.dot(dist_rows, dist, preferred_element_type=jnp.float32)
        bilinear = jnp.dot(pair_rows, pair, preferred_element_type=jnp.float32)
        high, low = split2(jnp.exp2(power) * bilinear)
        for half in (high, low):
            term = lax.dot_general(half, pull, across, preferred_element_type=jnp.float32)
            total = term if total is None else total + term
    return total


def kernel(width, vectors, chunk, rows, columns, fresh, started, *refs):
    refs = list(refs)
    take = lambda count: [refs.pop(0) for _ in range(count)]
    row_refs = take(rows)
    column_refs = take(columns)
    ready = [] if fresh else take(2 * rows)
    before = take(rows) if started else []
    out = take(rows)
    made = take(2 * rows) if fresh else ready
    prepared = [prepared_columns(ref[...], width, vectors) for ref in column_refs]
    for place in range(rows):
        dist_ref, pair_ref = made[2 * place : 2 * place + 2]
        if fresh:
            dist_ref[...], pair_ref[...] = prepared_rows(row_refs[place][...], width, vectors)
        points = row_refs[place].shape[1]
        for start in range(0, points, chunk):
            span = pl.ds(start, chunk)
            total = block_terms(dist_ref[span], pair_ref[span], prepared).T
            pulled = total[:width] + total[width : 2 * width]
            sums = total[2 * width : 2 * width + 1]
            value = (pulled - row_refs[place][:width, span] * sums) / width
            if started:
                value += before[place][:, span]
            out[place][:, span] = value


def pair_terms(row_blocks, column_blocks, width, vectors, ready=None, before=None):
    points = row_blocks[0].shape[1]
    rows, columns = len(row_blocks), len(column_blocks)
    fresh, started = ready is None, before is not None
    shape = jax.ShapeDtypeStruct
    out_shape = [shape((width, points), jnp.float32)] * rows
    if fresh:
        out_shape += [
            shape((points, 3 * width + NORM_ROWS), jnp.bfloat16),
            shape((points, 6 * vectors), jnp.bfloat16),
        ] * rows
    operands = list(row_blocks) + list(column_blocks) + (ready or []) + (before or [])
    results = pl.pallas_call(
        functools.partial(
            kernel, width, vectors, min(512, points), rows, columns, fresh, started
        ),
        out_shape=out_shape,
        in_specs=[pl.BlockSpec(memory_space=pltpu.VMEM)] * len(operands),
        out_specs=[pl.BlockSpec(memory_space=pltpu.VMEM)] * len(out_shape),
        compiler_params=pltpu.CompilerParams(vmem_limit_bytes=VMEM_LIMIT),
        cost_estimate=pl.CostEstimate(flops=1, bytes_accessed=1, transcendentals=1),
    )(*operands)
    results = list(results)
    return results[:rows], results[rows:] if fresh else ready


def packed(features, solves, probes):
    width, points = features.shape
    vectors = solves.shape[0]

    def body(features_ref, solves_ref, probes_ref, out_ref):
        out_ref[:width] = features_ref[...]
        out_ref[width : width + vectors] = solves_ref[...]
        out_ref[width + vectors :] = probes_ref[...]

    return pl.pallas_call(
        body,
        out_shape=jax.ShapeDtypeStruct((width + 2 * vectors, points), jnp.float32),
        compiler_params=pltpu.CompilerParams(vmem_limit_bytes=4 << 20),
    )(features, solves, probes)


def local(features, solves, probes):
    width = features.shape[0]
    vectors = solves.shape[0]
    count = lax.axis_size("blk")
    terms = functools.partial(pair_terms, width=width, vectors=vectors)
    swap = lambda value, bit: swapped(value, "blk", bit)
    tied = lax.optimization_barrier

    top = count // 2
    beside = [1 << place for place in range(1, count.bit_length() - 2) if place != 2]
    mine = packed(features, solves, probes)
    far = swap(mine, top)
    near = swap(mine, 4)
    direct = [swap(mine, bit) for bit in beside]
    sibling = swap(mine, 1)

    def spread(block):
        blocks = [block]
        for bit in beside:
            blocks += [swap(other, bit) for other in blocks]
        return blocks

    early = [mine] + direct
    here, ready_here = terms([mine, sibling], early)
    far, near, here = tied((far, near, here))
    near_sibling = swap(near, 1)
    far_columns = spread(far)
    here, _ = terms([mine, sibling], [far], ready=ready_here, before=here)
    near_sibling, here = tied((near_sibling, here))
    there, ready_there = terms([near, near_sibling], early + [far])
    last = far_columns[1:]
    last[0], there = tied((last[0], there))
    there, _ = terms([near, near_sibling], last, ready=ready_there, before=there)
    here, _ = terms([mine, sibling], last, ready=ready_here, before=here)

    toward_near = there[0] + swap(there[1], 1)
    from_near = swap(toward_near, 4)
    return here[0] + swap(here[1], 1) + from_near


def solution(mesh):
    in_specs = (P(None, ("groups", "blk")), P(None, ("groups", "blk")), P(None, ("groups", "blk")))
    out_specs = P(None, ("groups", "blk"))
    return jax.shard_map(local, mesh=mesh, in_specs=in_specs, out_specs=out_specs, check_vma=False)
```

```python
import functools

import jax
import jax.numpy as jnp
from jax import lax
from jax.experimental import pallas as pl
from jax.experimental.pallas import tpu as pltpu
from jax.sharding import PartitionSpec as P

LOG2E = 1.4426950408889634
NORM_ROWS = 16
VMEM_LIMIT = 24 << 20


def swapped(value, axis, bit):
    count = lax.axis_size(axis)
    return lax.ppermute(value, axis, [(source, source ^ bit) for source in range(count)])


def split2(value):
    high = value.astype(jnp.bfloat16)
    low = (value - high.astype(jnp.float32)).astype(jnp.bfloat16)
    return high, low


def term_weights(vectors):
    position = lax.broadcasted_iota(jnp.int32, (2 * vectors, 1), 0)
    first = (position == 0) | (position == vectors)
    return jnp.where(first, 0.5, -0.5 / (vectors - 1)).astype(jnp.float32)


def norm_rows(norms, first):
    high = norms.astype(jnp.bfloat16).astype(jnp.float32)
    rest = norms - high
    mid = rest.astype(jnp.bfloat16).astype(jnp.float32)
    row = lax.broadcasted_iota(jnp.int32, (NORM_ROWS, norms.shape[1]), 0)
    at, ones = (0, 3) if first else (3, 0)
    rows = jnp.where((row >= ones) & (row < ones + 3), 1.0, 0.0)
    for place, part in enumerate((high, mid, rest - mid)):
        rows = jnp.where(row == at + place, part, rows)
    return rows.astype(jnp.bfloat16)


def prepared_rows(block, width, vectors):
    feat = block[:width]
    scale = LOG2E / (2.0 * width)
    norms = jnp.sum(feat * feat, axis=0, keepdims=True) * -scale
    high, low = split2(feat * (2.0 * scale))
    dist = jnp.concatenate([high, low, high, norm_rows(norms, True)], 0)
    high, low = split2(block[width:] * term_weights(vectors))
    pair = jnp.concatenate([high, low, high], 0)
    return dist.T, pair.T


def prepared_columns(block, width, vectors):
    feat = block[:width]
    scale = LOG2E / (2.0 * width)
    norms = jnp.sum(feat * feat, axis=0, keepdims=True) * -scale
    high, low = split2(feat)
    dist = jnp.concatenate([high, high, low, norm_rows(norms, False)], 0)
    vecs = jnp.concatenate([block[width + vectors :], block[width : width + vectors]], 0)
    vec_high, vec_low = split2(vecs)
    pair = jnp.concatenate([vec_high, vec_high, vec_low], 0)
    ones = jnp.ones((2 * width, block.shape[1]), jnp.bfloat16)
    pull = jnp.concatenate([high, low, ones], 0)
    return dist, pair, pull


def block_terms(dist_rows, pair_rows, columns):
    across = (((1,), (1,)), ((), ()))
    total = None
    for dist, pair, pull in columns:
        power = jnp.dot(dist_rows, dist, preferred_element_type=jnp.float32)
        bilinear = jnp.dot(pair_rows, pair, preferred_element_type=jnp.float32)
        high, low = split2(jnp.exp2(power) * bilinear)
        for half in (high, low):
            term = lax.dot_general(half, pull, across, preferred_element_type=jnp.float32)
            total = term if total is None else total + term
    return total


def kernel(width, vectors, chunk, rows, columns, fresh, started, *refs):
    refs = list(refs)
    take = lambda count: [refs.pop(0) for _ in range(count)]
    row_refs = take(rows)
    column_refs = take(columns)
    ready = [] if fresh else take(2 * rows)
    before = take(rows) if started else []
    out = take(rows)
    made = take(2 * rows) if fresh else ready
    prepared = [prepared_columns(ref[...], width, vectors) for ref in column_refs]
    for place in range(rows):
        dist_ref, pair_ref = made[2 * place : 2 * place + 2]
        if fresh:
            dist_ref[...], pair_ref[...] = prepared_rows(row_refs[place][...], width, vectors)
        points = row_refs[place].shape[1]
        for start in range(0, points, chunk):
            span = pl.ds(start, chunk)
            total = block_terms(dist_ref[span], pair_ref[span], prepared).T
            pulled = total[:width] + total[width : 2 * width]
            sums = total[2 * width : 2 * width + 1]
            value = (pulled - row_refs[place][:width, span] * sums) / width
            if started:
                value += before[place][:, span]
            out[place][:, span] = value


def pair_terms(row_blocks, column_blocks, width, vectors, ready=None, before=None):
    points = row_blocks[0].shape[1]
    rows, columns = len(row_blocks), len(column_blocks)
    fresh, started = ready is None, before is not None
    shape = jax.ShapeDtypeStruct
    out_shape = [shape((width, points), jnp.float32)] * rows
    if fresh:
        out_shape += [
            shape((points, 3 * width + NORM_ROWS), jnp.bfloat16),
            shape((points, 6 * vectors), jnp.bfloat16),
        ] * rows
    operands = list(row_blocks) + list(column_blocks) + (ready or []) + (before or [])
    results = pl.pallas_call(
        functools.partial(
            kernel, width, vectors, min(512, points), rows, columns, fresh, started
        ),
        out_shape=out_shape,
        in_specs=[pl.BlockSpec(memory_space=pltpu.VMEM)] * len(operands),
        out_specs=[pl.BlockSpec(memory_space=pltpu.VMEM)] * len(out_shape),
        compiler_params=pltpu.CompilerParams(vmem_limit_bytes=VMEM_LIMIT),
        cost_estimate=pl.CostEstimate(flops=1, bytes_accessed=1, transcendentals=1),
    )(*operands)
    results = list(results)
    return results[:rows], results[rows:] if fresh else ready


def packed(features, solves, probes):
    width, points = features.shape
    vectors = solves.shape[0]

    def body(features_ref, solves_ref, probes_ref, out_ref, arrived):
        parts = ((features_ref, 0), (solves_ref, width), (probes_ref, width + vectors))
        copies = [
            pltpu.make_async_copy(ref, out_ref.at[pl.ds(start, ref.shape[0])], arrived.at[place])
            for place, (ref, start) in enumerate(parts)
        ]
        for copy in copies:
            copy.start()
        for copy in copies:
            copy.wait()

    return pl.pallas_call(
        body,
        out_shape=jax.ShapeDtypeStruct((width + 2 * vectors, points), jnp.float32),
        in_specs=[pl.BlockSpec(memory_space=pltpu.HBM)] * 3,
        out_specs=pl.BlockSpec(memory_space=pltpu.HBM),
        scratch_shapes=[pltpu.SemaphoreType.DMA((3,))],
        compiler_params=pltpu.CompilerParams(vmem_limit_bytes=60 << 20),
    )(features, solves, probes)


def local(features, solves, probes):
    width = features.shape[0]
    vectors = solves.shape[0]
    count = lax.axis_size("blk")
    terms = functools.partial(pair_terms, width=width, vectors=vectors)
    swap = lambda value, bit: swapped(value, "blk", bit)
    tied = lax.optimization_barrier

    top = count // 2
    beside = [1 << place for place in range(1, count.bit_length() - 2) if place != 2]
    mine = packed(features, solves, probes)
    far = swap(mine, top)
    near = swap(mine, 4)
    direct = [swap(mine, bit) for bit in beside]
    sibling = swap(mine, 1)

    here, ready_here = terms([mine], [mine, sibling])
    *direct, here[0] = tied((*direct, here[0]))
    direct_siblings = [swap(block, 1) for block in direct]
    here, _ = terms([mine], direct, ready=ready_here, before=here)
    far, near, here[0] = tied((far, near, here[0]))
    last = []
    for bit in beside:
        last += [swap(block, bit) for block in [far] + last]
    far_sibling = swap(far, 1)
    here, _ = terms([mine], direct_siblings + [far], ready=ready_here, before=here)
    early = [mine, sibling, *direct, *direct_siblings, far]
    there, ready_there = terms([near], early)
    last[0], here[0], there[0] = tied((last[0], here[0], there[0]))
    last_siblings = [swap(block, 1) for block in last]
    both = [mine, near]
    ready = ready_here + ready_there
    (toward_here, toward_there), _ = terms(
        both, [far_sibling, *last], ready=ready, before=here + there
    )
    there, _ = terms([near], last_siblings, ready=ready_there, before=[toward_there])
    from_near = swap(there[0], 4)
    here, _ = terms([mine], last_siblings, ready=ready_here, before=[toward_here])
    return here[0] + from_near


def solution(mesh):
    in_specs = (P(None, ("groups", "blk")), P(None, ("groups", "blk")), P(None, ("groups", "blk")))
    out_specs = P(None, ("groups", "blk"))
    return jax.shard_map(local, mesh=mesh, in_specs=in_specs, out_specs=out_specs, check_vma=False)
```

```python
import functools

import jax
import jax.numpy as jnp
from jax import lax
from jax.experimental import pallas as pl
from jax.experimental.pallas import tpu as pltpu
from jax.sharding import PartitionSpec as P

LOG2E = 1.4426950408889634
NORM_ROWS = 16
ONES_ROWS = 16
VMEM_LIMIT = 24 << 20


def swapped(value, axis, bit):
    count = lax.axis_size(axis)
    return lax.ppermute(value, axis, [(source, source ^ bit) for source in range(count)])


def split2(value):
    high = value.astype(jnp.bfloat16)
    low = (value - high.astype(jnp.float32)).astype(jnp.bfloat16)
    return high, low


def term_weights(vectors):
    position = lax.broadcasted_iota(jnp.int32, (2 * vectors, 1), 0)
    first = (position == 0) | (position == vectors)
    return jnp.where(first, 0.5, -0.5 / (vectors - 1)).astype(jnp.float32)


def norm_rows(norms, first):
    high = norms.astype(jnp.bfloat16).astype(jnp.float32)
    rest = norms - high
    mid = rest.astype(jnp.bfloat16).astype(jnp.float32)
    row = lax.broadcasted_iota(jnp.int32, (NORM_ROWS, norms.shape[1]), 0)
    at, ones = (0, 3) if first else (3, 0)
    rows = jnp.where((row >= ones) & (row < ones + 3), 1.0, 0.0)
    for place, part in enumerate((high, mid, rest - mid)):
        rows = jnp.where(row == at + place, part, rows)
    return rows.astype(jnp.bfloat16)


def prepared_mine(block, width, vectors):
    feat = block[:width]
    scale = LOG2E / (2.0 * width)
    norms = jnp.sum(feat * feat, axis=0, keepdims=True) * -scale
    high, low = split2(feat * (2.0 * scale))
    dist = jnp.concatenate([high, low, high, norm_rows(norms, True)], 0)
    high, low = split2(block[width:] * term_weights(vectors))
    return dist, jnp.concatenate([high, low, high], 0)


def prepared_theirs(block, width, vectors):
    feat = block[:width]
    scale = LOG2E / (2.0 * width)
    norms = jnp.sum(feat * feat, axis=0, keepdims=True) * -scale
    high, low = split2(feat)
    dist = jnp.concatenate([high, high, low, norm_rows(norms, False)], 0)
    vecs = jnp.concatenate([block[width + vectors :], block[width : width + vectors]], 0)
    vec_high, vec_low = split2(vecs)
    pair = jnp.concatenate([vec_high, vec_high, vec_low], 0)
    ones = jnp.ones((ONES_ROWS, block.shape[1]), jnp.bfloat16)
    return dist.T, pair.T, jnp.concatenate([high, ones, low], 0)


def product(left, right):
    return jnp.dot(left, right, preferred_element_type=jnp.float32)


def block_terms(mine, theirs, width):
    dist_mine, pair_mine = mine
    dist_theirs, pair_theirs, pull = theirs
    coupling = jnp.exp2(product(dist_theirs, dist_mine)) * product(pair_theirs, pair_mine)
    high, low = split2(coupling)
    from_high = product(pull, high)
    from_low = product(pull[: width + ONES_ROWS], low)
    pulled = from_high[:width] + from_high[width + ONES_ROWS :] + from_low[:width]
    return pulled, from_high[width : width + 1] + from_low[width : width + 1]


def kernel(width, vectors, jobs, count, *refs):
    blocks, refs = refs[:count], refs[count:]
    before, out = refs[: -len(jobs)], refs[-len(jobs) :]
    used = sorted({theirs for _, columns in jobs for theirs in columns})
    theirs = {place: prepared_theirs(blocks[place][...], width, vectors) for place in used}
    for place, (row, columns) in enumerate(jobs):
        mine = prepared_mine(blocks[row][...], width, vectors)
        terms = [block_terms(mine, theirs[column], width) for column in columns]
        pulled = sum(term[0] for term in terms)
        sums = sum(term[1] for term in terms)
        value = (pulled - blocks[row][:width] * sums) / width
        out[place][...] = value + before[place][...] if place < len(before) else value


def pair_terms(jobs, width, vectors, before=()):
    blocks = []

    def place(block):
        for index, other in enumerate(blocks):
            if other is block:
                return index
        blocks.append(block)
        return len(blocks) - 1

    placed = [(place(row), [place(column) for column in columns]) for row, columns in jobs]
    points = blocks[0].shape[1]
    operands = blocks + list(before)
    out_shape = [jax.ShapeDtypeStruct((width, points), jnp.float32)] * len(jobs)
    return list(
        pl.pallas_call(
            functools.partial(kernel, width, vectors, placed, len(blocks)),
            out_shape=out_shape,
            in_specs=[pl.BlockSpec(memory_space=pltpu.VMEM)] * len(operands),
            out_specs=[pl.BlockSpec(memory_space=pltpu.VMEM)] * len(out_shape),
            compiler_params=pltpu.CompilerParams(vmem_limit_bytes=VMEM_LIMIT),
        )(*operands)
    )


def packed(features, solves, probes):
    width, points = features.shape
    vectors = solves.shape[0]

    def body(features_ref, solves_ref, probes_ref, out_ref):
        out_ref[:width] = features_ref[...]
        out_ref[width : width + vectors] = solves_ref[...]
        out_ref[width + vectors :] = probes_ref[...]

    return pl.pallas_call(
        body,
        out_shape=jax.ShapeDtypeStruct((width + 2 * vectors, points), jnp.float32),
        compiler_params=pltpu.CompilerParams(vmem_limit_bytes=60 << 20),
    )(features, solves, probes)


def local(features, solves, probes):
    width = features.shape[0]
    vectors = solves.shape[0]
    count = lax.axis_size("blk")
    terms = functools.partial(pair_terms, width=width, vectors=vectors)
    swap = lambda value, bit: swapped(value, "blk", bit)
    tied = lax.optimization_barrier

    top = count // 2
    beside = [1 << place for place in range(1, count.bit_length() - 2) if place != 2]
    mine = packed(features, solves, probes)
    sibling = swap(mine, 1)
    far = swap(mine, top)
    near = swap(mine, 4)
    direct = [swap(mine, bit) for bit in beside]

    here = terms([(mine, [mine, sibling])])
    far, here[0] = tied((far, here[0]))
    last = []
    for bit in beside:
        last += [swap(block, bit) for block in [far] + last]
    siblings = [swap(block, 1) for block in [far] + direct]
    both = terms(
        [(mine, [far] + direct), (near, [mine, sibling, far] + direct)],
        before=here,
    )
    both = terms([(mine, siblings), (near, siblings)], before=both)
    last[0], *both = tied((last[0], *both))
    last_siblings = [swap(block, 1) for block in last]
    here, there = terms([(mine, last), (near, last)], before=both)
    (there,) = terms([(near, last_siblings)], before=[there])
    from_near = swap(there, 4)
    (here,) = terms([(mine, last_siblings)], before=[here])
    return here + from_near


def solution(mesh):
    in_specs = (P(None, ("groups", "blk")), P(None, ("groups", "blk")), P(None, ("groups", "blk")))
    out_specs = P(None, ("groups", "blk"))
    return jax.shard_map(local, mesh=mesh, in_specs=in_specs, out_specs=out_specs, check_vma=False)
```

```python
import functools

import jax
import jax.numpy as jnp
from jax import lax
from jax.experimental import pallas as pl
from jax.experimental.pallas import tpu as pltpu
from jax.sharding import PartitionSpec as P

LOG2E = 1.4426950408889634
NORM_ROWS = 16
ONES_ROWS = 16
CHUNK = 256
VMEM_LIMIT = 24 << 20


def swapped(value, axis, bit):
    count = lax.axis_size(axis)
    return lax.ppermute(value, axis, [(source, source ^ bit) for source in range(count)])


def split2(value):
    high = value.astype(jnp.bfloat16)
    low = (value - high.astype(jnp.float32)).astype(jnp.bfloat16)
    return high, low


def term_weights(vectors):
    position = lax.broadcasted_iota(jnp.int32, (2 * vectors, 1), 0)
    first = (position == 0) | (position == vectors)
    return jnp.where(first, 0.5, -0.5 / (vectors - 1)).astype(jnp.float32)


def norm_rows(norms, first):
    high = norms.astype(jnp.bfloat16).astype(jnp.float32)
    rest = norms - high
    mid = rest.astype(jnp.bfloat16).astype(jnp.float32)
    row = lax.broadcasted_iota(jnp.int32, (NORM_ROWS, norms.shape[1]), 0)
    at, ones = (0, 3) if first else (3, 0)
    rows = jnp.where((row >= ones) & (row < ones + 3), 1.0, 0.0)
    for place, part in enumerate((high, mid, rest - mid)):
        rows = jnp.where(row == at + place, part, rows)
    return rows.astype(jnp.bfloat16)


def prepared_mine(block, width, vectors):
    feat = block[:width]
    scale = LOG2E / (2.0 * width)
    norms = jnp.sum(feat * feat, axis=0, keepdims=True) * -scale
    high, low = split2(feat * (2.0 * scale))
    dist = jnp.concatenate([high, low, high, norm_rows(norms, True)], 0)
    high, low = split2(block[width:] * term_weights(vectors))
    return dist, jnp.concatenate([high, low, high], 0)


def prepared_theirs(block, width, vectors):
    feat = block[:width]
    scale = LOG2E / (2.0 * width)
    norms = jnp.sum(feat * feat, axis=0, keepdims=True) * -scale
    high, low = split2(feat)
    dist = jnp.concatenate([high, high, low, norm_rows(norms, False)], 0)
    vecs = jnp.concatenate([block[width + vectors :], block[width : width + vectors]], 0)
    vec_high, vec_low = split2(vecs)
    pair = jnp.concatenate([vec_high, vec_high, vec_low], 0)
    ones = jnp.ones((ONES_ROWS, block.shape[1]), jnp.bfloat16)
    return dist.T, pair.T, jnp.concatenate([high, ones, low], 0)


def product(left, right):
    return jnp.dot(left, right, preferred_element_type=jnp.float32)


def pulled_terms(mine, theirs, width):
    points = mine[0].shape[1]
    chunks = []
    for start in range(0, points, CHUNK):
        dist_mine, pair_mine = (part[:, start : start + CHUNK] for part in mine)
        from_high = from_low = None
        for dist_theirs, pair_theirs, pull in theirs:
            for first in range(0, points, CHUNK):
                rows = slice(first, first + CHUNK)
                power = product(dist_theirs[rows], dist_mine)
                coupling = jnp.exp2(power) * product(pair_theirs[rows], pair_mine)
                high, low = split2(coupling)
                term_high = product(pull[:, rows], high)
                term_low = product(pull[: width + ONES_ROWS, rows], low)
                from_high = term_high if from_high is None else from_high + term_high
                from_low = term_low if from_low is None else from_low + term_low
        pulled = from_high[:width] + from_high[width + ONES_ROWS :] + from_low[:width]
        chunks.append((pulled, from_high[width : width + 1] + from_low[width : width + 1]))
    return (jnp.concatenate(parts, 1) for parts in zip(*chunks))


def kernel(width, vectors, jobs, count, *refs):
    blocks, refs = refs[:count], refs[count:]
    before, out = refs[: -len(jobs)], refs[-len(jobs) :]
    used = sorted({theirs for _, columns in jobs for theirs in columns})
    theirs = {place: prepared_theirs(blocks[place][...], width, vectors) for place in used}
    for place, (row, columns) in enumerate(jobs):
        mine = prepared_mine(blocks[row][...], width, vectors)
        pulled, sums = pulled_terms(mine, [theirs[column] for column in columns], width)
        value = (pulled - blocks[row][:width] * sums) / width
        out[place][...] = value + before[place][...] if place < len(before) else value


def pair_terms(jobs, width, vectors, before=()):
    blocks = []

    def place(block):
        for index, other in enumerate(blocks):
            if other is block:
                return index
        blocks.append(block)
        return len(blocks) - 1

    placed = [(place(row), [place(column) for column in columns]) for row, columns in jobs]
    points = blocks[0].shape[1]
    operands = blocks + list(before)
    out_shape = [jax.ShapeDtypeStruct((width, points), jnp.float32)] * len(jobs)
    return list(
        pl.pallas_call(
            functools.partial(kernel, width, vectors, placed, len(blocks)),
            out_shape=out_shape,
            in_specs=[pl.BlockSpec(memory_space=pltpu.VMEM)] * len(operands),
            out_specs=[pl.BlockSpec(memory_space=pltpu.VMEM)] * len(out_shape),
            compiler_params=pltpu.CompilerParams(vmem_limit_bytes=VMEM_LIMIT),
        )(*operands)
    )


def packed(features, solves, probes):
    width, points = features.shape
    vectors = solves.shape[0]

    def body(features_ref, solves_ref, probes_ref, out_ref):
        out_ref[:width] = features_ref[...]
        out_ref[width : width + vectors] = solves_ref[...]
        out_ref[width + vectors :] = probes_ref[...]

    return pl.pallas_call(
        body,
        out_shape=jax.ShapeDtypeStruct((width + 2 * vectors, points), jnp.float32),
        compiler_params=pltpu.CompilerParams(vmem_limit_bytes=60 << 20),
    )(features, solves, probes)


def local(features, solves, probes):
    width = features.shape[0]
    vectors = solves.shape[0]
    count = lax.axis_size("blk")
    terms = functools.partial(pair_terms, width=width, vectors=vectors)
    swap = lambda value, bit: swapped(value, "blk", bit)
    tied = lax.optimization_barrier

    top = count // 2
    beside = [1 << place for place in range(1, count.bit_length() - 2) if place != 2]
    mine = packed(features, solves, probes)
    sibling = swap(mine, 1)
    far = swap(mine, top)
    near = swap(mine, 4)
    direct = [swap(mine, bit) for bit in beside]

    here = terms([(mine, [mine, sibling])])
    far, here[0] = tied((far, here[0]))
    last = []
    for bit in beside:
        last += [swap(block, bit) for block in [far] + last]
    siblings = [swap(block, 1) for block in [far] + direct]
    both = terms(
        [(mine, [far] + direct), (near, [mine, sibling, far] + direct)],
        before=here,
    )
    both = terms([(mine, siblings), (near, siblings)], before=both)
    last[0], *both = tied((last[0], *both))
    last_siblings = [swap(block, 1) for block in last]
    here, there = terms([(mine, last), (near, last)], before=both)
    (there,) = terms([(near, last_siblings)], before=[there])
    from_near = swap(there, 4)
    (here,) = terms([(mine, last_siblings)], before=[here])
    return here + from_near


def solution(mesh):
    in_specs = (P(None, ("groups", "blk")), P(None, ("groups", "blk")), P(None, ("groups", "blk")))
    out_specs = P(None, ("groups", "blk"))
    return jax.shard_map(local, mesh=mesh, in_specs=in_specs, out_specs=out_specs, check_vma=False)
```

```python
import functools

import jax
import jax.numpy as jnp
from jax import lax
from jax.experimental import pallas as pl
from jax.experimental.pallas import tpu as pltpu
from jax.sharding import PartitionSpec as P

LOG2E = 1.4426950408889634
NORM_ROWS = 16
ONES_ROWS = 16
VMEM_LIMIT = 24 << 20


def swapped(value, axis, bit):
    count = lax.axis_size(axis)
    return lax.ppermute(value, axis, [(source, source ^ bit) for source in range(count)])


def split2(value):
    high = value.astype(jnp.bfloat16)
    low = (value - high.astype(jnp.float32)).astype(jnp.bfloat16)
    return high, low


def term_weights(vectors):
    position = lax.broadcasted_iota(jnp.int32, (2 * vectors, 1), 0)
    first = (position == 0) | (position == vectors)
    return jnp.where(first, 0.5, -0.5 / (vectors - 1)).astype(jnp.float32)


def norm_rows(norms, first):
    high = norms.astype(jnp.bfloat16).astype(jnp.float32)
    rest = norms - high
    mid = rest.astype(jnp.bfloat16).astype(jnp.float32)
    row = lax.broadcasted_iota(jnp.int32, (NORM_ROWS, norms.shape[1]), 0)
    at, ones = (0, 3) if first else (3, 0)
    rows = jnp.where((row >= ones) & (row < ones + 3), 1.0, 0.0)
    for place, part in enumerate((high, mid, rest - mid)):
        rows = jnp.where(row == at + place, part, rows)
    return rows.astype(jnp.bfloat16)


def prepared_mine(block, width, vectors):
    feat = block[:width]
    scale = LOG2E / (2.0 * width)
    norms = jnp.sum(feat * feat, axis=0, keepdims=True) * -scale
    high, low = split2(feat * (2.0 * scale))
    dist = jnp.concatenate([high, low, high, norm_rows(norms, True)], 0)
    high, low = split2(block[width:] * term_weights(vectors))
    return dist, jnp.concatenate([high, low, high], 0)


def prepared_theirs(block, width, vectors):
    feat = block[:width]
    scale = LOG2E / (2.0 * width)
    norms = jnp.sum(feat * feat, axis=0, keepdims=True) * -scale
    high, low = split2(feat)
    dist = jnp.concatenate([high, high, low, norm_rows(norms, False)], 0)
    vecs = jnp.concatenate([block[width + vectors :], block[width : width + vectors]], 0)
    vec_high, vec_low = split2(vecs)
    pair = jnp.concatenate([vec_high, vec_high, vec_low], 0)
    ones = jnp.ones((ONES_ROWS, block.shape[1]), jnp.bfloat16)
    return dist.T, pair.T, jnp.concatenate([high, ones, low], 0)


def product(left, right):
    return jnp.dot(left, right, preferred_element_type=jnp.float32)


def pulled_terms(mine, theirs, width):
    dist_mine, pair_mine = mine
    dist_theirs, pair_theirs, pull = theirs
    coupling = jnp.exp2(product(dist_theirs, dist_mine)) * product(pair_theirs, pair_mine)
    high, low = split2(coupling)
    from_high = product(pull, high)
    from_low = product(pull[: width + ONES_ROWS], low)
    pulled = from_high[:width] + from_high[width + ONES_ROWS :] + from_low[:width]
    return pulled, from_high[width : width + 1] + from_low[width : width + 1]


def stacked(theirs):
    dist, pair, pull = zip(*theirs)
    return jnp.concatenate(dist, 0), jnp.concatenate(pair, 0), jnp.concatenate(pull, 1)


def kernel(width, vectors, jobs, count, *refs):
    blocks, refs = refs[:count], refs[count:]
    before, out = refs[: -len(jobs)], refs[-len(jobs) :]
    used = sorted({theirs for _, columns in jobs for theirs in columns})
    theirs = {place: prepared_theirs(blocks[place][...], width, vectors) for place in used}
    for place, (row, columns) in enumerate(jobs):
        mine = prepared_mine(blocks[row][...], width, vectors)
        pulled, sums = pulled_terms(mine, stacked([theirs[column] for column in columns]), width)
        value = (pulled - blocks[row][:width] * sums) / width
        out[place][...] = value + before[place][...] if place < len(before) else value


def pair_terms(jobs, width, vectors, before=()):
    blocks = []

    def place(block):
        for index, other in enumerate(blocks):
            if other is block:
                return index
        blocks.append(block)
        return len(blocks) - 1

    placed = [(place(row), [place(column) for column in columns]) for row, columns in jobs]
    points = blocks[0].shape[1]
    operands = blocks + list(before)
    out_shape = [jax.ShapeDtypeStruct((width, points), jnp.float32)] * len(jobs)
    return list(
        pl.pallas_call(
            functools.partial(kernel, width, vectors, placed, len(blocks)),
            out_shape=out_shape,
            in_specs=[pl.BlockSpec(memory_space=pltpu.VMEM)] * len(operands),
            out_specs=[pl.BlockSpec(memory_space=pltpu.VMEM)] * len(out_shape),
            compiler_params=pltpu.CompilerParams(vmem_limit_bytes=VMEM_LIMIT),
            cost_estimate=pl.CostEstimate(
                flops=2 * points * points * 2048 * sum(len(columns) for _, columns in jobs),
                bytes_accessed=4 * points * 96 * len(operands),
                transcendentals=points * points,
            ),
        )(*operands)
    )


def packed(features, solves, probes):
    width, points = features.shape
    vectors = solves.shape[0]

    def body(features_ref, solves_ref, probes_ref, out_ref):
        out_ref[:width] = features_ref[...]
        out_ref[width : width + vectors] = solves_ref[...]
        out_ref[width + vectors :] = probes_ref[...]

    return pl.pallas_call(
        body,
        out_shape=jax.ShapeDtypeStruct((width + 2 * vectors, points), jnp.float32),
        compiler_params=pltpu.CompilerParams(vmem_limit_bytes=60 << 20),
    )(features, solves, probes)


def local(features, solves, probes):
    width = features.shape[0]
    vectors = solves.shape[0]
    count = lax.axis_size("blk")
    terms = functools.partial(pair_terms, width=width, vectors=vectors)
    swap = lambda value, bit: swapped(value, "blk", bit)
    tied = lax.optimization_barrier

    beside = [1 << place for place in range(3, count.bit_length() - 1)]
    mine = packed(features, solves, probes)
    sibling = swap(mine, 1)
    far = swap(mine, beside[-1])
    sent, sibling = tied((mine, sibling))
    near_y = swap(sent, 2)
    near_z = swap(sent, 4)

    home = [mine, sibling]
    (here,) = terms([(mine, home)])
    near_z, near_y, here = tied((near_z, near_y, here))
    near_both = swap(near_z, 2)
    toward_y, toward_z = terms([(near_y, home), (near_z, home)])
    near_both, toward_y = tied((near_both, toward_y))
    (toward_both,) = terms([(near_both, home)])

    far, toward_both = tied((far, toward_both))
    columns = [far]
    for bit in reversed(beside[:-1]):
        columns += [swap(block, bit) for block in [mine] + columns]
    for block in columns:
        other = swap(block, 1)
        toward_both, toward_y, toward_z = terms(
            [(near_both, [block]), (near_y, [block]), (near_z, [block])],
            before=[toward_both, toward_y, toward_z],
        )
        other, toward_both = tied((other, toward_both))
        toward_both, toward_y, toward_z = terms(
            [(near_both, [other]), (near_y, [other]), (near_z, [other])],
            before=[toward_both, toward_y, toward_z],
        )
        (here,) = terms([(mine, [block, other])], before=[here])
    return here + swap(toward_both, 6) + swap(toward_y, 2) + swap(toward_z, 4)


def solution(mesh):
    in_specs = (P(None, ("groups", "blk")), P(None, ("groups", "blk")), P(None, ("groups", "blk")))
    out_specs = P(None, ("groups", "blk"))
    return jax.shard_map(local, mesh=mesh, in_specs=in_specs, out_specs=out_specs, check_vma=False)
```

```python
import functools

import jax
import jax.numpy as jnp
from jax import lax
from jax.experimental import pallas as pl
from jax.experimental.pallas import tpu as pltpu
from jax.sharding import PartitionSpec as P

LOG2E = 1.4426950408889634
NORM_ROWS = 16
ONES_ROWS = 16
STACK = 4
VMEM_LIMIT = 24 << 20


def swapped(value, axis, bit):
    count = lax.axis_size(axis)
    return lax.ppermute(value, axis, [(source, source ^ bit) for source in range(count)])


def split2(value):
    high = value.astype(jnp.bfloat16)
    low = (value - high.astype(jnp.float32)).astype(jnp.bfloat16)
    return high, low


def term_weights(vectors):
    position = lax.broadcasted_iota(jnp.int32, (2 * vectors, 1), 0)
    first = (position == 0) | (position == vectors)
    return jnp.where(first, 0.5, -0.5 / (vectors - 1)).astype(jnp.float32)


def norm_rows(norms, first):
    high = norms.astype(jnp.bfloat16).astype(jnp.float32)
    rest = norms - high
    mid = rest.astype(jnp.bfloat16).astype(jnp.float32)
    row = lax.broadcasted_iota(jnp.int32, (NORM_ROWS, norms.shape[1]), 0)
    at, ones = (0, 3) if first else (3, 0)
    rows = jnp.where((row >= ones) & (row < ones + 3), 1.0, 0.0)
    for place, part in enumerate((high, mid, rest - mid)):
        rows = jnp.where(row == at + place, part, rows)
    return rows.astype(jnp.bfloat16)


def prepared_mine(block, width, vectors):
    feat = block[:width]
    scale = LOG2E / (2.0 * width)
    norms = jnp.sum(feat * feat, axis=0, keepdims=True) * -scale
    high, low = split2(feat * (2.0 * scale))
    dist = jnp.concatenate([high, low, high, norm_rows(norms, True)], 0)
    high, low = split2(block[width:] * term_weights(vectors))
    return dist, jnp.concatenate([high, low, high], 0)


def prepared_theirs(block, width, vectors):
    feat = block[:width]
    scale = LOG2E / (2.0 * width)
    norms = jnp.sum(feat * feat, axis=0, keepdims=True) * -scale
    high, low = split2(feat)
    dist = jnp.concatenate([high, high, low, norm_rows(norms, False)], 0)
    vecs = jnp.concatenate([block[width + vectors :], block[width : width + vectors]], 0)
    vec_high, vec_low = split2(vecs)
    pair = jnp.concatenate([vec_high, vec_high, vec_low], 0)
    ones = jnp.ones((ONES_ROWS, block.shape[1]), jnp.bfloat16)
    return dist.T, pair.T, jnp.concatenate([high, ones, low], 0)


def product(left, right):
    return jnp.dot(left, right, preferred_element_type=jnp.float32)


def pulled_terms(mine, theirs, width):
    dist_mine, pair_mine = mine
    dist_theirs, pair_theirs, pull = theirs
    coupling = jnp.exp2(product(dist_theirs, dist_mine)) * product(pair_theirs, pair_mine)
    high, low = split2(coupling)
    from_high = product(pull, high)
    from_low = product(pull[: width + ONES_ROWS], low)
    pulled = from_high[:width] + from_high[width + ONES_ROWS :] + from_low[:width]
    return pulled, from_high[width : width + 1] + from_low[width : width + 1]


def stacked(theirs):
    dist, pair, pull = zip(*theirs)
    return jnp.concatenate(dist, 0), jnp.concatenate(pair, 0), jnp.concatenate(pull, 1)


def kernel(width, vectors, jobs, count, *refs):
    blocks, refs = refs[:count], refs[count:]
    before, out = refs[: -len(jobs)], refs[-len(jobs) :]
    used = sorted({theirs for _, columns in jobs for theirs in columns})
    theirs = {place: prepared_theirs(blocks[place][...], width, vectors) for place in used}
    for place, (row, columns) in enumerate(jobs):
        mine = prepared_mine(blocks[row][...], width, vectors)
        parts = [
            pulled_terms(mine, stacked([theirs[column] for column in columns[at : at + STACK]]), width)
            for at in range(0, len(columns), STACK)
        ]
        pulled, sums = (sum(part) for part in zip(*parts))
        value = (pulled - blocks[row][:width] * sums) / width
        out[place][...] = value + before[place][...] if place < len(before) else value


def pair_terms(jobs, width, vectors, before=(), weight=2048):
    blocks = []

    def place(block):
        for index, other in enumerate(blocks):
            if other is block:
                return index
        blocks.append(block)
        return len(blocks) - 1

    placed = [(place(row), [place(column) for column in columns]) for row, columns in jobs]
    points = blocks[0].shape[1]
    operands = blocks + list(before)
    out_shape = [jax.ShapeDtypeStruct((width, points), jnp.float32)] * len(jobs)
    return list(
        pl.pallas_call(
            functools.partial(kernel, width, vectors, placed, len(blocks)),
            out_shape=out_shape,
            in_specs=[pl.BlockSpec(memory_space=pltpu.VMEM)] * len(operands),
            out_specs=[pl.BlockSpec(memory_space=pltpu.VMEM)] * len(out_shape),
            compiler_params=pltpu.CompilerParams(vmem_limit_bytes=VMEM_LIMIT),
            cost_estimate=pl.CostEstimate(
                flops=2 * points * points * weight * sum(len(columns) for _, columns in jobs),
                bytes_accessed=4 * points * 96 * len(operands),
                transcendentals=points * points,
            ),
        )(*operands)
    )


def packed(features, solves, probes):
    width, points = features.shape
    vectors = solves.shape[0]

    def body(features_ref, solves_ref, probes_ref, out_ref):
        out_ref[:width] = features_ref[...]
        out_ref[width : width + vectors] = solves_ref[...]
        out_ref[width + vectors :] = probes_ref[...]

    return pl.pallas_call(
        body,
        out_shape=jax.ShapeDtypeStruct((width + 2 * vectors, points), jnp.float32),
        compiler_params=pltpu.CompilerParams(vmem_limit_bytes=60 << 20),
    )(features, solves, probes)


def local(features, solves, probes):
    width = features.shape[0]
    vectors = solves.shape[0]
    count = lax.axis_size("blk")
    terms = functools.partial(pair_terms, width=width, vectors=vectors)
    swap = lambda value, bit: swapped(value, "blk", bit)
    tied = lax.optimization_barrier

    bits = [1 << place for place in range(count.bit_length() - 1)]
    top, beside = bits[-1], [bit for bit in bits[:-1] if bit not in (1, 4)]
    far_features = swap(features, top)
    mine = packed(features, solves, probes)
    far_vectors = swap(mine[width:], top)
    sibling = swap(mine, 1)
    near = swap(mine, 4)
    direct = [swap(mine, bit) for bit in beside]

    far_features, own = tied((far_features, mine))
    (here,) = terms([(own, [own])], weight=512)
    far_vectors, here = tied((far_vectors, here))
    split = [far_features, far_vectors]
    far = jnp.concatenate(split, 0)
    last = []
    for bit in beside:
        pieces = [split] + [[block[:width], block[width:]] for block in last]
        last += [jnp.concatenate([swap(piece, bit) for piece in pair], 0) for pair in pieces]
    first = [far] + direct
    siblings = [swap(block, 1) for block in first]
    (there,) = terms([(near, [mine, sibling] + first)], weight=64)
    (there,) = terms([(near, siblings)], before=[there], weight=2048)
    last[0], there = tied((last[0], there))
    last_siblings = [swap(block, 1) for block in last]
    (there,) = terms([(near, last)], before=[there])
    (there,) = terms([(near, last_siblings)], before=[there])
    from_near = swap(there, 4)
    rest = [sibling] + first + siblings + last + last_siblings
    (here,) = terms([(mine, rest)], before=[here])
    return here + from_near


def solution(mesh):
    in_specs = (P(None, ("groups", "blk")), P(None, ("groups", "blk")), P(None, ("groups", "blk")))
    out_specs = P(None, ("groups", "blk"))
    return jax.shard_map(local, mesh=mesh, in_specs=in_specs, out_specs=out_specs, check_vma=False)
```

```python
import functools

import jax
import jax.numpy as jnp
from jax import lax
from jax.experimental import pallas as pl
from jax.experimental.pallas import tpu as pltpu
from jax.sharding import PartitionSpec as P

LOG2E = 1.4426950408889634
NORM_ROWS = 16
ONES_ROWS = 16
STACK = 4
VMEM_LIMIT = 24 << 20


def swapped(value, axis, bit):
    count = lax.axis_size(axis)
    return lax.ppermute(value, axis, [(source, source ^ bit) for source in range(count)])


def split2(value):
    high = value.astype(jnp.bfloat16)
    low = (value - high.astype(jnp.float32)).astype(jnp.bfloat16)
    return high, low


def term_weights(vectors):
    position = lax.broadcasted_iota(jnp.int32, (2 * vectors, 1), 0)
    first = (position == 0) | (position == vectors)
    return jnp.where(first, 0.5, -0.5 / (vectors - 1)).astype(jnp.float32)


def norm_rows(norms, first):
    high = norms.astype(jnp.bfloat16).astype(jnp.float32)
    rest = norms - high
    mid = rest.astype(jnp.bfloat16).astype(jnp.float32)
    row = lax.broadcasted_iota(jnp.int32, (NORM_ROWS, norms.shape[1]), 0)
    at, ones = (0, 3) if first else (3, 0)
    rows = jnp.where((row >= ones) & (row < ones + 3), 1.0, 0.0)
    for place, part in enumerate((high, mid, rest - mid)):
        rows = jnp.where(row == at + place, part, rows)
    return rows.astype(jnp.bfloat16)


def prepared_mine(block, width, vectors):
    feat = block[:width]
    scale = LOG2E / (2.0 * width)
    norms = jnp.sum(feat * feat, axis=0, keepdims=True) * -scale
    high, low = split2(feat * (2.0 * scale))
    dist = jnp.concatenate([high, low, high, norm_rows(norms, True)], 0)
    high, low = split2(block[width:] * term_weights(vectors))
    return dist, jnp.concatenate([high, low, high], 0)


def prepared_theirs(block, width, vectors):
    feat = block[:width]
    scale = LOG2E / (2.0 * width)
    norms = jnp.sum(feat * feat, axis=0, keepdims=True) * -scale
    high, low = split2(feat)
    dist = jnp.concatenate([high, high, low, norm_rows(norms, False)], 0)
    vecs = jnp.concatenate([block[width + vectors :], block[width : width + vectors]], 0)
    vec_high, vec_low = split2(vecs)
    pair = jnp.concatenate([vec_high, vec_high, vec_low], 0)
    ones = jnp.ones((ONES_ROWS, block.shape[1]), jnp.bfloat16)
    return dist.T, pair.T, jnp.concatenate([high, ones, low], 0)


def product(left, right):
    return jnp.dot(left, right, preferred_element_type=jnp.float32)


def pulled_terms(mine, theirs, width):
    dist_mine, pair_mine = mine
    dist_theirs, pair_theirs, pull = theirs
    coupling = jnp.exp2(product(dist_theirs, dist_mine)) * product(pair_theirs, pair_mine)
    high, low = split2(coupling)
    from_high = product(pull, high)
    from_low = product(pull[: width + ONES_ROWS], low)
    pulled = from_high[:width] + from_high[width + ONES_ROWS :] + from_low[:width]
    return pulled, from_high[width : width + 1] + from_low[width : width + 1]


def stacked(theirs):
    dist, pair, pull = zip(*theirs)
    return jnp.concatenate(dist, 0), jnp.concatenate(pair, 0), jnp.concatenate(pull, 1)


def kernel(width, vectors, jobs, count, *refs):
    blocks, refs = refs[:count], refs[count:]
    before, out = refs[: -len(jobs)], refs[-len(jobs) :]
    used = sorted({theirs for _, columns in jobs for theirs in columns})
    theirs = {place: prepared_theirs(blocks[place][...], width, vectors) for place in used}
    for place, (row, columns) in enumerate(jobs):
        mine = prepared_mine(blocks[row][...], width, vectors)
        parts = [
            pulled_terms(mine, stacked([theirs[column] for column in columns[at : at + STACK]]), width)
            for at in range(0, len(columns), STACK)
        ]
        pulled, sums = (sum(part) for part in zip(*parts))
        value = (pulled - blocks[row][:width] * sums) / width
        out[place][...] = value + before[place][...] if place < len(before) else value


def pair_terms(jobs, width, vectors, before=(), weight=2048):
    blocks = []

    def place(block):
        for index, other in enumerate(blocks):
            if other is block:
                return index
        blocks.append(block)
        return len(blocks) - 1

    placed = [(place(row), [place(column) for column in columns]) for row, columns in jobs]
    points = blocks[0].shape[1]
    operands = blocks + list(before)
    out_shape = [jax.ShapeDtypeStruct((width, points), jnp.float32)] * len(jobs)
    return list(
        pl.pallas_call(
            functools.partial(kernel, width, vectors, placed, len(blocks)),
            out_shape=out_shape,
            in_specs=[pl.BlockSpec(memory_space=pltpu.VMEM)] * len(operands),
            out_specs=[pl.BlockSpec(memory_space=pltpu.VMEM)] * len(out_shape),
            compiler_params=pltpu.CompilerParams(vmem_limit_bytes=VMEM_LIMIT),
            cost_estimate=pl.CostEstimate(
                flops=2 * points * points * weight * sum(len(columns) for _, columns in jobs),
                bytes_accessed=4 * points * 96 * len(operands),
                transcendentals=points * points,
            ),
        )(*operands)
    )


def packed(features, solves, probes):
    width, points = features.shape
    vectors = solves.shape[0]

    def body(features_ref, solves_ref, probes_ref, out_ref, vectors_ref):
        out_ref[:width] = features_ref[...]
        for first, ref in ((0, solves_ref), (vectors, probes_ref)):
            out_ref[width + first : width + first + vectors] = ref[...]
            vectors_ref[first : first + vectors] = ref[...]

    return pl.pallas_call(
        body,
        out_shape=[
            jax.ShapeDtypeStruct((rows, points), jnp.float32)
            for rows in (width + 2 * vectors, 2 * vectors)
        ],
        compiler_params=pltpu.CompilerParams(vmem_limit_bytes=60 << 20),
    )(features, solves, probes)


def local(features, solves, probes):
    width = features.shape[0]
    vectors = solves.shape[0]
    count = lax.axis_size("blk")
    terms = functools.partial(pair_terms, width=width, vectors=vectors)
    swap = lambda value, bit: swapped(value, "blk", bit)
    tied = lax.optimization_barrier

    bits = [1 << place for place in range(count.bit_length() - 1)]
    top, beside = bits[-1], [bit for bit in bits[:-1] if bit not in (1, 4)]
    far_features = swap(features, top)
    mine, my_vectors = packed(features, solves, probes)
    far_vectors = swap(my_vectors, top)
    sibling = swap(mine, 1)
    near = swap(mine, 4)
    direct = [swap(mine, bit) for bit in beside]

    far_features, own = tied((far_features, mine))
    (here,) = terms([(own, [own])], weight=512)
    far_vectors, here = tied((far_vectors, here))
    split = [far_features, far_vectors]
    far = jnp.concatenate(split, 0)
    last = []
    for bit in beside:
        pieces = [split] + [[block[:width], block[width:]] for block in last]
        last += [jnp.concatenate([swap(piece, bit) for piece in pair], 0) for pair in pieces]
    first = [far] + direct
    siblings = [swap(block, 1) for block in first]
    (there,) = terms([(near, [mine, sibling] + first)], weight=512)
    (there,) = terms([(near, siblings)], before=[there], weight=2048)
    last[0], there = tied((last[0], there))
    last_siblings = [swap(block, 1) for block in last]
    (there,) = terms([(near, last)], before=[there])
    (there,) = terms([(near, last_siblings)], before=[there])
    from_near = swap(there, 4)
    rest = [sibling] + first + siblings + last + last_siblings
    (here,) = terms([(mine, rest)], before=[here])
    return here + from_near


def solution(mesh):
    in_specs = (P(None, ("groups", "blk")), P(None, ("groups", "blk")), P(None, ("groups", "blk")))
    out_specs = P(None, ("groups", "blk"))
    return jax.shard_map(local, mesh=mesh, in_specs=in_specs, out_specs=out_specs, check_vma=False)
```

```python
import functools

import jax
import jax.numpy as jnp
from jax import lax
from jax.experimental import pallas as pl
from jax.experimental.pallas import tpu as pltpu
from jax.sharding import PartitionSpec as P

LOG2E = 1.4426950408889634
NORM_ROWS = 16
ONES_ROWS = 16
STACK = 4
VMEM_LIMIT = 24 << 20


def swapped(value, axis, bit):
    count = lax.axis_size(axis)
    return lax.ppermute(value, axis, [(source, source ^ bit) for source in range(count)])


def split2(value):
    high = value.astype(jnp.bfloat16)
    low = (value - high.astype(jnp.float32)).astype(jnp.bfloat16)
    return high, low


def term_weights(vectors):
    position = lax.broadcasted_iota(jnp.int32, (2 * vectors, 1), 0)
    first = (position == 0) | (position == vectors)
    return jnp.where(first, 0.5, -0.5 / (vectors - 1)).astype(jnp.float32)


def norm_rows(norms, first):
    high = norms.astype(jnp.bfloat16).astype(jnp.float32)
    rest = norms - high
    mid = rest.astype(jnp.bfloat16).astype(jnp.float32)
    row = lax.broadcasted_iota(jnp.int32, (NORM_ROWS, norms.shape[1]), 0)
    at, ones = (0, 3) if first else (3, 0)
    rows = jnp.where((row >= ones) & (row < ones + 3), 1.0, 0.0)
    for place, part in enumerate((high, mid, rest - mid)):
        rows = jnp.where(row == at + place, part, rows)
    return rows.astype(jnp.bfloat16)


def prepared_mine(block, width, vectors):
    feat = block[:width]
    scale = LOG2E / (2.0 * width)
    norms = jnp.sum(feat * feat, axis=0, keepdims=True) * -scale
    high, low = split2(feat * (2.0 * scale))
    dist = jnp.concatenate([high, low, high, norm_rows(norms, True)], 0)
    high, low = split2(block[width:] * term_weights(vectors))
    return dist, jnp.concatenate([high, low, high], 0)


def prepared_theirs(block, width, vectors):
    feat = block[:width]
    scale = LOG2E / (2.0 * width)
    norms = jnp.sum(feat * feat, axis=0, keepdims=True) * -scale
    high, low = split2(feat)
    dist = jnp.concatenate([high, high, low, norm_rows(norms, False)], 0)
    vecs = jnp.concatenate([block[width + vectors :], block[width : width + vectors]], 0)
    vec_high, vec_low = split2(vecs)
    pair = jnp.concatenate([vec_high, vec_high, vec_low], 0)
    ones = jnp.ones((ONES_ROWS, block.shape[1]), jnp.bfloat16)
    return dist.T, pair.T, jnp.concatenate([high, ones, low], 0)


def product(left, right):
    return jnp.dot(left, right, preferred_element_type=jnp.float32)


def pulled_terms(mine, theirs, width):
    dist_mine, pair_mine = mine
    dist_theirs, pair_theirs, pull = theirs
    coupling = jnp.exp2(product(dist_theirs, dist_mine)) * product(pair_theirs, pair_mine)
    high, low = split2(coupling)
    from_high = product(pull, high)
    from_low = product(pull[: width + ONES_ROWS], low)
    pulled = from_high[:width] + from_high[width + ONES_ROWS :] + from_low[:width]
    return pulled, from_high[width : width + 1] + from_low[width : width + 1]


def stacked(theirs):
    dist, pair, pull = zip(*theirs)
    return jnp.concatenate(dist, 0), jnp.concatenate(pair, 0), jnp.concatenate(pull, 1)


def kernel(width, vectors, jobs, count, pieces, *refs):
    blocks, refs = refs[:count], refs[count:]
    results = len(jobs) * pieces
    before, out = refs[:-results], refs[-results:]
    used = sorted({theirs for _, columns in jobs for theirs in columns})
    theirs = {place: prepared_theirs(blocks[place][...], width, vectors) for place in used}
    for place, (row, columns) in enumerate(jobs):
        mine = prepared_mine(blocks[row][...], width, vectors)
        parts = [
            pulled_terms(mine, stacked([theirs[column] for column in columns[at : at + STACK]]), width)
            for at in range(0, len(columns), STACK)
        ]
        pulled, sums = (sum(part) for part in zip(*parts))
        value = (pulled - blocks[row][:width] * sums) / width
        value = value + before[place][...] if place < len(before) else value
        rows = width // pieces
        for piece in range(pieces):
            out[place * pieces + piece][...] = value[piece * rows : (piece + 1) * rows]


def pair_terms(jobs, width, vectors, before=(), weight=2048, pieces=1):
    blocks = []

    def place(block):
        for index, other in enumerate(blocks):
            if other is block:
                return index
        blocks.append(block)
        return len(blocks) - 1

    placed = [(place(row), [place(column) for column in columns]) for row, columns in jobs]
    points = blocks[0].shape[1]
    operands = blocks + list(before)
    shape = jax.ShapeDtypeStruct((width // pieces, points), jnp.float32)
    out_shape = [shape] * (len(jobs) * pieces)
    return list(
        pl.pallas_call(
            functools.partial(kernel, width, vectors, placed, len(blocks), pieces),
            out_shape=out_shape,
            in_specs=[pl.BlockSpec(memory_space=pltpu.VMEM)] * len(operands),
            out_specs=[pl.BlockSpec(memory_space=pltpu.VMEM)] * len(out_shape),
            compiler_params=pltpu.CompilerParams(vmem_limit_bytes=VMEM_LIMIT),
            cost_estimate=pl.CostEstimate(
                flops=2 * points * points * weight * sum(len(columns) for _, columns in jobs),
                bytes_accessed=4 * points * 96 * len(operands),
                transcendentals=points * points,
            ),
        )(*operands)
    )


def packed(features, solves, probes):
    width, points = features.shape
    vectors = solves.shape[0]

    def body(features_ref, solves_ref, probes_ref, out_ref, vectors_ref):
        out_ref[:width] = features_ref[...]
        for first, ref in ((0, solves_ref), (vectors, probes_ref)):
            out_ref[width + first : width + first + vectors] = ref[...]
            vectors_ref[first : first + vectors] = ref[...]

    return pl.pallas_call(
        body,
        out_shape=[
            jax.ShapeDtypeStruct((rows, points), jnp.float32)
            for rows in (width + 2 * vectors, 2 * vectors)
        ],
        compiler_params=pltpu.CompilerParams(vmem_limit_bytes=60 << 20),
    )(features, solves, probes)


def local(features, solves, probes):
    width = features.shape[0]
    vectors = solves.shape[0]
    count = lax.axis_size("blk")
    terms = functools.partial(pair_terms, width=width, vectors=vectors)
    swap = lambda value, bit: swapped(value, "blk", bit)
    tied = lax.optimization_barrier

    bits = [1 << place for place in range(count.bit_length() - 1)]
    top, beside = bits[-1], [bit for bit in bits[:-1] if bit not in (1, 4)]
    far_features = swap(features, top)
    mine, my_vectors = packed(features, solves, probes)
    far_vectors = swap(my_vectors, top)
    sibling = swap(mine, 1)
    near = swap(mine, 4)
    direct = [swap(mine, bit) for bit in beside]

    (here,) = terms([(mine, [mine])], weight=64)
    far_features, far_vectors, here = tied((far_features, far_vectors, here))
    far = [far_features, far_vectors]
    last = []
    for bit in beside:
        for pair in [far] + last:
            last = last + [[swap(piece, bit) for piece in pair]]
    first = [jnp.concatenate(far, 0)] + direct
    (there,) = terms([(near, [mine, sibling] + first)], weight=2048)
    swapped_first = swap(jnp.concatenate(first, 0), 1)
    siblings = jnp.split(swapped_first, len(first), 0)
    (there,) = terms([(near, siblings)], before=[there], weight=64)
    *pieces, there = tied((*[piece for pair in last for piece in pair], there))
    last = [jnp.concatenate(pieces[at : at + 2], 0) for at in range(0, len(pieces), 2)]
    last_siblings = [swap(block, 1) for block in last]
    (there,) = terms([(near, last)], before=[there], weight=64)
    rest = [sibling] + first + siblings + last + last_siblings
    toward_near = terms([(near, last_siblings)], before=[there], weight=64, pieces=2)
    from_near = jnp.concatenate([swap(piece, 4) for piece in toward_near], 0)
    (here,) = terms([(mine, rest)], before=[here], weight=2048)
    return here + from_near


def solution(mesh):
    in_specs = (P(None, ("groups", "blk")), P(None, ("groups", "blk")), P(None, ("groups", "blk")))
    out_specs = P(None, ("groups", "blk"))
    return jax.shard_map(local, mesh=mesh, in_specs=in_specs, out_specs=out_specs, check_vma=False)
```

```python
import functools

import jax
import jax.numpy as jnp
from jax import lax
from jax.experimental import pallas as pl
from jax.experimental.pallas import tpu as pltpu
from jax.sharding import PartitionSpec as P

LOG2E = 1.4426950408889634
NORM_ROWS = 16
ONES_ROWS = 16
STACK = 4
VMEM_LIMIT = 24 << 20


def swapped(value, axis, bit):
    count = lax.axis_size(axis)
    return lax.ppermute(value, axis, [(source, source ^ bit) for source in range(count)])


def split2(value):
    high = value.astype(jnp.bfloat16)
    low = (value - high.astype(jnp.float32)).astype(jnp.bfloat16)
    return high, low


def term_weights(vectors):
    position = lax.broadcasted_iota(jnp.int32, (2 * vectors, 1), 0)
    first = (position == 0) | (position == vectors)
    return jnp.where(first, 0.5, -0.5 / (vectors - 1)).astype(jnp.float32)


def norm_rows(norms, first):
    high = norms.astype(jnp.bfloat16).astype(jnp.float32)
    rest = norms - high
    mid = rest.astype(jnp.bfloat16).astype(jnp.float32)
    row = lax.broadcasted_iota(jnp.int32, (NORM_ROWS, norms.shape[1]), 0)
    at, ones = (0, 3) if first else (3, 0)
    rows = jnp.where((row >= ones) & (row < ones + 3), 1.0, 0.0)
    for place, part in enumerate((high, mid, rest - mid)):
        rows = jnp.where(row == at + place, part, rows)
    return rows.astype(jnp.bfloat16)


def prepared_mine(block, width, vectors):
    feat = block[:width]
    scale = LOG2E / (2.0 * width)
    norms = jnp.sum(feat * feat, axis=0, keepdims=True) * -scale
    high, low = split2(feat * (2.0 * scale))
    dist = jnp.concatenate([high, low, high, norm_rows(norms, True)], 0)
    high, low = split2(block[width:] * term_weights(vectors))
    return dist, jnp.concatenate([high, low, high], 0)


def prepared_theirs(block, width, vectors):
    feat = block[:width]
    scale = LOG2E / (2.0 * width)
    norms = jnp.sum(feat * feat, axis=0, keepdims=True) * -scale
    high, low = split2(feat)
    dist = jnp.concatenate([high, high, low, norm_rows(norms, False)], 0)
    vecs = jnp.concatenate([block[width + vectors :], block[width : width + vectors]], 0)
    vec_high, vec_low = split2(vecs)
    pair = jnp.concatenate([vec_high, vec_high, vec_low], 0)
    ones = jnp.ones((ONES_ROWS, block.shape[1]), jnp.bfloat16)
    return dist.T, pair.T, jnp.concatenate([high, ones, low], 0)


def product(left, right):
    return jnp.dot(left, right, preferred_element_type=jnp.float32)


def pulled_terms(mine, theirs, width):
    dist_mine, pair_mine = mine
    dist_theirs, pair_theirs, pull = theirs
    coupling = jnp.exp2(product(dist_theirs, dist_mine)) * product(pair_theirs, pair_mine)
    high, low = split2(coupling)
    from_high = product(pull, high)
    from_low = product(pull[: width + ONES_ROWS], low)
    pulled = from_high[:width] + from_high[width + ONES_ROWS :] + from_low[:width]
    return pulled, from_high[width : width + 1] + from_low[width : width + 1]


def stacked(theirs):
    dist, pair, pull = zip(*theirs)
    return jnp.concatenate(dist, 0), jnp.concatenate(pair, 0), jnp.concatenate(pull, 1)


def kernel(width, vectors, jobs, count, pieces, *refs):
    blocks, refs = refs[:count], refs[count:]
    results = len(jobs) * pieces
    before, out = refs[:-results], refs[-results:]
    used = sorted({theirs for _, columns in jobs for theirs in columns})
    theirs = {place: prepared_theirs(blocks[place][...], width, vectors) for place in used}
    for place, (row, columns) in enumerate(jobs):
        mine = prepared_mine(blocks[row][...], width, vectors)
        parts = [
            pulled_terms(mine, stacked([theirs[column] for column in columns[at : at + STACK]]), width)
            for at in range(0, len(columns), STACK)
        ]
        pulled, sums = (sum(part) for part in zip(*parts))
        value = (pulled - blocks[row][:width] * sums) / width
        value = value + before[place][...] if place < len(before) else value
        rows = width // pieces
        for piece in range(pieces):
            out[place * pieces + piece][...] = value[piece * rows : (piece + 1) * rows]


def pair_terms(jobs, width, vectors, before=(), weight=2048, pieces=1):
    blocks = []

    def place(block):
        for index, other in enumerate(blocks):
            if other is block:
                return index
        blocks.append(block)
        return len(blocks) - 1

    placed = [(place(row), [place(column) for column in columns]) for row, columns in jobs]
    points = blocks[0].shape[1]
    operands = blocks + list(before)
    shape = jax.ShapeDtypeStruct((width // pieces, points), jnp.float32)
    out_shape = [shape] * (len(jobs) * pieces)
    return list(
        pl.pallas_call(
            functools.partial(kernel, width, vectors, placed, len(blocks), pieces),
            out_shape=out_shape,
            in_specs=[pl.BlockSpec(memory_space=pltpu.VMEM)] * len(operands),
            out_specs=[pl.BlockSpec(memory_space=pltpu.VMEM)] * len(out_shape),
            compiler_params=pltpu.CompilerParams(vmem_limit_bytes=VMEM_LIMIT),
            cost_estimate=pl.CostEstimate(
                flops=2 * points * points * weight * sum(len(columns) for _, columns in jobs),
                bytes_accessed=4 * points * 96 * len(operands),
                transcendentals=points * points,
            ),
        )(*operands)
    )


def packed(features, solves, probes):
    width, points = features.shape
    vectors = solves.shape[0]

    def body(features_ref, solves_ref, probes_ref, out_ref, vectors_ref):
        out_ref[:width] = features_ref[...]
        for first, ref in ((0, solves_ref), (vectors, probes_ref)):
            out_ref[width + first : width + first + vectors] = ref[...]
            vectors_ref[first : first + vectors] = ref[...]

    return pl.pallas_call(
        body,
        out_shape=[
            jax.ShapeDtypeStruct((rows, points), jnp.float32)
            for rows in (width + 2 * vectors, 2 * vectors)
        ],
        compiler_params=pltpu.CompilerParams(vmem_limit_bytes=60 << 20),
    )(features, solves, probes)


def local(features, solves, probes):
    width = features.shape[0]
    vectors = solves.shape[0]
    count = lax.axis_size("blk")
    terms = functools.partial(pair_terms, width=width, vectors=vectors)
    swap = lambda value, bit: swapped(value, "blk", bit)
    tied = lax.optimization_barrier

    bits = [1 << place for place in range(count.bit_length() - 1)]
    top, beside = bits[-1], [bit for bit in bits[:-1] if bit not in (1, 4)]
    far_features = swap(features, top)
    mine, my_vectors = packed(features, solves, probes)
    far_vectors = swap(my_vectors, top)
    sibling = swap(mine, 1)
    near = swap(mine, 4)
    direct = [swap(mine, bit) for bit in beside]

    (here,) = terms([(mine, [mine])], weight=512)
    far_features, far_vectors, here = tied((far_features, far_vectors, here))
    far = [far_features, far_vectors]
    last = []
    for bit in beside:
        for pair in [far] + last:
            last = last + [[swap(piece, bit) for piece in pair]]
    (there,) = terms([(near, [mine])], weight=256)
    *direct, there = tied((*direct, there))
    first = [jnp.concatenate(far, 0)] + direct
    siblings = jnp.split(swap(jnp.concatenate(first, 0), 1), len(first), 0)
    (there,) = terms([(near, [sibling] + first)], before=[there], weight=2048)
    there, here = terms([(near, siblings), (mine, first)], before=[there, here], weight=64)
    *pieces, there = tied((*[piece for pair in last for piece in pair], there))
    last = [jnp.concatenate(pieces[at : at + 2], 0) for at in range(0, len(pieces), 2)]
    last_siblings = [swap(block, 1) for block in last]
    there, here = terms([(near, last), (mine, last)], before=[there, here], weight=64)
    toward_near = terms([(near, last_siblings)], before=[there], weight=64, pieces=2)
    from_near = jnp.concatenate([swap(piece, 4) for piece in toward_near], 0)
    rest = [sibling] + siblings + last_siblings
    (here,) = terms([(mine, rest)], before=[here], weight=2048)
    return here + from_near


def solution(mesh):
    in_specs = (P(None, ("groups", "blk")), P(None, ("groups", "blk")), P(None, ("groups", "blk")))
    out_specs = P(None, ("groups", "blk"))
    return jax.shard_map(local, mesh=mesh, in_specs=in_specs, out_specs=out_specs, check_vma=False)
```

```python
import functools

import jax
import jax.numpy as jnp
from jax import lax
from jax.experimental import pallas as pl
from jax.experimental.pallas import tpu as pltpu
from jax.sharding import PartitionSpec as P

LOG2E = 1.4426950408889634
NORM_ROWS = 16
ONES_ROWS = 16
STACK = 4
VMEM_LIMIT = 24 << 20


def swapped(value, axis, bit):
    count = lax.axis_size(axis)
    return lax.ppermute(value, axis, [(source, source ^ bit) for source in range(count)])


def split2(value):
    high = value.astype(jnp.bfloat16)
    low = (value - high.astype(jnp.float32)).astype(jnp.bfloat16)
    return high, low


def term_weights(vectors):
    position = lax.broadcasted_iota(jnp.int32, (2 * vectors, 1), 0)
    first = (position == 0) | (position == vectors)
    return jnp.where(first, 0.5, -0.5 / (vectors - 1)).astype(jnp.float32)


def norm_rows(norms, first):
    high = norms.astype(jnp.bfloat16).astype(jnp.float32)
    rest = norms - high
    mid = rest.astype(jnp.bfloat16).astype(jnp.float32)
    row = lax.broadcasted_iota(jnp.int32, (NORM_ROWS, norms.shape[1]), 0)
    at, ones = (0, 3) if first else (3, 0)
    rows = jnp.where((row >= ones) & (row < ones + 3), 1.0, 0.0)
    for place, part in enumerate((high, mid, rest - mid)):
        rows = jnp.where(row == at + place, part, rows)
    return rows.astype(jnp.bfloat16)


def prepared_mine(block, width, vectors):
    feat = block[:width]
    scale = LOG2E / (2.0 * width)
    norms = jnp.sum(feat * feat, axis=0, keepdims=True) * -scale
    high, low = split2(feat * (2.0 * scale))
    dist = jnp.concatenate([high, low, high, norm_rows(norms, True)], 0)
    high, low = split2(block[width:] * term_weights(vectors))
    return dist, jnp.concatenate([high, low, high], 0)


def prepared_theirs(block, width, vectors):
    feat = block[:width]
    scale = LOG2E / (2.0 * width)
    norms = jnp.sum(feat * feat, axis=0, keepdims=True) * -scale
    high, low = split2(feat)
    dist = jnp.concatenate([high, high, low, norm_rows(norms, False)], 0)
    vecs = jnp.concatenate([block[width + vectors :], block[width : width + vectors]], 0)
    vec_high, vec_low = split2(vecs)
    pair = jnp.concatenate([vec_high, vec_high, vec_low], 0)
    ones = jnp.ones((ONES_ROWS, block.shape[1]), jnp.bfloat16)
    return dist.T, pair.T, jnp.concatenate([high, ones, low], 0)


def product(left, right):
    return jnp.dot(left, right, preferred_element_type=jnp.float32)


def pulled_terms(mine, theirs, width):
    dist_mine, pair_mine = mine
    dist_theirs, pair_theirs, pull = theirs
    coupling = jnp.exp2(product(dist_theirs, dist_mine)) * product(pair_theirs, pair_mine)
    high, low = split2(coupling)
    from_high = product(pull, high)
    from_low = product(pull[: width + ONES_ROWS], low)
    pulled = from_high[:width] + from_high[width + ONES_ROWS :] + from_low[:width]
    return pulled, from_high[width : width + 1] + from_low[width : width + 1]


def stacked(theirs):
    dist, pair, pull = zip(*theirs)
    return jnp.concatenate(dist, 0), jnp.concatenate(pair, 0), jnp.concatenate(pull, 1)


def kernel(width, vectors, jobs, count, pieces, *refs):
    blocks, refs = refs[:count], refs[count:]
    results = len(jobs) * pieces
    before, out = refs[:-results], refs[-results:]
    used = sorted({theirs for _, columns in jobs for theirs in columns})
    theirs = {place: prepared_theirs(blocks[place][...], width, vectors) for place in used}
    for place, (row, columns) in enumerate(jobs):
        mine = prepared_mine(blocks[row][...], width, vectors)
        parts = [
            pulled_terms(mine, stacked([theirs[column] for column in columns[at : at + STACK]]), width)
            for at in range(0, len(columns), STACK)
        ]
        pulled, sums = (sum(part) for part in zip(*parts))
        value = (pulled - blocks[row][:width] * sums) / width
        value = value + before[place][...] if place < len(before) else value
        rows = width // pieces
        for piece in range(pieces):
            out[place * pieces + piece][...] = value[piece * rows : (piece + 1) * rows]


def pair_terms(jobs, width, vectors, before=(), weight=2048, pieces=1):
    blocks = []

    def place(block):
        for index, other in enumerate(blocks):
            if other is block:
                return index
        blocks.append(block)
        return len(blocks) - 1

    placed = [(place(row), [place(column) for column in columns]) for row, columns in jobs]
    points = blocks[0].shape[1]
    operands = blocks + list(before)
    shape = jax.ShapeDtypeStruct((width // pieces, points), jnp.float32)
    out_shape = [shape] * (len(jobs) * pieces)
    return list(
        pl.pallas_call(
            functools.partial(kernel, width, vectors, placed, len(blocks), pieces),
            out_shape=out_shape,
            in_specs=[pl.BlockSpec(memory_space=pltpu.VMEM)] * len(operands),
            out_specs=[pl.BlockSpec(memory_space=pltpu.VMEM)] * len(out_shape),
            compiler_params=pltpu.CompilerParams(vmem_limit_bytes=VMEM_LIMIT),
            cost_estimate=pl.CostEstimate(
                flops=2 * points * points * weight * sum(len(columns) for _, columns in jobs),
                bytes_accessed=4 * points * 96 * len(operands),
                transcendentals=points * points,
            ),
        )(*operands)
    )


def packed(features, solves, probes):
    width, points = features.shape
    vectors = solves.shape[0]

    def body(features_ref, solves_ref, probes_ref, out_ref, vectors_ref):
        out_ref[:width] = features_ref[...]
        for first, ref in ((0, solves_ref), (vectors, probes_ref)):
            out_ref[width + first : width + first + vectors] = ref[...]
            vectors_ref[first : first + vectors] = ref[...]

    return pl.pallas_call(
        body,
        out_shape=[
            jax.ShapeDtypeStruct((rows, points), jnp.float32)
            for rows in (width + 2 * vectors, 2 * vectors)
        ],
        compiler_params=pltpu.CompilerParams(vmem_limit_bytes=60 << 20),
    )(features, solves, probes)


def local(features, solves, probes):
    width = features.shape[0]
    vectors = solves.shape[0]
    count = lax.axis_size("blk")
    terms = functools.partial(pair_terms, width=width, vectors=vectors)
    swap = lambda value, bit: swapped(value, "blk", bit)
    tied = lax.optimization_barrier

    bits = [1 << place for place in range(count.bit_length() - 1)]
    top, beside = bits[-1], [bit for bit in bits[:-1] if bit not in (1, 4)]
    far_features = swap(features, top)
    mine, my_vectors = packed(features, solves, probes)
    far_vectors = swap(my_vectors, top)
    sibling = swap(mine, 1)
    near = swap(mine, 4)
    direct = [swap(mine, bit) for bit in beside]

    (here,) = terms([(mine, [mine])], weight=512)
    far_features, far_vectors, here = tied((far_features, far_vectors, here))
    far = [far_features, far_vectors]
    last = []
    for bit in beside:
        for pair in [far] + last:
            last = last + [[swap(piece, bit) for piece in pair]]
    far = jnp.concatenate(far, 0)
    (here,) = terms([(mine, [sibling, far])], before=[here], weight=256)
    near, *direct, here = tied((near, *direct, here))
    first = [far] + direct
    siblings = jnp.split(swap(jnp.concatenate(first, 0), 1), len(first), 0)
    (there,) = terms([(near, [mine, sibling] + first)], weight=2048)
    (there,) = terms([(near, siblings)], before=[there], weight=100000)
    *pieces, there = tied((*[piece for pair in last for piece in pair], there))
    last = [jnp.concatenate(pieces[at : at + 2], 0) for at in range(0, len(pieces), 2)]
    last_siblings = [swap(block, 1) for block in last]
    there, here = terms([(near, last), (mine, last)], before=[there, here], weight=64)
    toward_near = terms([(near, last_siblings)], before=[there], weight=8, pieces=2)
    from_near = jnp.concatenate([swap(piece, 4) for piece in toward_near], 0)
    rest = direct + siblings + last_siblings
    (here,) = terms([(mine, rest)], before=[here], weight=100000)
    return here + from_near


def solution(mesh):
    in_specs = (P(None, ("groups", "blk")), P(None, ("groups", "blk")), P(None, ("groups", "blk")))
    out_specs = P(None, ("groups", "blk"))
    return jax.shard_map(local, mesh=mesh, in_specs=in_specs, out_specs=out_specs, check_vma=False)
```

```python
import functools

import jax
import jax.numpy as jnp
from jax import lax
from jax.experimental import pallas as pl
from jax.experimental.pallas import tpu as pltpu
from jax.sharding import PartitionSpec as P

LOG2E = 1.4426950408889634
NORM_ROWS = 16
ONES_ROWS = 16
STACK = 4
VMEM_LIMIT = 24 << 20


def swapped(value, axis, bit):
    count = lax.axis_size(axis)
    return lax.ppermute(value, axis, [(source, source ^ bit) for source in range(count)])


def split2(value):
    high = value.astype(jnp.bfloat16)
    low = (value - high.astype(jnp.float32)).astype(jnp.bfloat16)
    return high, low


def term_weights(vectors):
    position = lax.broadcasted_iota(jnp.int32, (2 * vectors, 1), 0)
    first = (position == 0) | (position == vectors)
    return jnp.where(first, 0.5, -0.5 / (vectors - 1)).astype(jnp.float32)


def norm_rows(norms, first):
    high = norms.astype(jnp.bfloat16).astype(jnp.float32)
    rest = norms - high
    mid = rest.astype(jnp.bfloat16).astype(jnp.float32)
    row = lax.broadcasted_iota(jnp.int32, (NORM_ROWS, norms.shape[1]), 0)
    at, ones = (0, 3) if first else (3, 0)
    rows = jnp.where((row >= ones) & (row < ones + 3), 1.0, 0.0)
    for place, part in enumerate((high, mid, rest - mid)):
        rows = jnp.where(row == at + place, part, rows)
    return rows.astype(jnp.bfloat16)


def prepared_mine(block, width, vectors):
    feat = block[:width]
    scale = LOG2E / (2.0 * width)
    norms = jnp.sum(feat * feat, axis=0, keepdims=True) * -scale
    high, low = split2(feat * (2.0 * scale))
    dist = jnp.concatenate([high, low, high, norm_rows(norms, True)], 0)
    high, low = split2(block[width:] * term_weights(vectors))
    return dist, jnp.concatenate([high, low, high], 0)


def prepared_theirs(block, width, vectors):
    feat = block[:width]
    scale = LOG2E / (2.0 * width)
    norms = jnp.sum(feat * feat, axis=0, keepdims=True) * -scale
    high, low = split2(feat)
    dist = jnp.concatenate([high, high, low, norm_rows(norms, False)], 0)
    vecs = jnp.concatenate([block[width + vectors :], block[width : width + vectors]], 0)
    vec_high, vec_low = split2(vecs)
    pair = jnp.concatenate([vec_high, vec_high, vec_low], 0)
    ones = jnp.ones((ONES_ROWS, block.shape[1]), jnp.bfloat16)
    return dist.T, pair.T, jnp.concatenate([high, ones, low], 0)


def product(left, right):
    return jnp.dot(left, right, preferred_element_type=jnp.float32)


def pulled_terms(mine, theirs, width):
    dist_mine, pair_mine = mine
    dist_theirs, pair_theirs, pull = theirs
    coupling = jnp.exp2(product(dist_theirs, dist_mine)) * product(pair_theirs, pair_mine)
    high, low = split2(coupling)
    from_high = product(pull, high)
    from_low = product(pull[: width + ONES_ROWS], low)
    pulled = from_high[:width] + from_high[width + ONES_ROWS :] + from_low[:width]
    return pulled, from_high[width : width + 1] + from_low[width : width + 1]


def stacked(theirs):
    dist, pair, pull = zip(*theirs)
    return jnp.concatenate(dist, 0), jnp.concatenate(pair, 0), jnp.concatenate(pull, 1)


def kernel(width, vectors, jobs, count, pieces, *refs):
    blocks, refs = refs[:count], refs[count:]
    results = len(jobs) * pieces
    before, out = refs[:-results], refs[-results:]
    used = sorted({theirs for _, columns in jobs for theirs in columns})
    theirs = {place: prepared_theirs(blocks[place][...], width, vectors) for place in used}
    for place, (row, columns) in enumerate(jobs):
        mine = prepared_mine(blocks[row][...], width, vectors)
        parts = [
            pulled_terms(mine, stacked([theirs[column] for column in columns[at : at + STACK]]), width)
            for at in range(0, len(columns), STACK)
        ]
        pulled, sums = (sum(part) for part in zip(*parts))
        value = (pulled - blocks[row][:width] * sums) / width
        value = value + before[place][...] if place < len(before) else value
        rows = width // pieces
        for piece in range(pieces):
            out[place * pieces + piece][...] = value[piece * rows : (piece + 1) * rows]


def pair_terms(jobs, width, vectors, before=(), weight=2048, pieces=1):
    blocks = []

    def place(block):
        for index, other in enumerate(blocks):
            if other is block:
                return index
        blocks.append(block)
        return len(blocks) - 1

    placed = [(place(row), [place(column) for column in columns]) for row, columns in jobs]
    points = blocks[0].shape[1]
    operands = blocks + list(before)
    shape = jax.ShapeDtypeStruct((width // pieces, points), jnp.float32)
    out_shape = [shape] * (len(jobs) * pieces)
    return list(
        pl.pallas_call(
            functools.partial(kernel, width, vectors, placed, len(blocks), pieces),
            out_shape=out_shape,
            in_specs=[pl.BlockSpec(memory_space=pltpu.VMEM)] * len(operands),
            out_specs=[pl.BlockSpec(memory_space=pltpu.VMEM)] * len(out_shape),
            compiler_params=pltpu.CompilerParams(vmem_limit_bytes=VMEM_LIMIT),
            cost_estimate=pl.CostEstimate(
                flops=2 * points * points * weight * sum(len(columns) for _, columns in jobs),
                bytes_accessed=4 * points * 96 * len(operands),
                transcendentals=points * points,
            ),
        )(*operands)
    )


def packed(features, solves, probes):
    width, points = features.shape
    vectors = solves.shape[0]

    def body(features_ref, solves_ref, probes_ref, out_ref, vectors_ref):
        out_ref[:width] = features_ref[...]
        for first, ref in ((0, solves_ref), (vectors, probes_ref)):
            out_ref[width + first : width + first + vectors] = ref[...]
            vectors_ref[first : first + vectors] = ref[...]

    return pl.pallas_call(
        body,
        out_shape=[
            jax.ShapeDtypeStruct((rows, points), jnp.float32)
            for rows in (width + 2 * vectors, 2 * vectors)
        ],
        compiler_params=pltpu.CompilerParams(vmem_limit_bytes=60 << 20),
    )(features, solves, probes)


def local(features, solves, probes):
    width = features.shape[0]
    vectors = solves.shape[0]
    count = lax.axis_size("blk")
    terms = functools.partial(pair_terms, width=width, vectors=vectors)
    swap = lambda value, bit: swapped(value, "blk", bit)
    tied = lax.optimization_barrier

    bits = [1 << place for place in range(count.bit_length() - 1)]
    top, beside = bits[-1], [bit for bit in bits[:-1] if bit not in (1, 4)]
    far_features = swap(features, top)
    mine, my_vectors = packed(features, solves, probes)
    far_vectors = swap(my_vectors, top)
    sibling = swap(mine, 1)
    near = swap(mine, 4)
    direct = [swap(mine, bit) for bit in beside]

    (here,) = terms([(mine, [mine])], weight=1024)
    far_features, far_vectors, here = tied((far_features, far_vectors, here))
    far = [far_features, far_vectors]
    last = []
    for bit in beside:
        for pair in [far] + last:
            last = last + [[swap(piece, bit) for piece in pair]]
    first = [jnp.concatenate(far, 0)] + direct
    siblings = [swap(block, 1) for block in first]
    (there,) = terms([(near, [mine, sibling] + first)], weight=1024)
    there, here = terms([(near, siblings), (mine, first)], before=[there, here], weight=2048)
    *pieces, there = tied((*[piece for pair in last for piece in pair], there))
    last = [jnp.concatenate(pieces[at : at + 2], 0) for at in range(0, len(pieces), 2)]
    last_siblings = [swap(block, 1) for block in last]
    there, here = terms([(near, last), (mine, last)], before=[there, here], weight=64)
    (there,) = terms([(near, last_siblings)], before=[there], weight=2048)
    from_near = swap(there, 4)
    rest = [sibling] + siblings + last_siblings
    (here,) = terms([(mine, rest)], before=[here], weight=2048)
    return here + from_near


def solution(mesh):
    in_specs = (P(None, ("groups", "blk")), P(None, ("groups", "blk")), P(None, ("groups", "blk")))
    out_specs = P(None, ("groups", "blk"))
    return jax.shard_map(local, mesh=mesh, in_specs=in_specs, out_specs=out_specs, check_vma=False)
```

```python
import functools

import jax
import jax.numpy as jnp
from jax import lax
from jax.experimental import pallas as pl
from jax.experimental.pallas import tpu as pltpu
from jax.sharding import PartitionSpec as P

LOG2E = 1.4426950408889634
NORM_ROWS = 16
ONES_ROWS = 16
STACK = 4
VMEM_LIMIT = 24 << 20


def swapped(value, axis, bit):
    count = lax.axis_size(axis)
    return lax.ppermute(value, axis, [(source, source ^ bit) for source in range(count)])


def split2(value):
    high = value.astype(jnp.bfloat16)
    low = (value - high.astype(jnp.float32)).astype(jnp.bfloat16)
    return high, low


def term_weights(vectors):
    position = lax.broadcasted_iota(jnp.int32, (2 * vectors, 1), 0)
    first = (position == 0) | (position == vectors)
    return jnp.where(first, 0.5, -0.5 / (vectors - 1)).astype(jnp.float32)


def norm_rows(norms, first):
    high = norms.astype(jnp.bfloat16).astype(jnp.float32)
    rest = norms - high
    mid = rest.astype(jnp.bfloat16).astype(jnp.float32)
    row = lax.broadcasted_iota(jnp.int32, (NORM_ROWS, norms.shape[1]), 0)
    at, ones = (0, 3) if first else (3, 0)
    rows = jnp.where((row >= ones) & (row < ones + 3), 1.0, 0.0)
    for place, part in enumerate((high, mid, rest - mid)):
        rows = jnp.where(row == at + place, part, rows)
    return rows.astype(jnp.bfloat16)


def prepared_mine(block, width, vectors):
    feat = block[:width]
    scale = LOG2E / (2.0 * width)
    norms = jnp.sum(feat * feat, axis=0, keepdims=True) * -scale
    high, low = split2(feat * (2.0 * scale))
    dist = jnp.concatenate([high, low, high, norm_rows(norms, True)], 0)
    high, low = split2(block[width:] * term_weights(vectors))
    return dist, jnp.concatenate([high, low, high], 0)


def prepared_theirs(block, width, vectors):
    feat = block[:width]
    scale = LOG2E / (2.0 * width)
    norms = jnp.sum(feat * feat, axis=0, keepdims=True) * -scale
    high, low = split2(feat)
    dist = jnp.concatenate([high, high, low, norm_rows(norms, False)], 0)
    vecs = jnp.concatenate([block[width + vectors :], block[width : width + vectors]], 0)
    vec_high, vec_low = split2(vecs)
    pair = jnp.concatenate([vec_high, vec_high, vec_low], 0)
    ones = jnp.ones((ONES_ROWS, block.shape[1]), jnp.bfloat16)
    return dist.T, pair.T, jnp.concatenate([high, ones, low], 0)


def product(left, right):
    return jnp.dot(left, right, preferred_element_type=jnp.float32)


def pulled_terms(mine, theirs, width):
    dist_mine, pair_mine = mine
    dist_theirs, pair_theirs, pull = theirs
    coupling = jnp.exp2(product(dist_theirs, dist_mine)) * product(pair_theirs, pair_mine)
    high, low = split2(coupling)
    from_high = product(pull, high)
    from_low = product(pull[: width + ONES_ROWS], low)
    pulled = from_high[:width] + from_high[width + ONES_ROWS :] + from_low[:width]
    return pulled, from_high[width : width + 1] + from_low[width : width + 1]


def stacked(theirs):
    dist, pair, pull = zip(*theirs)
    return jnp.concatenate(dist, 0), jnp.concatenate(pair, 0), jnp.concatenate(pull, 1)


def kernel(width, vectors, jobs, count, pieces, *refs):
    blocks, refs = refs[:count], refs[count:]
    results = len(jobs) * pieces
    before, out = refs[:-results], refs[-results:]
    used = sorted({theirs for _, columns in jobs for theirs in columns})
    theirs = {place: prepared_theirs(blocks[place][...], width, vectors) for place in used}
    for place, (row, columns) in enumerate(jobs):
        mine = prepared_mine(blocks[row][...], width, vectors)
        parts = [
            pulled_terms(mine, stacked([theirs[column] for column in columns[at : at + STACK]]), width)
            for at in range(0, len(columns), STACK)
        ]
        pulled, sums = (sum(part) for part in zip(*parts))
        value = (pulled - blocks[row][:width] * sums) / width
        value = value + before[place][...] if place < len(before) else value
        rows = width // pieces
        for piece in range(pieces):
            out[place * pieces + piece][...] = value[piece * rows : (piece + 1) * rows]


def pair_terms(jobs, width, vectors, before=(), weight=2048, pieces=1):
    blocks = []

    def place(block):
        for index, other in enumerate(blocks):
            if other is block:
                return index
        blocks.append(block)
        return len(blocks) - 1

    placed = [(place(row), [place(column) for column in columns]) for row, columns in jobs]
    points = blocks[0].shape[1]
    operands = blocks + list(before)
    shape = jax.ShapeDtypeStruct((width // pieces, points), jnp.float32)
    out_shape = [shape] * (len(jobs) * pieces)
    return list(
        pl.pallas_call(
            functools.partial(kernel, width, vectors, placed, len(blocks), pieces),
            out_shape=out_shape,
            in_specs=[pl.BlockSpec(memory_space=pltpu.VMEM)] * len(operands),
            out_specs=[pl.BlockSpec(memory_space=pltpu.VMEM)] * len(out_shape),
            compiler_params=pltpu.CompilerParams(vmem_limit_bytes=VMEM_LIMIT),
            cost_estimate=pl.CostEstimate(
                flops=2 * points * points * weight * sum(len(columns) for _, columns in jobs),
                bytes_accessed=4 * points * 96 * len(operands),
                transcendentals=points * points,
            ),
        )(*operands)
    )


def packed(features, solves, probes):
    width, points = features.shape
    vectors = solves.shape[0]

    def body(features_ref, solves_ref, probes_ref, out_ref, vectors_ref):
        out_ref[:width] = features_ref[...]
        for first, ref in ((0, solves_ref), (vectors, probes_ref)):
            out_ref[width + first : width + first + vectors] = ref[...]
            vectors_ref[first : first + vectors] = ref[...]

    return pl.pallas_call(
        body,
        out_shape=[
            jax.ShapeDtypeStruct((rows, points), jnp.float32)
            for rows in (width + 2 * vectors, 2 * vectors)
        ],
        compiler_params=pltpu.CompilerParams(vmem_limit_bytes=60 << 20),
    )(features, solves, probes)


def local(features, solves, probes):
    width = features.shape[0]
    vectors = solves.shape[0]
    count = lax.axis_size("blk")
    terms = functools.partial(pair_terms, width=width, vectors=vectors)
    swap = lambda value, bit: swapped(value, "blk", bit)
    tied = lax.optimization_barrier

    bits = [1 << place for place in range(count.bit_length() - 1)]
    top, beside = bits[-1], [bit for bit in bits[:-1] if bit not in (1, 4)]
    far_features = swap(features, top)
    mine, my_vectors = packed(features, solves, probes)
    far_vectors = swap(my_vectors, top)
    sibling = swap(mine, 1)
    near = swap(mine, 4)
    direct = [swap(mine, bit) for bit in beside]

    (here,) = terms([(mine, [mine])], weight=1024)
    far_features, far_vectors, here = tied((far_features, far_vectors, here))
    far = [far_features, far_vectors]
    last = []
    for bit in beside:
        for pair in [far] + last:
            last = last + [[swap(piece, bit) for piece in pair]]
    first = [jnp.concatenate(far, 0)] + direct
    siblings = [swap(block, 1) for block in first]
    (there,) = terms([(near, [mine, sibling] + first)], weight=1024)
    (there,) = terms([(near, siblings)], before=[there], weight=512)
    *pieces, there = tied((*[piece for pair in last for piece in pair], there))
    last = [jnp.concatenate(pieces[at : at + 2], 0) for at in range(0, len(pieces), 2)]
    last_siblings = [swap(block, 1) for block in last]
    there, here = terms([(near, last), (mine, last)], before=[there, here], weight=64)
    toward_near = terms([(near, last_siblings)], before=[there], weight=64, pieces=2)
    from_near = jnp.concatenate([swap(piece, 4) for piece in toward_near], 0)
    rest = [sibling] + first + siblings + last_siblings
    (here,) = terms([(mine, rest)], before=[here], weight=2048)
    return here + from_near


def solution(mesh):
    in_specs = (P(None, ("groups", "blk")), P(None, ("groups", "blk")), P(None, ("groups", "blk")))
    out_specs = P(None, ("groups", "blk"))
    return jax.shard_map(local, mesh=mesh, in_specs=in_specs, out_specs=out_specs, check_vma=False)
```

```python
import functools

import jax
import jax.numpy as jnp
from jax import lax
from jax.experimental import pallas as pl
from jax.experimental.pallas import tpu as pltpu
from jax.sharding import PartitionSpec as P

LOG2E = 1.4426950408889634
NORM_ROWS = 16
ONES_ROWS = 16
STACK = 4
VMEM_LIMIT = 24 << 20


def swapped(value, axis, bit):
    count = lax.axis_size(axis)
    return lax.ppermute(value, axis, [(source, source ^ bit) for source in range(count)])


def split2(value):
    high = value.astype(jnp.bfloat16)
    low = (value - high.astype(jnp.float32)).astype(jnp.bfloat16)
    return high, low


def term_weights(vectors):
    position = lax.broadcasted_iota(jnp.int32, (2 * vectors, 1), 0)
    first = (position == 0) | (position == vectors)
    return jnp.where(first, 0.5, -0.5 / (vectors - 1)).astype(jnp.float32)


def norm_rows(norms, first):
    high = norms.astype(jnp.bfloat16).astype(jnp.float32)
    rest = norms - high
    mid = rest.astype(jnp.bfloat16).astype(jnp.float32)
    row = lax.broadcasted_iota(jnp.int32, (NORM_ROWS, norms.shape[1]), 0)
    at, ones = (0, 3) if first else (3, 0)
    rows = jnp.where((row >= ones) & (row < ones + 3), 1.0, 0.0)
    for place, part in enumerate((high, mid, rest - mid)):
        rows = jnp.where(row == at + place, part, rows)
    return rows.astype(jnp.bfloat16)


def prepared_mine(block, width, vectors):
    feat = block[:width]
    scale = LOG2E / (2.0 * width)
    norms = jnp.sum(feat * feat, axis=0, keepdims=True) * -scale
    high, low = split2(feat * (2.0 * scale))
    dist = jnp.concatenate([high, low, high, norm_rows(norms, True)], 0)
    high, low = split2(block[width:] * term_weights(vectors))
    return dist, jnp.concatenate([high, low, high], 0)


def prepared_theirs(block, width, vectors):
    feat = block[:width]
    scale = LOG2E / (2.0 * width)
    norms = jnp.sum(feat * feat, axis=0, keepdims=True) * -scale
    high, low = split2(feat)
    dist = jnp.concatenate([high, high, low, norm_rows(norms, False)], 0)
    vecs = jnp.concatenate([block[width + vectors :], block[width : width + vectors]], 0)
    vec_high, vec_low = split2(vecs)
    pair = jnp.concatenate([vec_high, vec_high, vec_low], 0)
    ones = jnp.ones((ONES_ROWS, block.shape[1]), jnp.bfloat16)
    return dist.T, pair.T, jnp.concatenate([high, ones, low], 0)


def product(left, right):
    return jnp.dot(left, right, preferred_element_type=jnp.float32)


def pulled_terms(mine, theirs, width):
    dist_mine, pair_mine = mine
    dist_theirs, pair_theirs, pull = theirs
    coupling = jnp.exp2(product(dist_theirs, dist_mine)) * product(pair_theirs, pair_mine)
    high, low = split2(coupling)
    from_high = product(pull, high)
    from_low = product(pull[: width + ONES_ROWS], low)
    pulled = from_high[:width] + from_high[width + ONES_ROWS :] + from_low[:width]
    return pulled, from_high[width : width + 1] + from_low[width : width + 1]


def stacked(theirs):
    dist, pair, pull = zip(*theirs)
    return jnp.concatenate(dist, 0), jnp.concatenate(pair, 0), jnp.concatenate(pull, 1)


def kernel(width, vectors, jobs, count, pieces, *refs):
    blocks, refs = refs[:count], refs[count:]
    results = len(jobs) * pieces
    before, out = refs[:-results], refs[-results:]
    used = sorted({theirs for _, columns in jobs for theirs in columns})
    theirs = {place: prepared_theirs(blocks[place][...], width, vectors) for place in used}
    for place, (row, columns) in enumerate(jobs):
        mine = prepared_mine(blocks[row][...], width, vectors)
        parts = [
            pulled_terms(mine, stacked([theirs[column] for column in columns[at : at + STACK]]), width)
            for at in range(0, len(columns), STACK)
        ]
        pulled, sums = (sum(part) for part in zip(*parts))
        value = (pulled - blocks[row][:width] * sums) / width
        value = value + before[place][...] if place < len(before) else value
        rows = width // pieces
        for piece in range(pieces):
            out[place * pieces + piece][...] = value[piece * rows : (piece + 1) * rows]


def pair_terms(jobs, width, vectors, before=(), weight=2048, pieces=1):
    blocks = []

    def place(block):
        for index, other in enumerate(blocks):
            if other is block:
                return index
        blocks.append(block)
        return len(blocks) - 1

    placed = [(place(row), [place(column) for column in columns]) for row, columns in jobs]
    points = blocks[0].shape[1]
    operands = blocks + list(before)
    shape = jax.ShapeDtypeStruct((width // pieces, points), jnp.float32)
    out_shape = [shape] * (len(jobs) * pieces)
    return list(
        pl.pallas_call(
            functools.partial(kernel, width, vectors, placed, len(blocks), pieces),
            out_shape=out_shape,
            in_specs=[pl.BlockSpec(memory_space=pltpu.VMEM)] * len(operands),
            out_specs=[pl.BlockSpec(memory_space=pltpu.VMEM)] * len(out_shape),
            compiler_params=pltpu.CompilerParams(vmem_limit_bytes=VMEM_LIMIT),
            cost_estimate=pl.CostEstimate(
                flops=2 * points * points * weight * sum(len(columns) for _, columns in jobs),
                bytes_accessed=4 * points * 96 * len(operands),
                transcendentals=points * points,
            ),
        )(*operands)
    )


def packed(features, solves, probes):
    width, points = features.shape
    vectors = solves.shape[0]

    def body(features_ref, solves_ref, probes_ref, out_ref):
        out_ref[:width] = features_ref[...]
        out_ref[width : width + vectors] = solves_ref[...]
        out_ref[width + vectors :] = probes_ref[...]

    return pl.pallas_call(
        body,
        out_shape=jax.ShapeDtypeStruct((width + 2 * vectors, points), jnp.float32),
        compiler_params=pltpu.CompilerParams(vmem_limit_bytes=60 << 20),
    )(features, solves, probes)


def local(features, solves, probes):
    width = features.shape[0]
    vectors = solves.shape[0]
    count = lax.axis_size("blk")
    terms = functools.partial(pair_terms, width=width, vectors=vectors)
    swap = lambda value, bit: swapped(value, "blk", bit)
    tied = lax.optimization_barrier

    bits = [1 << place for place in range(count.bit_length() - 1)]
    top, beside = bits[-1], [bit for bit in bits[:-1] if bit not in (1, 4)]
    far_features = swap(features, top)
    far_vectors = [swap(part, top) for part in (solves, probes)]
    mine = packed(features, solves, probes)
    sibling = swap(mine, 1)
    near = swap(mine, 4)
    direct = [swap(mine, bit) for bit in beside]

    far_features, own = tied((far_features, mine))
    (here,) = terms([(own, [own])], weight=1024)
    *far_vectors, here = tied((*far_vectors, here))
    far = [far_features, jnp.concatenate(far_vectors, 0)]
    last = []
    for bit in beside:
        for pair in [far] + last:
            last = last + [[swap(piece, bit) for piece in pair]]
    first = [jnp.concatenate(far, 0)] + direct
    siblings = [swap(block, 1) for block in first]
    (there,) = terms([(near, [mine, sibling] + first)], weight=1024)
    (there,) = terms([(near, siblings)], before=[there], weight=512)
    *pieces, there = tied((*[piece for pair in last for piece in pair], there))
    last = [jnp.concatenate(pieces[at : at + 2], 0) for at in range(0, len(pieces), 2)]
    last_siblings = [swap(block, 1) for block in last]
    there, here = terms([(near, last), (mine, last)], before=[there, here], weight=64)
    toward_near = terms([(near, last_siblings)], before=[there], weight=64)
    from_near = swap(toward_near[0], 4)
    rest = [sibling] + first + siblings + last_siblings
    (here,) = terms([(mine, rest)], before=[here], weight=2048)
    return here + from_near


def solution(mesh):
    in_specs = (P(None, ("groups", "blk")), P(None, ("groups", "blk")), P(None, ("groups", "blk")))
    out_specs = P(None, ("groups", "blk"))
    return jax.shard_map(local, mesh=mesh, in_specs=in_specs, out_specs=out_specs, check_vma=False)
```

```python
import functools

import jax
import jax.numpy as jnp
from jax import lax
from jax.experimental import pallas as pl
from jax.experimental.pallas import tpu as pltpu
from jax.sharding import PartitionSpec as P

LOG2E = 1.4426950408889634
NORM_ROWS = 16
ONES_ROWS = 16
STACK = 4
VMEM_LIMIT = 24 << 20


def swapped(value, axis, bit):
    count = lax.axis_size(axis)
    return lax.ppermute(value, axis, [(source, source ^ bit) for source in range(count)])


def split2(value):
    high = value.astype(jnp.bfloat16)
    low = (value - high.astype(jnp.float32)).astype(jnp.bfloat16)
    return high, low


def term_weights(vectors):
    position = lax.broadcasted_iota(jnp.int32, (2 * vectors, 1), 0)
    first = (position == 0) | (position == vectors)
    return jnp.where(first, 0.5, -0.5 / (vectors - 1)).astype(jnp.float32)


def norm_rows(norms, first):
    high = norms.astype(jnp.bfloat16).astype(jnp.float32)
    rest = norms - high
    mid = rest.astype(jnp.bfloat16).astype(jnp.float32)
    row = lax.broadcasted_iota(jnp.int32, (NORM_ROWS, norms.shape[1]), 0)
    at, ones = (0, 3) if first else (3, 0)
    rows = jnp.where((row >= ones) & (row < ones + 3), 1.0, 0.0)
    for place, part in enumerate((high, mid, rest - mid)):
        rows = jnp.where(row == at + place, part, rows)
    return rows.astype(jnp.bfloat16)


def prepared_mine(block, width, vectors):
    feat = block[:width]
    scale = LOG2E / (2.0 * width)
    norms = jnp.sum(feat * feat, axis=0, keepdims=True) * -scale
    high, low = split2(feat * (2.0 * scale))
    dist = jnp.concatenate([high, low, high, norm_rows(norms, True)], 0)
    high, low = split2(block[width:] * term_weights(vectors))
    return dist, jnp.concatenate([high, low, high], 0)


def prepared_theirs(block, width, vectors):
    feat = block[:width]
    scale = LOG2E / (2.0 * width)
    norms = jnp.sum(feat * feat, axis=0, keepdims=True) * -scale
    high, low = split2(feat)
    dist = jnp.concatenate([high, high, low, norm_rows(norms, False)], 0)
    vecs = jnp.concatenate([block[width + vectors :], block[width : width + vectors]], 0)
    vec_high, vec_low = split2(vecs)
    pair = jnp.concatenate([vec_high, vec_high, vec_low], 0)
    ones = jnp.ones((ONES_ROWS, block.shape[1]), jnp.bfloat16)
    return dist.T, pair.T, jnp.concatenate([high, ones, low], 0)


def product(left, right):
    return jnp.dot(left, right, preferred_element_type=jnp.float32)


def pulled_terms(mine, theirs, width):
    dist_mine, pair_mine = mine
    dist_theirs, pair_theirs, pull = theirs
    coupling = jnp.exp2(product(dist_theirs, dist_mine)) * product(pair_theirs, pair_mine)
    high, low = split2(coupling)
    from_high = product(pull, high)
    from_low = product(pull[: width + ONES_ROWS], low)
    pulled = from_high[:width] + from_high[width + ONES_ROWS :] + from_low[:width]
    return pulled, from_high[width : width + 1] + from_low[width : width + 1]


def stacked(theirs):
    dist, pair, pull = zip(*theirs)
    return jnp.concatenate(dist, 0), jnp.concatenate(pair, 0), jnp.concatenate(pull, 1)


def kernel(width, vectors, jobs, count, pieces, *refs):
    blocks, refs = refs[:count], refs[count:]
    results = len(jobs) * pieces
    before, out = refs[:-results], refs[-results:]
    used = sorted({theirs for _, columns in jobs for theirs in columns})
    theirs = {place: prepared_theirs(blocks[place][...], width, vectors) for place in used}
    for place, (row, columns) in enumerate(jobs):
        mine = prepared_mine(blocks[row][...], width, vectors)
        parts = [
            pulled_terms(mine, stacked([theirs[column] for column in columns[at : at + STACK]]), width)
            for at in range(0, len(columns), STACK)
        ]
        pulled, sums = (sum(part) for part in zip(*parts))
        value = (pulled - blocks[row][:width] * sums) / width
        value = value + before[place][...] if place < len(before) else value
        rows = width // pieces
        for piece in range(pieces):
            out[place * pieces + piece][...] = value[piece * rows : (piece + 1) * rows]


def pair_terms(jobs, width, vectors, before=(), weight=2048, pieces=1):
    blocks = []

    def place(block):
        for index, other in enumerate(blocks):
            if other is block:
                return index
        blocks.append(block)
        return len(blocks) - 1

    placed = [(place(row), [place(column) for column in columns]) for row, columns in jobs]
    points = blocks[0].shape[1]
    operands = blocks + list(before)
    shape = jax.ShapeDtypeStruct((width // pieces, points), jnp.float32)
    out_shape = [shape] * (len(jobs) * pieces)
    return list(
        pl.pallas_call(
            functools.partial(kernel, width, vectors, placed, len(blocks), pieces),
            out_shape=out_shape,
            in_specs=[pl.BlockSpec(memory_space=pltpu.VMEM)] * len(operands),
            out_specs=[pl.BlockSpec(memory_space=pltpu.VMEM)] * len(out_shape),
            compiler_params=pltpu.CompilerParams(vmem_limit_bytes=VMEM_LIMIT),
            cost_estimate=pl.CostEstimate(
                flops=2 * points * points * weight * sum(len(columns) for _, columns in jobs),
                bytes_accessed=4 * points * 96 * len(operands),
                transcendentals=points * points,
            ),
        )(*operands)
    )


def packed(features, solves, probes):
    width, points = features.shape
    vectors = solves.shape[0]

    def body(features_ref, solves_ref, probes_ref, out_ref, vectors_ref):
        out_ref[:width] = features_ref[...]
        for first, ref in ((0, solves_ref), (vectors, probes_ref)):
            out_ref[width + first : width + first + vectors] = ref[...]
            vectors_ref[first : first + vectors] = ref[...]

    return pl.pallas_call(
        body,
        out_shape=[
            jax.ShapeDtypeStruct((rows, points), jnp.float32)
            for rows in (width + 2 * vectors, 2 * vectors)
        ],
        compiler_params=pltpu.CompilerParams(vmem_limit_bytes=60 << 20),
    )(features, solves, probes)


def local(features, solves, probes):
    width = features.shape[0]
    vectors = solves.shape[0]
    count = lax.axis_size("blk")
    terms = functools.partial(pair_terms, width=width, vectors=vectors)
    swap = lambda value, bit: swapped(value, "blk", bit)
    tied = lax.optimization_barrier

    bits = [1 << place for place in range(count.bit_length() - 1)]
    top, beside = bits[-1], [bit for bit in bits[:-1] if bit not in (1, 4)]
    far_features = swap(features, top)
    mine, my_vectors = packed(features, solves, probes)
    far_vectors = swap(my_vectors, top)
    sibling = swap(mine, 1)
    near = swap(mine, 4)
    direct = [swap(mine, bit) for bit in beside]

    far_features, own = tied((far_features, mine))
    (here,) = terms([(own, [own])], weight=2048)
    near, here = tied((near, here))
    (there,) = terms([(near, [mine, sibling] + direct)], weight=1024)
    far_vectors, there = tied((far_vectors, there))
    far = [far_features, far_vectors]
    last = []
    for bit in beside:
        for pair in [far] + last:
            last = last + [[swap(piece, bit) for piece in pair]]
    first = [jnp.concatenate(far, 0)] + direct
    siblings = jnp.split(swap(jnp.concatenate(first, 0), 1), len(first), 0)
    there, here = terms([(near, first[:1]), (mine, first[:1])], before=[there, here], weight=30000)
    (there,) = terms([(near, siblings)], before=[there], weight=8)
    *pieces, there = tied((*[piece for pair in last for piece in pair], there))
    last = [jnp.concatenate(pieces[at : at + 2], 0) for at in range(0, len(pieces), 2)]
    last_siblings = [swap(block, 1) for block in last]
    there, here = terms([(near, last), (mine, last)], before=[there, here], weight=64)
    (toward_near,) = terms([(near, last_siblings)], before=[there], weight=64)
    from_near = swap(toward_near, 4)
    rest = [sibling] + direct + siblings + last_siblings
    (here,) = terms([(mine, rest)], before=[here], weight=2048)
    return here + from_near


def solution(mesh):
    in_specs = (P(None, ("groups", "blk")), P(None, ("groups", "blk")), P(None, ("groups", "blk")))
    out_specs = P(None, ("groups", "blk"))
    return jax.shard_map(local, mesh=mesh, in_specs=in_specs, out_specs=out_specs, check_vma=False)
```

```python
import functools

import jax
import jax.numpy as jnp
from jax import lax
from jax.experimental import pallas as pl
from jax.experimental.pallas import tpu as pltpu
from jax.sharding import PartitionSpec as P

LOG2E = 1.4426950408889634
NORM_ROWS = 16
ONES_ROWS = 16
STACK = 4
VMEM_LIMIT = 24 << 20


def swapped(value, axis, bit):
    count = lax.axis_size(axis)
    return lax.ppermute(value, axis, [(source, source ^ bit) for source in range(count)])


def split2(value):
    high = value.astype(jnp.bfloat16)
    low = (value - high.astype(jnp.float32)).astype(jnp.bfloat16)
    return high, low


def term_weights(vectors):
    position = lax.broadcasted_iota(jnp.int32, (2 * vectors, 1), 0)
    first = (position == 0) | (position == vectors)
    return jnp.where(first, 0.5, -0.5 / (vectors - 1)).astype(jnp.float32)


def norm_rows(norms, first):
    high = norms.astype(jnp.bfloat16).astype(jnp.float32)
    rest = norms - high
    mid = rest.astype(jnp.bfloat16).astype(jnp.float32)
    row = lax.broadcasted_iota(jnp.int32, (NORM_ROWS, norms.shape[1]), 0)
    at, ones = (0, 3) if first else (3, 0)
    rows = jnp.where((row >= ones) & (row < ones + 3), 1.0, 0.0)
    for place, part in enumerate((high, mid, rest - mid)):
        rows = jnp.where(row == at + place, part, rows)
    return rows.astype(jnp.bfloat16)


def prepared_mine(block, width, vectors):
    feat = block[:width]
    scale = LOG2E / (2.0 * width)
    norms = jnp.sum(feat * feat, axis=0, keepdims=True) * -scale
    high, low = split2(feat * (2.0 * scale))
    dist = jnp.concatenate([high, low, high, norm_rows(norms, True)], 0)
    high, low = split2(block[width:] * term_weights(vectors))
    return dist, jnp.concatenate([high, low, high], 0)


def prepared_theirs(block, width, vectors):
    feat = block[:width]
    scale = LOG2E / (2.0 * width)
    norms = jnp.sum(feat * feat, axis=0, keepdims=True) * -scale
    high, low = split2(feat)
    dist = jnp.concatenate([high, high, low, norm_rows(norms, False)], 0)
    vecs = jnp.concatenate([block[width + vectors :], block[width : width + vectors]], 0)
    vec_high, vec_low = split2(vecs)
    pair = jnp.concatenate([vec_high, vec_high, vec_low], 0)
    ones = jnp.ones((ONES_ROWS, block.shape[1]), jnp.bfloat16)
    return dist, pair, jnp.concatenate([high, ones, low], 0)


def product(left, right):
    return jnp.dot(left, right, preferred_element_type=jnp.float32)


def pair_product(left, right):
    first = (((0,), (0,)), ((), ()))
    return lax.dot_general(left, right, first, preferred_element_type=jnp.float32)


def pulled_terms(mine, theirs, width):
    dist_mine, pair_mine = mine
    dist_theirs, pair_theirs, pull = theirs
    power = pair_product(dist_theirs, dist_mine)
    coupling = jnp.exp2(power) * pair_product(pair_theirs, pair_mine)
    high, low = split2(coupling)
    from_high = product(pull, high)
    from_low = product(pull[: width + ONES_ROWS], low)
    pulled = from_high[:width] + from_high[width + ONES_ROWS :] + from_low[:width]
    return pulled, from_high[width : width + 1] + from_low[width : width + 1]


def stacked(theirs):
    dist, pair, pull = zip(*theirs)
    return tuple(jnp.concatenate(part, 1) for part in (dist, pair, pull))


def kernel(width, vectors, jobs, count, pieces, *refs):
    blocks, refs = refs[:count], refs[count:]
    results = len(jobs) * pieces
    before, out = refs[:-results], refs[-results:]
    used = sorted({theirs for _, columns in jobs for theirs in columns})
    theirs = {place: prepared_theirs(blocks[place][...], width, vectors) for place in used}
    for place, (row, columns) in enumerate(jobs):
        mine = prepared_mine(blocks[row][...], width, vectors)
        parts = [
            pulled_terms(mine, stacked([theirs[column] for column in columns[at : at + STACK]]), width)
            for at in range(0, len(columns), STACK)
        ]
        pulled, sums = (sum(part) for part in zip(*parts))
        value = (pulled - blocks[row][:width] * sums) / width
        value = value + before[place][...] if place < len(before) else value
        rows = width // pieces
        for piece in range(pieces):
            out[place * pieces + piece][...] = value[piece * rows : (piece + 1) * rows]


def pair_terms(jobs, width, vectors, before=(), weight=2048, pieces=1):
    blocks = []

    def place(block):
        for index, other in enumerate(blocks):
            if other is block:
                return index
        blocks.append(block)
        return len(blocks) - 1

    placed = [(place(row), [place(column) for column in columns]) for row, columns in jobs]
    points = blocks[0].shape[1]
    operands = blocks + list(before)
    shape = jax.ShapeDtypeStruct((width // pieces, points), jnp.float32)
    out_shape = [shape] * (len(jobs) * pieces)
    return list(
        pl.pallas_call(
            functools.partial(kernel, width, vectors, placed, len(blocks), pieces),
            out_shape=out_shape,
            in_specs=[pl.BlockSpec(memory_space=pltpu.VMEM)] * len(operands),
            out_specs=[pl.BlockSpec(memory_space=pltpu.VMEM)] * len(out_shape),
            compiler_params=pltpu.CompilerParams(vmem_limit_bytes=VMEM_LIMIT),
            cost_estimate=pl.CostEstimate(
                flops=2 * points * points * weight * sum(len(columns) for _, columns in jobs),
                bytes_accessed=4 * points * 96 * len(operands),
                transcendentals=points * points,
            ),
        )(*operands)
    )


def packed(features, solves, probes):
    width, points = features.shape
    vectors = solves.shape[0]

    def body(features_ref, solves_ref, probes_ref, out_ref, vectors_ref):
        out_ref[:width] = features_ref[...]
        for first, ref in ((0, solves_ref), (vectors, probes_ref)):
            out_ref[width + first : width + first + vectors] = ref[...]
            vectors_ref[first : first + vectors] = ref[...]

    return pl.pallas_call(
        body,
        out_shape=[
            jax.ShapeDtypeStruct((rows, points), jnp.float32)
            for rows in (width + 2 * vectors, 2 * vectors)
        ],
        compiler_params=pltpu.CompilerParams(vmem_limit_bytes=60 << 20),
    )(features, solves, probes)


def local(features, solves, probes):
    width = features.shape[0]
    vectors = solves.shape[0]
    count = lax.axis_size("blk")
    terms = functools.partial(pair_terms, width=width, vectors=vectors)
    swap = lambda value, bit: swapped(value, "blk", bit)
    tied = lax.optimization_barrier

    bits = [1 << place for place in range(count.bit_length() - 1)]
    top, beside = bits[-1], [bit for bit in bits[:-1] if bit not in (1, 4)]
    far_features = swap(features, top)
    mine, my_vectors = packed(features, solves, probes)
    far_vectors = swap(my_vectors, top)
    sibling = swap(mine, 1)
    near = swap(mine, 4)
    direct = [swap(mine, bit) for bit in beside]

    (here,) = terms([(mine, [mine])], weight=1024)
    far_features, far_vectors, here = tied((far_features, far_vectors, here))
    far = [far_features, far_vectors]
    last = []
    for bit in beside:
        for pair in [far] + last:
            last = last + [[swap(piece, bit) for piece in pair]]
    first = [jnp.concatenate(far, 0)] + direct
    siblings = [swap(block, 1) for block in first]
    (there,) = terms([(near, [mine, sibling] + first)], weight=1024)
    (there,) = terms([(near, siblings)], before=[there], weight=512)
    *pieces, there = tied((*[piece for pair in last for piece in pair], there))
    last = [jnp.concatenate(pieces[at : at + 2], 0) for at in range(0, len(pieces), 2)]
    last_siblings = [swap(block, 1) for block in last]
    there, here = terms([(near, last), (mine, last)], before=[there, here], weight=64)
    toward_near = terms([(near, last_siblings)], before=[there], weight=64, pieces=2)
    from_near = jnp.concatenate([swap(piece, 4) for piece in toward_near], 0)
    rest = [sibling] + first + siblings + last_siblings
    (here,) = terms([(mine, rest)], before=[here], weight=2048)
    return here + from_near


def solution(mesh):
    in_specs = (P(None, ("groups", "blk")), P(None, ("groups", "blk")), P(None, ("groups", "blk")))
    out_specs = P(None, ("groups", "blk"))
    return jax.shard_map(local, mesh=mesh, in_specs=in_specs, out_specs=out_specs, check_vma=False)
```

```python
import functools

import jax
import jax.numpy as jnp
from jax import lax
from jax.experimental import pallas as pl
from jax.experimental.pallas import tpu as pltpu
from jax.sharding import PartitionSpec as P

LOG2E = 1.4426950408889634
NORM_ROWS = 16
ONES_ROWS = 16
STACK = 4
VMEM_LIMIT = 24 << 20


def swapped(value, axis, bit):
    count = lax.axis_size(axis)
    return lax.ppermute(value, axis, [(source, source ^ bit) for source in range(count)])


def split2(value):
    high = value.astype(jnp.bfloat16)
    low = (value - high.astype(jnp.float32)).astype(jnp.bfloat16)
    return high, low


def term_weights(vectors):
    position = lax.broadcasted_iota(jnp.int32, (2 * vectors, 1), 0)
    first = (position == 0) | (position == vectors)
    return jnp.where(first, 0.5, -0.5 / (vectors - 1)).astype(jnp.float32)


def norm_rows(norms, first):
    high = norms.astype(jnp.bfloat16).astype(jnp.float32)
    rest = norms - high
    mid = rest.astype(jnp.bfloat16).astype(jnp.float32)
    row = lax.broadcasted_iota(jnp.int32, (NORM_ROWS, norms.shape[1]), 0)
    at, ones = (0, 3) if first else (3, 0)
    rows = jnp.where((row >= ones) & (row < ones + 3), 1.0, 0.0)
    for place, part in enumerate((high, mid, rest - mid)):
        rows = jnp.where(row == at + place, part, rows)
    return rows.astype(jnp.bfloat16)


def prepared_mine(block, width, vectors):
    feat = block[:width]
    scale = LOG2E / (2.0 * width)
    norms = jnp.sum(feat * feat, axis=0, keepdims=True) * -scale
    high, low = split2(feat * (2.0 * scale))
    dist = jnp.concatenate([high, low, high, norm_rows(norms, True)], 0)
    high, low = split2(block[width:] * term_weights(vectors))
    return dist, jnp.concatenate([high, low, high], 0)


def prepared_theirs(block, width, vectors):
    feat = block[:width]
    scale = LOG2E / (2.0 * width)
    norms = jnp.sum(feat * feat, axis=0, keepdims=True) * -scale
    high, low = split2(feat)
    dist = jnp.concatenate([high, high, low, norm_rows(norms, False)], 0)
    vecs = jnp.concatenate([block[width + vectors :], block[width : width + vectors]], 0)
    vec_high, vec_low = split2(vecs)
    pair = jnp.concatenate([vec_high, vec_high, vec_low], 0)
    ones = jnp.ones((ONES_ROWS, block.shape[1]), jnp.bfloat16)
    return dist.T, pair.T, jnp.concatenate([high, ones, low], 0)


def product(left, right):
    return jnp.dot(left, right, preferred_element_type=jnp.float32)


def pulled_terms(mine, theirs, width):
    dist_mine, pair_mine = mine
    dist_theirs, pair_theirs, pull = theirs
    coupling = jnp.exp2(product(dist_theirs, dist_mine)) * product(pair_theirs, pair_mine)
    high, low = split2(coupling)
    from_high = product(pull, high)
    from_low = product(pull[: width + ONES_ROWS], low)
    pulled = from_high[:width] + from_high[width + ONES_ROWS :] + from_low[:width]
    return pulled, from_high[width : width + 1] + from_low[width : width + 1]


def stacked(theirs):
    dist, pair, pull = zip(*theirs)
    return jnp.concatenate(dist, 0), jnp.concatenate(pair, 0), jnp.concatenate(pull, 1)


def kernel(width, vectors, jobs, count, span, *refs):
    blocks, refs = refs[:count], refs[count:]
    before, out = refs[: -len(jobs)], refs[-len(jobs) :]
    used = sorted({theirs for _, columns in jobs for theirs in columns})
    theirs = {place: prepared_theirs(blocks[place][...], width, vectors) for place in used}
    for place, (row, columns) in enumerate(jobs):
        block = blocks[row][:, span]
        mine = prepared_mine(block, width, vectors)
        parts = [
            pulled_terms(mine, stacked([theirs[column] for column in columns[at : at + STACK]]), width)
            for at in range(0, len(columns), STACK)
        ]
        pulled, sums = (sum(part) for part in zip(*parts))
        value = (pulled - block[:width] * sums) / width
        out[place][...] = value + before[place][:, span] if place < len(before) else value


def pair_terms(jobs, width, vectors, before=(), weight=2048, span=None):
    blocks = []

    def place(block):
        for index, other in enumerate(blocks):
            if other is block:
                return index
        blocks.append(block)
        return len(blocks) - 1

    placed = [(place(row), [place(column) for column in columns]) for row, columns in jobs]
    points = blocks[0].shape[1]
    operands = blocks + list(before)
    first, count = span or (0, points)
    out_shape = [jax.ShapeDtypeStruct((width, count), jnp.float32)] * len(jobs)
    return list(
        pl.pallas_call(
            functools.partial(kernel, width, vectors, placed, len(blocks), pl.ds(first, count)),
            out_shape=out_shape,
            in_specs=[pl.BlockSpec(memory_space=pltpu.VMEM)] * len(operands),
            out_specs=[pl.BlockSpec(memory_space=pltpu.VMEM)] * len(out_shape),
            compiler_params=pltpu.CompilerParams(vmem_limit_bytes=VMEM_LIMIT),
            cost_estimate=pl.CostEstimate(
                flops=2 * points * points * weight * sum(len(columns) for _, columns in jobs),
                bytes_accessed=4 * points * 96 * len(operands),
                transcendentals=points * points,
            ),
        )(*operands)
    )


def packed(features, solves, probes):
    width, points = features.shape
    vectors = solves.shape[0]

    def body(features_ref, solves_ref, probes_ref, out_ref, vectors_ref):
        out_ref[:width] = features_ref[...]
        for first, ref in ((0, solves_ref), (vectors, probes_ref)):
            out_ref[width + first : width + first + vectors] = ref[...]
            vectors_ref[first : first + vectors] = ref[...]

    return pl.pallas_call(
        body,
        out_shape=[
            jax.ShapeDtypeStruct((rows, points), jnp.float32)
            for rows in (width + 2 * vectors, 2 * vectors)
        ],
        compiler_params=pltpu.CompilerParams(vmem_limit_bytes=60 << 20),
    )(features, solves, probes)


def local(features, solves, probes):
    width = features.shape[0]
    vectors = solves.shape[0]
    count = lax.axis_size("blk")
    terms = functools.partial(pair_terms, width=width, vectors=vectors)
    swap = lambda value, bit: swapped(value, "blk", bit)
    tied = lax.optimization_barrier

    bits = [1 << place for place in range(count.bit_length() - 1)]
    top, beside = bits[-1], [bit for bit in bits[:-1] if bit not in (1, 4)]
    far_features = swap(features, top)
    mine, my_vectors = packed(features, solves, probes)
    far_vectors = swap(my_vectors, top)
    sibling = swap(mine, 1)
    near = swap(mine, 4)
    direct = [swap(mine, bit) for bit in beside]

    (here,) = terms([(mine, [mine])], weight=1024)
    far_features, far_vectors, here = tied((far_features, far_vectors, here))
    far = [far_features, far_vectors]
    last = []
    for bit in beside:
        for pair in [far] + last:
            last = last + [[swap(piece, bit) for piece in pair]]
    first = [jnp.concatenate(far, 0)] + direct
    siblings = [swap(block, 1) for block in first]
    (there,) = terms([(near, [mine, sibling] + first)], weight=1024)
    (there,) = terms([(near, siblings)], before=[there], weight=512)
    *pieces, there = tied((*[piece for pair in last for piece in pair], there))
    last = [jnp.concatenate(pieces[at : at + 2], 0) for at in range(0, len(pieces), 2)]
    last_siblings = [swap(block, 1) for block in last]
    there, here = terms([(near, last), (mine, last)], before=[there, here], weight=64)
    half = mine.shape[1] // 2
    (first_half,) = terms([(near, last_siblings)], before=[there], weight=64, span=(0, half))
    last_siblings[0], first_half = tied((last_siblings[0], first_half))
    (second_half,) = terms([(near, last_siblings)], before=[there], weight=8, span=(half, half))
    from_near = [swap(piece, 4) for piece in (first_half, second_half)]
    (here,) = terms([(mine, [sibling] + first)], before=[here], weight=8)
    from_near[0], here = tied((from_near[0], here))
    (here,) = terms([(mine, siblings + last_siblings)], before=[here], weight=8)
    return here + jnp.concatenate(from_near, 1)


def solution(mesh):
    in_specs = (P(None, ("groups", "blk")), P(None, ("groups", "blk")), P(None, ("groups", "blk")))
    out_specs = P(None, ("groups", "blk"))
    return jax.shard_map(local, mesh=mesh, in_specs=in_specs, out_specs=out_specs, check_vma=False)
```

```python
import functools

import jax
import jax.numpy as jnp
from jax import lax
from jax.experimental import pallas as pl
from jax.experimental.pallas import tpu as pltpu
from jax.sharding import PartitionSpec as P

LOG2E = 1.4426950408889634
NORM_ROWS = 16
ONES_ROWS = 16
STACK = 4
VMEM_LIMIT = 16 << 20


def swapped(value, axis, bit):
    count = lax.axis_size(axis)
    return lax.ppermute(value, axis, [(source, source ^ bit) for source in range(count)])


def split2(value):
    high = value.astype(jnp.bfloat16)
    low = (value - high.astype(jnp.float32)).astype(jnp.bfloat16)
    return high, low


def term_weights(vectors):
    position = lax.broadcasted_iota(jnp.int32, (2 * vectors, 1), 0)
    first = (position == 0) | (position == vectors)
    return jnp.where(first, 0.5, -0.5 / (vectors - 1)).astype(jnp.float32)


def norm_rows(norms, first):
    high = norms.astype(jnp.bfloat16).astype(jnp.float32)
    rest = norms - high
    mid = rest.astype(jnp.bfloat16).astype(jnp.float32)
    row = lax.broadcasted_iota(jnp.int32, (NORM_ROWS, norms.shape[1]), 0)
    at, ones = (0, 3) if first else (3, 0)
    rows = jnp.where((row >= ones) & (row < ones + 3), 1.0, 0.0)
    for place, part in enumerate((high, mid, rest - mid)):
        rows = jnp.where(row == at + place, part, rows)
    return rows.astype(jnp.bfloat16)


def prepared_mine(block, width, vectors):
    feat = block[:width]
    scale = LOG2E / (2.0 * width)
    norms = jnp.sum(feat * feat, axis=0, keepdims=True) * -scale
    high, low = split2(feat * (2.0 * scale))
    dist = jnp.concatenate([high, low, high, norm_rows(norms, True)], 0)
    high, low = split2(block[width:] * term_weights(vectors))
    return dist, jnp.concatenate([high, low, high], 0)


def prepared_theirs(block, width, vectors):
    feat = block[:width]
    scale = LOG2E / (2.0 * width)
    norms = jnp.sum(feat * feat, axis=0, keepdims=True) * -scale
    high, low = split2(feat)
    dist = jnp.concatenate([high, high, low, norm_rows(norms, False)], 0)
    vecs = jnp.concatenate([block[width + vectors :], block[width : width + vectors]], 0)
    vec_high, vec_low = split2(vecs)
    pair = jnp.concatenate([vec_high, vec_high, vec_low], 0)
    ones = jnp.ones((ONES_ROWS, block.shape[1]), jnp.bfloat16)
    return dist.T, pair.T, jnp.concatenate([high, ones, low], 0)


def product(left, right):
    return jnp.dot(left, right, preferred_element_type=jnp.float32)


def pulled_terms(mine, theirs, width):
    dist_mine, pair_mine = mine
    dist_theirs, pair_theirs, pull = theirs
    coupling = jnp.exp2(product(dist_theirs, dist_mine)) * product(pair_theirs, pair_mine)
    high, low = split2(coupling)
    from_high = product(pull, high)
    from_low = product(pull[: width + ONES_ROWS], low)
    pulled = from_high[:width] + from_high[width + ONES_ROWS :] + from_low[:width]
    return pulled, from_high[width : width + 1] + from_low[width : width + 1]


def stacked(theirs):
    dist, pair, pull = zip(*theirs)
    return jnp.concatenate(dist, 0), jnp.concatenate(pair, 0), jnp.concatenate(pull, 1)


def kernel(width, vectors, jobs, count, span, *refs):
    blocks, refs = refs[:count], refs[count:]
    before, out = refs[: -len(jobs)], refs[-len(jobs) :]
    used = sorted({theirs for _, columns in jobs for theirs in columns})
    theirs = {place: prepared_theirs(blocks[place][...], width, vectors) for place in used}
    for place, (row, columns) in enumerate(jobs):
        block = blocks[row][:, span]
        mine = prepared_mine(block, width, vectors)
        parts = [
            pulled_terms(mine, stacked([theirs[column] for column in columns[at : at + STACK]]), width)
            for at in range(0, len(columns), STACK)
        ]
        pulled, sums = (sum(part) for part in zip(*parts))
        value = (pulled - block[:width] * sums) / width
        out[place][...] = value + before[place][:, span] if place < len(before) else value


def pair_terms(jobs, width, vectors, before=(), weight=2048, span=None):
    blocks = []

    def place(block):
        for index, other in enumerate(blocks):
            if other is block:
                return index
        blocks.append(block)
        return len(blocks) - 1

    placed = [(place(row), [place(column) for column in columns]) for row, columns in jobs]
    points = blocks[0].shape[1]
    operands = blocks + list(before)
    first, count = span or (0, points)
    out_shape = [jax.ShapeDtypeStruct((width, count), jnp.float32)] * len(jobs)
    return list(
        pl.pallas_call(
            functools.partial(kernel, width, vectors, placed, len(blocks), pl.ds(first, count)),
            out_shape=out_shape,
            in_specs=[pl.BlockSpec(memory_space=pltpu.VMEM)] * len(operands),
            out_specs=[pl.BlockSpec(memory_space=pltpu.VMEM)] * len(out_shape),
            compiler_params=pltpu.CompilerParams(vmem_limit_bytes=VMEM_LIMIT),
            cost_estimate=pl.CostEstimate(
                flops=2 * points * points * weight * sum(len(columns) for _, columns in jobs),
                bytes_accessed=4 * points * 96 * len(operands),
                transcendentals=points * points,
            ),
        )(*operands)
    )


def packed(features, solves, probes):
    width, points = features.shape
    vectors = solves.shape[0]

    def body(features_ref, solves_ref, probes_ref, out_ref, vectors_ref):
        out_ref[:width] = features_ref[...]
        for first, ref in ((0, solves_ref), (vectors, probes_ref)):
            out_ref[width + first : width + first + vectors] = ref[...]
            vectors_ref[first : first + vectors] = ref[...]

    return pl.pallas_call(
        body,
        out_shape=[
            jax.ShapeDtypeStruct((rows, points), jnp.float32)
            for rows in (width + 2 * vectors, 2 * vectors)
        ],
        compiler_params=pltpu.CompilerParams(vmem_limit_bytes=60 << 20),
    )(features, solves, probes)


def local(features, solves, probes):
    width = features.shape[0]
    vectors = solves.shape[0]
    count = lax.axis_size("blk")
    terms = functools.partial(pair_terms, width=width, vectors=vectors)
    swap = lambda value, bit: swapped(value, "blk", bit)
    tied = lax.optimization_barrier

    bits = [1 << place for place in range(count.bit_length() - 1)]
    top, beside = bits[-1], [bit for bit in bits[:-1] if bit not in (1, 4)]
    far_features = swap(features, top)
    mine, my_vectors = packed(features, solves, probes)
    far_vectors = swap(my_vectors, top)
    sibling = swap(mine, 1)
    near = swap(mine, 4)
    direct = [swap(mine, bit) for bit in beside]

    (here,) = terms([(mine, [mine])], weight=1024)
    far_features, far_vectors, here = tied((far_features, far_vectors, here))
    far = [far_features, far_vectors]
    last = []
    for bit in beside:
        for pair in [far] + last:
            last = last + [[swap(piece, bit) for piece in pair]]
    first = [jnp.concatenate(far, 0)] + direct
    siblings = [swap(block, 1) for block in first]
    (there,) = terms([(near, [mine, sibling] + first)], weight=1024)
    (there,) = terms([(near, siblings)], before=[there], weight=512)
    *pieces, there = tied((*[piece for pair in last for piece in pair], there))
    last = [jnp.concatenate(pieces[at : at + 2], 0) for at in range(0, len(pieces), 2)]
    last_siblings = [swap(block, 1) for block in last]
    (there,) = terms([(near, last)], before=[there], weight=64)
    half = mine.shape[1] // 2
    (first_half,) = terms([(near, last_siblings)], before=[there], weight=64, span=(0, half))
    last_siblings[0], first_half = tied((last_siblings[0], first_half))
    (second_half,) = terms([(near, last_siblings)], before=[there], weight=8, span=(half, half))
    from_near = [swap(piece, 4) for piece in (first_half, second_half)]
    (here,) = terms([(mine, first + siblings[:1])], before=[here], weight=8)
    from_near[0], here = tied((from_near[0], here))
    (here,) = terms([(mine, [sibling] + siblings[1:] + last + last_siblings)], before=[here], weight=8)
    return here + jnp.concatenate(from_near, 1)


def solution(mesh):
    in_specs = (P(None, ("groups", "blk")), P(None, ("groups", "blk")), P(None, ("groups", "blk")))
    out_specs = P(None, ("groups", "blk"))
    return jax.shard_map(local, mesh=mesh, in_specs=in_specs, out_specs=out_specs, check_vma=False)
```

```python
import functools

import jax
import jax.numpy as jnp
from jax import lax
from jax.experimental import pallas as pl
from jax.experimental.pallas import tpu as pltpu
from jax.sharding import PartitionSpec as P

LOG2E = 1.4426950408889634
NORM_ROWS = 16
ONES_ROWS = 16
STACK = 4
VMEM_LIMIT = 24 << 20


def swapped(value, axis, bit):
    count = lax.axis_size(axis)
    return lax.ppermute(value, axis, [(source, source ^ bit) for source in range(count)])


def split2(value):
    high = value.astype(jnp.bfloat16)
    low = (value - high.astype(jnp.float32)).astype(jnp.bfloat16)
    return high, low


def term_weights(vectors):
    position = lax.broadcasted_iota(jnp.int32, (2 * vectors, 1), 0)
    first = (position == 0) | (position == vectors)
    return jnp.where(first, 0.5, -0.5 / (vectors - 1)).astype(jnp.float32)


def norm_rows(norms, first):
    high = norms.astype(jnp.bfloat16).astype(jnp.float32)
    rest = norms - high
    mid = rest.astype(jnp.bfloat16).astype(jnp.float32)
    row = lax.broadcasted_iota(jnp.int32, (NORM_ROWS, norms.shape[1]), 0)
    at, ones = (0, 3) if first else (3, 0)
    rows = jnp.where((row >= ones) & (row < ones + 3), 1.0, 0.0)
    for place, part in enumerate((high, mid, rest - mid)):
        rows = jnp.where(row == at + place, part, rows)
    return rows.astype(jnp.bfloat16)


def prepared_mine(block, width, vectors):
    feat = block[:width]
    scale = LOG2E / (2.0 * width)
    norms = jnp.sum(feat * feat, axis=0, keepdims=True) * -scale
    high, low = split2(feat * (2.0 * scale))
    dist = jnp.concatenate([high, low, high, norm_rows(norms, True)], 0)
    high, low = split2(block[width:] * term_weights(vectors))
    return dist, jnp.concatenate([high, low, high], 0)


def prepared_theirs(block, width, vectors):
    feat = block[:width]
    scale = LOG2E / (2.0 * width)
    norms = jnp.sum(feat * feat, axis=0, keepdims=True) * -scale
    high, low = split2(feat)
    dist = jnp.concatenate([high, high, low, norm_rows(norms, False)], 0)
    vecs = jnp.concatenate([block[width + vectors :], block[width : width + vectors]], 0)
    vec_high, vec_low = split2(vecs)
    pair = jnp.concatenate([vec_high, vec_high, vec_low], 0)
    ones = jnp.ones((ONES_ROWS, block.shape[1]), jnp.bfloat16)
    return dist.T, pair.T, jnp.concatenate([high, ones, low], 0)


def product(left, right):
    return jnp.dot(left, right, preferred_element_type=jnp.float32)


def pulled_terms(mine, theirs, width):
    dist_mine, pair_mine = mine
    dist_theirs, pair_theirs, pull = theirs
    coupling = jnp.exp2(product(dist_theirs, dist_mine)) * product(pair_theirs, pair_mine)
    high, low = split2(coupling)
    from_high = product(pull, high)
    from_low = product(pull[: width + ONES_ROWS], low)
    pulled = from_high[:width] + from_high[width + ONES_ROWS :] + from_low[:width]
    return pulled, from_high[width : width + 1] + from_low[width : width + 1]


def stacked(theirs):
    dist, pair, pull = zip(*theirs)
    return jnp.concatenate(dist, 0), jnp.concatenate(pair, 0), jnp.concatenate(pull, 1)


def kernel(width, vectors, jobs, count, pieces, *refs):
    blocks, refs = refs[:count], refs[count:]
    results = len(jobs) * pieces
    before, out = refs[:-results], refs[-results:]
    used = sorted({theirs for _, columns in jobs for theirs in columns})
    theirs = {place: prepared_theirs(blocks[place][...], width, vectors) for place in used}
    for place, (row, columns) in enumerate(jobs):
        mine = prepared_mine(blocks[row][...], width, vectors)
        parts = [
            pulled_terms(mine, stacked([theirs[column] for column in columns[at : at + STACK]]), width)
            for at in range(0, len(columns), STACK)
        ]
        pulled, sums = (sum(part) for part in zip(*parts))
        value = (pulled - blocks[row][:width] * sums) / width
        value = value + before[place][...] if place < len(before) else value
        rows = width // pieces
        for piece in range(pieces):
            out[place * pieces + piece][...] = value[piece * rows : (piece + 1) * rows]


def pair_terms(jobs, width, vectors, before=(), weight=2048, pieces=1):
    blocks = []

    def place(block):
        for index, other in enumerate(blocks):
            if other is block:
                return index
        blocks.append(block)
        return len(blocks) - 1

    placed = [(place(row), [place(column) for column in columns]) for row, columns in jobs]
    points = blocks[0].shape[1]
    operands = blocks + list(before)
    shape = jax.ShapeDtypeStruct((width // pieces, points), jnp.float32)
    out_shape = [shape] * (len(jobs) * pieces)
    return list(
        pl.pallas_call(
            functools.partial(kernel, width, vectors, placed, len(blocks), pieces),
            out_shape=out_shape,
            in_specs=[pl.BlockSpec(memory_space=pltpu.VMEM)] * len(operands),
            out_specs=[pl.BlockSpec(memory_space=pltpu.VMEM)] * len(out_shape),
            compiler_params=pltpu.CompilerParams(vmem_limit_bytes=VMEM_LIMIT),
            cost_estimate=pl.CostEstimate(
                flops=2 * points * points * weight * sum(len(columns) for _, columns in jobs),
                bytes_accessed=4 * points * 96 * len(operands),
                transcendentals=points * points,
            ),
        )(*operands)
    )


def packed(features, solves, probes):
    width, points = features.shape
    vectors = solves.shape[0]

    def body(features_ref, solves_ref, probes_ref, out_ref, vectors_ref):
        out_ref[:width] = features_ref[...]
        for first, ref in ((0, solves_ref), (vectors, probes_ref)):
            out_ref[width + first : width + first + vectors] = ref[...]
            vectors_ref[first : first + vectors] = ref[...]

    return pl.pallas_call(
        body,
        out_shape=[
            jax.ShapeDtypeStruct((rows, points), jnp.float32)
            for rows in (width + 2 * vectors, 2 * vectors)
        ],
        compiler_params=pltpu.CompilerParams(vmem_limit_bytes=60 << 20),
    )(features, solves, probes)


def local(features, solves, probes):
    width = features.shape[0]
    vectors = solves.shape[0]
    count = lax.axis_size("blk")
    terms = functools.partial(pair_terms, width=width, vectors=vectors)
    swap = lambda value, bit: swapped(value, "blk", bit)
    tied = lax.optimization_barrier

    bits = [1 << place for place in range(count.bit_length() - 1)]
    top, beside = bits[-1], [bit for bit in bits[:-1] if bit not in (1, 4)]
    far_features = swap(features, top)
    mine, my_vectors = packed(features, solves, probes)
    far_vectors = swap(my_vectors, top)
    sibling = swap(mine, 1)
    near = swap(mine, 4)
    direct = [swap(mine, bit) for bit in beside]

    (here,) = terms([(mine, [mine])], weight=512)
    far_features, far_vectors, here = tied((far_features, far_vectors, here))
    far = [far_features, far_vectors]
    last = []
    for bit in beside:
        for pair in [far] + last:
            last = last + [[swap(piece, bit) for piece in pair]]
    far = jnp.concatenate(far, 0)
    (here,) = terms([(mine, [sibling, far])], before=[here], weight=256)
    near, *direct, here = tied((near, *direct, here))
    first = [far] + direct
    siblings = jnp.split(swap(jnp.concatenate(first, 0), 1), len(first), 0)
    (there,) = terms([(near, [mine, sibling] + first)], weight=2048)
    (there,) = terms([(near, siblings)], before=[there], weight=64)
    *pieces, there = tied((*[piece for pair in last for piece in pair], there))
    last = [jnp.concatenate(pieces[at : at + 2], 0) for at in range(0, len(pieces), 2)]
    last_siblings = [swap(block, 1) for block in last]
    there, here = terms([(near, last), (mine, last)], before=[there, here], weight=64)
    toward_near = terms([(near, last_siblings)], before=[there], weight=64, pieces=2)
    from_near = jnp.concatenate([swap(piece, 4) for piece in toward_near], 0)
    rest = direct + siblings + last_siblings
    (here,) = terms([(mine, rest)], before=[here], weight=2048)
    return here + from_near


def solution(mesh):
    in_specs = (P(None, ("groups", "blk")), P(None, ("groups", "blk")), P(None, ("groups", "blk")))
    out_specs = P(None, ("groups", "blk"))
    return jax.shard_map(local, mesh=mesh, in_specs=in_specs, out_specs=out_specs, check_vma=False)
```

```python
import functools

import jax
import jax.numpy as jnp
from jax import lax
from jax.experimental import pallas as pl
from jax.experimental.pallas import tpu as pltpu
from jax.sharding import PartitionSpec as P

LOG2E = 1.4426950408889634
NORM_ROWS = 16
ONES_ROWS = 16
STACK = 4
VMEM_LIMIT = 24 << 20


def swapped(value, axis, bit):
    count = lax.axis_size(axis)
    return lax.ppermute(value, axis, [(source, source ^ bit) for source in range(count)])


def split2(value):
    high = value.astype(jnp.bfloat16)
    low = (value - high.astype(jnp.float32)).astype(jnp.bfloat16)
    return high, low


def term_weights(vectors):
    position = lax.broadcasted_iota(jnp.int32, (2 * vectors, 1), 0)
    first = (position == 0) | (position == vectors)
    return jnp.where(first, 0.5, -0.5 / (vectors - 1)).astype(jnp.float32)


def norm_rows(norms, first):
    high = norms.astype(jnp.bfloat16).astype(jnp.float32)
    rest = norms - high
    mid = rest.astype(jnp.bfloat16).astype(jnp.float32)
    row = lax.broadcasted_iota(jnp.int32, (NORM_ROWS, norms.shape[1]), 0)
    at, ones = (0, 3) if first else (3, 0)
    rows = jnp.where((row >= ones) & (row < ones + 3), 1.0, 0.0)
    for place, part in enumerate((high, mid, rest - mid)):
        rows = jnp.where(row == at + place, part, rows)
    return rows.astype(jnp.bfloat16)


def prepared_mine(block, width, vectors):
    feat = block[:width]
    scale = LOG2E / (2.0 * width)
    norms = jnp.sum(feat * feat, axis=0, keepdims=True) * -scale
    high, low = split2(feat * (2.0 * scale))
    dist = jnp.concatenate([high, low, high, norm_rows(norms, True)], 0)
    high, low = split2(block[width:] * term_weights(vectors))
    return dist, jnp.concatenate([high, low, high], 0)


def prepared_theirs(block, width, vectors):
    feat = block[:width]
    scale = LOG2E / (2.0 * width)
    norms = jnp.sum(feat * feat, axis=0, keepdims=True) * -scale
    high, low = split2(feat)
    dist = jnp.concatenate([high, high, low, norm_rows(norms, False)], 0)
    vecs = jnp.concatenate([block[width + vectors :], block[width : width + vectors]], 0)
    vec_high, vec_low = split2(vecs)
    pair = jnp.concatenate([vec_high, vec_high, vec_low], 0)
    ones = jnp.ones((ONES_ROWS, block.shape[1]), jnp.bfloat16)
    return dist.T, pair.T, jnp.concatenate([high, ones, low], 0)


def product(left, right):
    return jnp.dot(left, right, preferred_element_type=jnp.float32)


def pulled_terms(mine, theirs, width):
    dist_mine, pair_mine = mine
    dist_theirs, pair_theirs, pull = theirs
    coupling = jnp.exp2(product(dist_theirs, dist_mine)) * product(pair_theirs, pair_mine)
    high, low = split2(coupling)
    from_high = product(pull, high)
    from_low = product(pull[: width + ONES_ROWS], low)
    pulled = from_high[:width] + from_high[width + ONES_ROWS :] + from_low[:width]
    return pulled, from_high[width : width + 1] + from_low[width : width + 1]


def stacked(theirs):
    dist, pair, pull = zip(*theirs)
    return jnp.concatenate(dist, 0), jnp.concatenate(pair, 0), jnp.concatenate(pull, 1)


def kernel(width, vectors, jobs, count, pieces, *refs):
    blocks, refs = refs[:count], refs[count:]
    results = len(jobs) * pieces
    before, out = refs[:-results], refs[-results:]
    used = sorted({theirs for _, columns in jobs for theirs in columns})
    theirs = {place: prepared_theirs(blocks[place][...], width, vectors) for place in used}
    for place, (row, columns) in enumerate(jobs):
        mine = prepared_mine(blocks[row][...], width, vectors)
        parts = [
            pulled_terms(mine, stacked([theirs[column] for column in columns[at : at + STACK]]), width)
            for at in range(0, len(columns), STACK)
        ]
        pulled, sums = (sum(part) for part in zip(*parts))
        value = (pulled - blocks[row][:width] * sums) / width
        value = value + before[place][...] if place < len(before) else value
        rows = width // pieces
        for piece in range(pieces):
            out[place * pieces + piece][...] = value[piece * rows : (piece + 1) * rows]


def pair_terms(jobs, width, vectors, before=(), weight=2048, pieces=1):
    blocks = []

    def place(block):
        for index, other in enumerate(blocks):
            if other is block:
                return index
        blocks.append(block)
        return len(blocks) - 1

    placed = [(place(row), [place(column) for column in columns]) for row, columns in jobs]
    points = blocks[0].shape[1]
    operands = blocks + list(before)
    shape = jax.ShapeDtypeStruct((width // pieces, points), jnp.float32)
    out_shape = [shape] * (len(jobs) * pieces)
    return list(
        pl.pallas_call(
            functools.partial(kernel, width, vectors, placed, len(blocks), pieces),
            out_shape=out_shape,
            in_specs=[pl.BlockSpec(memory_space=pltpu.VMEM)] * len(operands),
            out_specs=[pl.BlockSpec(memory_space=pltpu.VMEM)] * len(out_shape),
            compiler_params=pltpu.CompilerParams(vmem_limit_bytes=VMEM_LIMIT),
            cost_estimate=pl.CostEstimate(
                flops=2 * points * points * weight * sum(len(columns) for _, columns in jobs),
                bytes_accessed=4 * points * 96 * len(operands),
                transcendentals=points * points,
            ),
        )(*operands)
    )


def packed(features, solves, probes):
    width, points = features.shape
    vectors = solves.shape[0]

    def body(features_ref, solves_ref, probes_ref, out_ref, vectors_ref):
        out_ref[:width] = features_ref[...]
        for first, ref in ((0, solves_ref), (vectors, probes_ref)):
            out_ref[width + first : width + first + vectors] = ref[...]
            vectors_ref[first : first + vectors] = ref[...]

    return pl.pallas_call(
        body,
        out_shape=[
            jax.ShapeDtypeStruct((rows, points), jnp.float32)
            for rows in (width + 2 * vectors, 2 * vectors)
        ],
        compiler_params=pltpu.CompilerParams(vmem_limit_bytes=60 << 20),
    )(features, solves, probes)


def local(features, solves, probes):
    width = features.shape[0]
    vectors = solves.shape[0]
    count = lax.axis_size("blk")
    terms = functools.partial(pair_terms, width=width, vectors=vectors)
    swap = lambda value, bit: swapped(value, "blk", bit)
    tied = lax.optimization_barrier

    bits = [1 << place for place in range(count.bit_length() - 1)]
    top, beside = bits[-1], [bit for bit in bits[:-1] if bit not in (1, 4)]
    far_features = swap(features, top)
    mine, my_vectors = packed(features, solves, probes)
    far_vectors = swap(my_vectors, top)
    sibling = swap(mine, 1)
    near = swap(mine, 4)
    direct = [swap(mine, bit) for bit in beside]

    (here,) = terms([(mine, [mine])], weight=64)
    far_features, far_vectors, here = tied((far_features, far_vectors, here))
    far = [far_features, far_vectors]
    last = []
    for bit in beside:
        for pair in [far] + last:
            last = last + [[swap(piece, bit) for piece in pair]]
    far = jnp.concatenate(far, 0)
    (here,) = terms([(mine, [far])], before=[here], weight=2048)
    near, sibling, *direct, here = tied((near, sibling, *direct, here))
    first = [far] + direct
    siblings = jnp.split(swap(jnp.concatenate(first, 0), 1), len(first), 0)
    (there,) = terms([(near, [mine, sibling] + first)], weight=2048)
    (there,) = terms([(near, siblings)], before=[there], weight=64)
    *pieces, there = tied((*[piece for pair in last for piece in pair], there))
    last = [jnp.concatenate(pieces[at : at + 2], 0) for at in range(0, len(pieces), 2)]
    last_siblings = [swap(block, 1) for block in last]
    (there,) = terms([(near, last)], before=[there], weight=64)
    toward_near = terms([(near, last_siblings)], before=[there], weight=64, pieces=2)
    from_near = jnp.concatenate([swap(piece, 4) for piece in toward_near], 0)
    rest = [sibling] + direct + siblings + last + last_siblings
    (here,) = terms([(mine, rest)], before=[here], weight=2048)
    return here + from_near


def solution(mesh):
    in_specs = (P(None, ("groups", "blk")), P(None, ("groups", "blk")), P(None, ("groups", "blk")))
    out_specs = P(None, ("groups", "blk"))
    return jax.shard_map(local, mesh=mesh, in_specs=in_specs, out_specs=out_specs, check_vma=False)
```

```python
import functools

import jax
import jax.numpy as jnp
from jax import lax
from jax.experimental import pallas as pl
from jax.experimental.pallas import tpu as pltpu
from jax.sharding import PartitionSpec as P

LOG2E = 1.4426950408889634
NORM_ROWS = 16
ONES_ROWS = 16
STACK = 7
VMEM_LIMIT = 24 << 20


def swapped(value, axis, bit):
    count = lax.axis_size(axis)
    return lax.ppermute(value, axis, [(source, source ^ bit) for source in range(count)])


def split2(value):
    high = value.astype(jnp.bfloat16)
    low = (value - high.astype(jnp.float32)).astype(jnp.bfloat16)
    return high, low


def term_weights(vectors):
    position = lax.broadcasted_iota(jnp.int32, (2 * vectors, 1), 0)
    first = (position == 0) | (position == vectors)
    return jnp.where(first, 0.5, -0.5 / (vectors - 1)).astype(jnp.float32)


def norm_rows(norms, first):
    high = norms.astype(jnp.bfloat16).astype(jnp.float32)
    rest = norms - high
    mid = rest.astype(jnp.bfloat16).astype(jnp.float32)
    row = lax.broadcasted_iota(jnp.int32, (NORM_ROWS, norms.shape[1]), 0)
    at, ones = (0, 3) if first else (3, 0)
    rows = jnp.where((row >= ones) & (row < ones + 3), 1.0, 0.0)
    for place, part in enumerate((high, mid, rest - mid)):
        rows = jnp.where(row == at + place, part, rows)
    return rows.astype(jnp.bfloat16)


def prepared_mine(block, width, vectors):
    feat = block[:width]
    scale = LOG2E / (2.0 * width)
    norms = jnp.sum(feat * feat, axis=0, keepdims=True) * -scale
    high, low = split2(feat * (2.0 * scale))
    dist = jnp.concatenate([high, low, high, norm_rows(norms, True)], 0)
    high, low = split2(block[width:] * term_weights(vectors))
    return dist, jnp.concatenate([high, low, high], 0)


def prepared_theirs(block, width, vectors):
    feat = block[:width]
    scale = LOG2E / (2.0 * width)
    norms = jnp.sum(feat * feat, axis=0, keepdims=True) * -scale
    high, low = split2(feat)
    dist = jnp.concatenate([high, high, low, norm_rows(norms, False)], 0)
    vecs = jnp.concatenate([block[width + vectors :], block[width : width + vectors]], 0)
    vec_high, vec_low = split2(vecs)
    pair = jnp.concatenate([vec_high, vec_high, vec_low], 0)
    ones = jnp.ones((ONES_ROWS, block.shape[1]), jnp.bfloat16)
    return dist.T, pair.T, jnp.concatenate([high, ones, low], 0)


def product(left, right):
    return jnp.dot(left, right, preferred_element_type=jnp.float32)


def pulled_terms(mine, theirs, width):
    dist_mine, pair_mine = mine
    dist_theirs, pair_theirs, pull = theirs
    coupling = jnp.exp2(product(dist_theirs, dist_mine)) * product(pair_theirs, pair_mine)
    high, low = split2(coupling)
    from_high = product(pull, high)
    from_low = product(pull[: width + ONES_ROWS], low)
    pulled = from_high[:width] + from_high[width + ONES_ROWS :] + from_low[:width]
    return pulled, from_high[width : width + 1] + from_low[width : width + 1]


def stacked(theirs):
    dist, pair, pull = zip(*theirs)
    return jnp.concatenate(dist, 0), jnp.concatenate(pair, 0), jnp.concatenate(pull, 1)


def kernel(width, vectors, jobs, count, pieces, *refs):
    blocks, refs = refs[:count], refs[count:]
    results = len(jobs) * pieces
    before, out = refs[:-results], refs[-results:]
    used = sorted({theirs for _, columns in jobs for theirs in columns})
    theirs = {place: prepared_theirs(blocks[place][...], width, vectors) for place in used}
    for place, (row, columns) in enumerate(jobs):
        mine = prepared_mine(blocks[row][...], width, vectors)
        parts = [
            pulled_terms(mine, stacked([theirs[column] for column in columns[at : at + STACK]]), width)
            for at in range(0, len(columns), STACK)
        ]
        pulled, sums = (sum(part) for part in zip(*parts))
        value = (pulled - blocks[row][:width] * sums) / width
        value = value + before[place][...] if place < len(before) else value
        rows = width // pieces
        for piece in range(pieces):
            out[place * pieces + piece][...] = value[piece * rows : (piece + 1) * rows]


def pair_terms(jobs, width, vectors, before=(), weight=2048, pieces=1):
    blocks = []

    def place(block):
        for index, other in enumerate(blocks):
            if other is block:
                return index
        blocks.append(block)
        return len(blocks) - 1

    placed = [(place(row), [place(column) for column in columns]) for row, columns in jobs]
    points = blocks[0].shape[1]
    operands = blocks + list(before)
    shape = jax.ShapeDtypeStruct((width // pieces, points), jnp.float32)
    out_shape = [shape] * (len(jobs) * pieces)
    return list(
        pl.pallas_call(
            functools.partial(kernel, width, vectors, placed, len(blocks), pieces),
            out_shape=out_shape,
            in_specs=[pl.BlockSpec(memory_space=pltpu.VMEM)] * len(operands),
            out_specs=[pl.BlockSpec(memory_space=pltpu.VMEM)] * len(out_shape),
            compiler_params=pltpu.CompilerParams(vmem_limit_bytes=VMEM_LIMIT),
            cost_estimate=pl.CostEstimate(
                flops=2 * points * points * weight * sum(len(columns) for _, columns in jobs),
                bytes_accessed=4 * points * 96 * len(operands),
                transcendentals=points * points,
            ),
        )(*operands)
    )


def packed(features, solves, probes):
    width, points = features.shape
    vectors = solves.shape[0]

    def body(features_ref, solves_ref, probes_ref, out_ref, vectors_ref):
        out_ref[:width] = features_ref[...]
        for first, ref in ((0, solves_ref), (vectors, probes_ref)):
            out_ref[width + first : width + first + vectors] = ref[...]
            vectors_ref[first : first + vectors] = ref[...]

    return pl.pallas_call(
        body,
        out_shape=[
            jax.ShapeDtypeStruct((rows, points), jnp.float32)
            for rows in (width + 2 * vectors, 2 * vectors)
        ],
        compiler_params=pltpu.CompilerParams(vmem_limit_bytes=60 << 20),
    )(features, solves, probes)


def local(features, solves, probes):
    width = features.shape[0]
    vectors = solves.shape[0]
    count = lax.axis_size("blk")
    terms = functools.partial(pair_terms, width=width, vectors=vectors)
    swap = lambda value, bit: swapped(value, "blk", bit)
    tied = lax.optimization_barrier

    bits = [1 << place for place in range(count.bit_length() - 1)]
    top, beside = bits[-1], [bit for bit in bits[:-1] if bit not in (1, 4)]
    far_features = swap(features, top)
    mine, my_vectors = packed(features, solves, probes)
    far_vectors = swap(my_vectors, top)
    sibling = swap(mine, 1)
    near = swap(mine, 4)
    direct = [swap(mine, bit) for bit in beside]

    (here,) = terms([(mine, [mine])], weight=64)
    far_features, far_vectors, here = tied((far_features, far_vectors, here))
    far = [far_features, far_vectors]
    last = []
    for bit in beside:
        for pair in [far] + last:
            last = last + [[swap(piece, bit) for piece in pair]]
    first = [jnp.concatenate(far, 0)] + direct
    (there,) = terms([(near, [mine, sibling] + first)], weight=2048)
    swapped_first = swap(jnp.concatenate(first, 0), 1)
    siblings = jnp.split(swapped_first, len(first), 0)
    (there,) = terms([(near, siblings)], before=[there], weight=64)
    *pieces, there = tied((*[piece for pair in last for piece in pair], there))
    last = [jnp.concatenate(pieces[at : at + 2], 0) for at in range(0, len(pieces), 2)]
    last_siblings = [swap(block, 1) for block in last]
    (there,) = terms([(near, last)], before=[there], weight=64)
    rest = [sibling] + first + siblings + last + last_siblings
    toward_near = terms([(near, last_siblings)], before=[there], weight=64, pieces=2)
    from_near = jnp.concatenate([swap(piece, 4) for piece in toward_near], 0)
    (here,) = terms([(mine, rest)], before=[here], weight=2048)
    return here + from_near


def solution(mesh):
    in_specs = (P(None, ("groups", "blk")), P(None, ("groups", "blk")), P(None, ("groups", "blk")))
    out_specs = P(None, ("groups", "blk"))
    return jax.shard_map(local, mesh=mesh, in_specs=in_specs, out_specs=out_specs, check_vma=False)
```

```python
import functools

import jax
import jax.numpy as jnp
from jax import lax
from jax.experimental import pallas as pl
from jax.experimental.pallas import tpu as pltpu
from jax.sharding import PartitionSpec as P

LOG2E = 1.4426950408889634
NORM_ROWS = 16
ONES_ROWS = 16
STACK = 4
VMEM_LIMIT = 24 << 20


def swapped(value, axis, bit):
    count = lax.axis_size(axis)
    return lax.ppermute(value, axis, [(source, source ^ bit) for source in range(count)])


def split2(value):
    high = value.astype(jnp.bfloat16)
    low = (value - high.astype(jnp.float32)).astype(jnp.bfloat16)
    return high, low


def term_weights(vectors):
    position = lax.broadcasted_iota(jnp.int32, (2 * vectors, 1), 0)
    first = (position == 0) | (position == vectors)
    return jnp.where(first, 0.5, -0.5 / (vectors - 1)).astype(jnp.float32)


def norm_rows(norms, first):
    high = norms.astype(jnp.bfloat16).astype(jnp.float32)
    rest = norms - high
    mid = rest.astype(jnp.bfloat16).astype(jnp.float32)
    row = lax.broadcasted_iota(jnp.int32, (NORM_ROWS, norms.shape[1]), 0)
    at, ones = (0, 3) if first else (3, 0)
    rows = jnp.where((row >= ones) & (row < ones + 3), 1.0, 0.0)
    for place, part in enumerate((high, mid, rest - mid)):
        rows = jnp.where(row == at + place, part, rows)
    return rows.astype(jnp.bfloat16)


def prepared_mine(block, width, vectors):
    feat = block[:width]
    scale = LOG2E / (2.0 * width)
    norms = jnp.sum(feat * feat, axis=0, keepdims=True) * -scale
    high, low = split2(feat * (2.0 * scale))
    dist = jnp.concatenate([high, low, high, norm_rows(norms, True)], 0)
    high, low = split2(block[width:] * term_weights(vectors))
    return dist, jnp.concatenate([high, low, high], 0)


def prepared_theirs(block, width, vectors):
    feat = block[:width]
    scale = LOG2E / (2.0 * width)
    norms = jnp.sum(feat * feat, axis=0, keepdims=True) * -scale
    high, low = split2(feat)
    dist = jnp.concatenate([high, high, low, norm_rows(norms, False)], 0)
    vecs = jnp.concatenate([block[width + vectors :], block[width : width + vectors]], 0)
    vec_high, vec_low = split2(vecs)
    pair = jnp.concatenate([vec_high, vec_high, vec_low], 0)
    ones = jnp.ones((ONES_ROWS, block.shape[1]), jnp.bfloat16)
    return dist.T, pair.T, jnp.concatenate([high, ones, low], 0)


def product(left, right):
    return jnp.dot(left, right, preferred_element_type=jnp.float32)


def pulled_terms(mine, theirs, width):
    dist_mine, pair_mine = mine
    dist_theirs, pair_theirs, pull = theirs
    coupling = jnp.exp2(product(dist_theirs, dist_mine)) * product(pair_theirs, pair_mine)
    high, low = split2(coupling)
    from_high = product(pull, high)
    from_low = product(pull[: width + ONES_ROWS], low)
    pulled = from_high[:width] + from_high[width + ONES_ROWS :] + from_low[:width]
    return pulled, from_high[width : width + 1] + from_low[width : width + 1]


def stacked(theirs):
    dist, pair, pull = zip(*theirs)
    return jnp.concatenate(dist, 0), jnp.concatenate(pair, 0), jnp.concatenate(pull, 1)


def kernel(width, vectors, jobs, count, pieces, *refs):
    blocks, refs = refs[:count], refs[count:]
    results = len(jobs) * pieces
    before, out = refs[:-results], refs[-results:]
    used = sorted({theirs for _, columns in jobs for theirs in columns})
    theirs = {place: prepared_theirs(blocks[place][...], width, vectors) for place in used}
    for place, (row, columns) in enumerate(jobs):
        mine = prepared_mine(blocks[row][...], width, vectors)
        parts = [
            pulled_terms(mine, stacked([theirs[column] for column in columns[at : at + STACK]]), width)
            for at in range(0, len(columns), STACK)
        ]
        pulled, sums = (sum(part) for part in zip(*parts))
        value = (pulled - blocks[row][:width] * sums) / width
        value = value + before[place][...] if place < len(before) else value
        rows = width // pieces
        for piece in range(pieces):
            out[place * pieces + piece][...] = value[piece * rows : (piece + 1) * rows]


def pair_terms(jobs, width, vectors, before=(), weight=2048, pieces=1):
    blocks = []

    def place(block):
        for index, other in enumerate(blocks):
            if other is block:
                return index
        blocks.append(block)
        return len(blocks) - 1

    placed = [(place(row), [place(column) for column in columns]) for row, columns in jobs]
    points = blocks[0].shape[1]
    operands = blocks + list(before)
    shape = jax.ShapeDtypeStruct((width // pieces, points), jnp.float32)
    out_shape = [shape] * (len(jobs) * pieces)
    return list(
        pl.pallas_call(
            functools.partial(kernel, width, vectors, placed, len(blocks), pieces),
            out_shape=out_shape,
            in_specs=[pl.BlockSpec(memory_space=pltpu.VMEM)] * len(operands),
            out_specs=[pl.BlockSpec(memory_space=pltpu.VMEM)] * len(out_shape),
            compiler_params=pltpu.CompilerParams(vmem_limit_bytes=VMEM_LIMIT),
            cost_estimate=pl.CostEstimate(
                flops=2 * points * points * weight * sum(len(columns) for _, columns in jobs),
                bytes_accessed=4 * points * 96 * len(operands),
                transcendentals=points * points,
            ),
        )(*operands)
    )


def packed(features, solves, probes):
    width, points = features.shape
    vectors = solves.shape[0]

    def body(features_ref, solves_ref, probes_ref, out_ref, vectors_ref):
        out_ref[:width] = features_ref[...]
        for first, ref in ((0, solves_ref), (vectors, probes_ref)):
            out_ref[width + first : width + first + vectors] = ref[...]
            vectors_ref[first : first + vectors] = ref[...]

    return pl.pallas_call(
        body,
        out_shape=[
            jax.ShapeDtypeStruct((rows, points), jnp.float32)
            for rows in (width + 2 * vectors, 2 * vectors)
        ],
        compiler_params=pltpu.CompilerParams(vmem_limit_bytes=60 << 20),
    )(features, solves, probes)


def local(features, solves, probes):
    width = features.shape[0]
    vectors = solves.shape[0]
    count = lax.axis_size("blk")
    terms = functools.partial(pair_terms, width=width, vectors=vectors)
    swap = lambda value, bit: swapped(value, "blk", bit)
    tied = lax.optimization_barrier

    bits = [1 << place for place in range(count.bit_length() - 1)]
    top, beside = bits[-1], [bit for bit in bits[:-1] if bit not in (1, 4)]
    far_features = swap(features, top)
    mine, my_vectors = packed(features, solves, probes)
    far_vectors = swap(my_vectors, top)
    sibling = swap(mine, 1)
    near = swap(mine, 4)
    direct = [swap(mine, bit) for bit in beside]

    (here,) = terms([(mine, [mine])], weight=64)
    far_features, far_vectors, here = tied((far_features, far_vectors, here))
    far = [far_features, far_vectors]
    last = []
    for bit in beside:
        for pair in [far] + last:
            last = last + [[swap(piece, bit) for piece in pair]]
    first = [jnp.concatenate(far, 0)] + direct
    (there,) = terms([(near, [mine, sibling] + first)], weight=2048)
    swapped_first = swap(jnp.concatenate(first, 0), 1)
    siblings = jnp.split(swapped_first, len(first), 0)
    (there,) = terms([(near, siblings)], before=[there], weight=64)
    *pieces, there = tied((*[piece for pair in last for piece in pair], there))
    last = [jnp.concatenate(pieces[at : at + 2], 0) for at in range(0, len(pieces), 2)]
    last_siblings = [swap(block, 1) for block in last]
    (there,) = terms([(near, last)], before=[there], weight=64)
    rest = [sibling] + first + siblings + last + last_siblings
    toward_near = terms([(near, last_siblings)], before=[there], weight=64)
    from_near = swap(toward_near[0], 4)
    (here,) = terms([(mine, rest)], before=[here], weight=2048)
    return here + from_near


def solution(mesh):
    in_specs = (P(None, ("groups", "blk")), P(None, ("groups", "blk")), P(None, ("groups", "blk")))
    out_specs = P(None, ("groups", "blk"))
    return jax.shard_map(local, mesh=mesh, in_specs=in_specs, out_specs=out_specs, check_vma=False)
```

```python
import functools

import jax
import jax.numpy as jnp
from jax import lax
from jax.experimental import pallas as pl
from jax.experimental.pallas import tpu as pltpu
from jax.sharding import PartitionSpec as P

LOG2E = 1.4426950408889634
NORM_ROWS = 16
ONES_ROWS = 16
STACK = 7
VMEM_LIMIT = 24 << 20


def swapped(value, axis, bit):
    count = lax.axis_size(axis)
    return lax.ppermute(value, axis, [(source, source ^ bit) for source in range(count)])


def split2(value):
    high = value.astype(jnp.bfloat16)
    low = (value - high.astype(jnp.float32)).astype(jnp.bfloat16)
    return high, low


def term_weights(vectors):
    position = lax.broadcasted_iota(jnp.int32, (2 * vectors, 1), 0)
    first = (position == 0) | (position == vectors)
    return jnp.where(first, 0.5, -0.5 / (vectors - 1)).astype(jnp.float32)


def norm_rows(norms, first):
    high = norms.astype(jnp.bfloat16).astype(jnp.float32)
    rest = norms - high
    mid = rest.astype(jnp.bfloat16).astype(jnp.float32)
    row = lax.broadcasted_iota(jnp.int32, (NORM_ROWS, norms.shape[1]), 0)
    at, ones = (0, 3) if first else (3, 0)
    rows = jnp.where((row >= ones) & (row < ones + 3), 1.0, 0.0)
    for place, part in enumerate((high, mid, rest - mid)):
        rows = jnp.where(row == at + place, part, rows)
    return rows.astype(jnp.bfloat16)


def prepared_mine(block, width, vectors):
    feat = block[:width]
    scale = LOG2E / (2.0 * width)
    norms = jnp.sum(feat * feat, axis=0, keepdims=True) * -scale
    high, low = split2(feat * (2.0 * scale))
    dist = jnp.concatenate([high, low, high, norm_rows(norms, True)], 0)
    high, low = split2(block[width:] * term_weights(vectors))
    return dist, jnp.concatenate([high, low, high], 0)


def prepared_theirs(block, width, vectors):
    feat = block[:width]
    scale = LOG2E / (2.0 * width)
    norms = jnp.sum(feat * feat, axis=0, keepdims=True) * -scale
    high, low = split2(feat)
    dist = jnp.concatenate([high, high, low, norm_rows(norms, False)], 0)
    vecs = jnp.concatenate([block[width + vectors :], block[width : width + vectors]], 0)
    vec_high, vec_low = split2(vecs)
    pair = jnp.concatenate([vec_high, vec_high, vec_low], 0)
    ones = jnp.ones((ONES_ROWS, block.shape[1]), jnp.bfloat16)
    return dist.T, pair.T, jnp.concatenate([high, ones, low], 0)


def product(left, right):
    return jnp.dot(left, right, preferred_element_type=jnp.float32)


def pulled_terms(mine, theirs, width):
    dist_mine, pair_mine = mine
    dist_theirs, pair_theirs, pull = theirs
    coupling = jnp.exp2(product(dist_theirs, dist_mine)) * product(pair_theirs, pair_mine)
    high, low = split2(coupling)
    from_high = product(pull, high)
    from_low = product(pull[: width + ONES_ROWS], low)
    pulled = from_high[:width] + from_high[width + ONES_ROWS :] + from_low[:width]
    return pulled, from_high[width : width + 1] + from_low[width : width + 1]


def stacked(theirs):
    dist, pair, pull = zip(*theirs)
    return jnp.concatenate(dist, 0), jnp.concatenate(pair, 0), jnp.concatenate(pull, 1)


def kernel(width, vectors, jobs, count, pieces, *refs):
    blocks, refs = refs[:count], refs[count:]
    results = len(jobs) * pieces
    before, out = refs[:-results], refs[-results:]
    used = sorted({theirs for _, columns in jobs for theirs in columns})
    theirs = {place: prepared_theirs(blocks[place][...], width, vectors) for place in used}
    for place, (row, columns) in enumerate(jobs):
        mine = prepared_mine(blocks[row][...], width, vectors)
        parts = [
            pulled_terms(mine, stacked([theirs[column] for column in columns[at : at + STACK]]), width)
            for at in range(0, len(columns), STACK)
        ]
        pulled, sums = (sum(part) for part in zip(*parts))
        value = (pulled - blocks[row][:width] * sums) / width
        value = value + before[place][...] if place < len(before) else value
        rows = width // pieces
        for piece in range(pieces):
            out[place * pieces + piece][...] = value[piece * rows : (piece + 1) * rows]


def pair_terms(jobs, width, vectors, before=(), weight=2048, pieces=1):
    blocks = []

    def place(block):
        for index, other in enumerate(blocks):
            if other is block:
                return index
        blocks.append(block)
        return len(blocks) - 1

    placed = [(place(row), [place(column) for column in columns]) for row, columns in jobs]
    points = blocks[0].shape[1]
    operands = blocks + list(before)
    shape = jax.ShapeDtypeStruct((width // pieces, points), jnp.float32)
    out_shape = [shape] * (len(jobs) * pieces)
    return list(
        pl.pallas_call(
            functools.partial(kernel, width, vectors, placed, len(blocks), pieces),
            out_shape=out_shape,
            in_specs=[pl.BlockSpec(memory_space=pltpu.VMEM)] * len(operands),
            out_specs=[pl.BlockSpec(memory_space=pltpu.VMEM)] * len(out_shape),
            compiler_params=pltpu.CompilerParams(vmem_limit_bytes=VMEM_LIMIT),
            cost_estimate=pl.CostEstimate(
                flops=2 * points * points * weight * sum(len(columns) for _, columns in jobs),
                bytes_accessed=4 * points * 96 * len(operands),
                transcendentals=points * points,
            ),
        )(*operands)
    )


def packed(features, solves, probes):
    width, points = features.shape
    vectors = solves.shape[0]

    def body(features_ref, solves_ref, probes_ref, out_ref, vectors_ref):
        out_ref[:width] = features_ref[...]
        for first, ref in ((0, solves_ref), (vectors, probes_ref)):
            out_ref[width + first : width + first + vectors] = ref[...]
            vectors_ref[first : first + vectors] = ref[...]

    return pl.pallas_call(
        body,
        out_shape=[
            jax.ShapeDtypeStruct((rows, points), jnp.float32)
            for rows in (width + 2 * vectors, 2 * vectors)
        ],
        compiler_params=pltpu.CompilerParams(vmem_limit_bytes=60 << 20),
    )(features, solves, probes)


def local(features, solves, probes):
    width = features.shape[0]
    vectors = solves.shape[0]
    count = lax.axis_size("blk")
    terms = functools.partial(pair_terms, width=width, vectors=vectors)
    swap = lambda value, bit: swapped(value, "blk", bit)
    tied = lax.optimization_barrier

    bits = [1 << place for place in range(count.bit_length() - 1)]
    top, beside = bits[-1], [bit for bit in bits[:-1] if bit not in (1, 4)]
    far_features = swap(features, top)
    mine, my_vectors = packed(features, solves, probes)
    far_vectors = swap(my_vectors, top)
    sibling = swap(mine, 1)
    near = swap(mine, 4)
    direct = [swap(mine, bit) for bit in beside]

    (here,) = terms([(mine, [mine])], weight=64)
    far_features, far_vectors, here = tied((far_features, far_vectors, here))
    far = [far_features, far_vectors]
    last = []
    for bit in beside:
        for pair in [far] + last:
            last = last + [[swap(piece, bit) for piece in pair]]
    first = [jnp.concatenate(far, 0)] + direct
    (there,) = terms([(near, [mine, sibling] + first)], weight=2048)
    swapped_first = swap(jnp.concatenate(first, 0), 1)
    siblings = jnp.split(swapped_first, len(first), 0)
    (there,) = terms([(near, siblings)], before=[there], weight=64)
    *pieces, there = tied((*[piece for pair in last for piece in pair], there))
    last = [jnp.concatenate(pieces[at : at + 2], 0) for at in range(0, len(pieces), 2)]
    last_siblings = [swap(block, 1) for block in last]
    (there,) = terms([(near, last)], before=[there], weight=64)
    rest = [sibling] + first + siblings + last + last_siblings
    toward_near = terms([(near, last_siblings)], before=[there], weight=64)
    from_near = swap(toward_near[0], 4)
    (here,) = terms([(mine, rest)], before=[here], weight=2048)
    return here + from_near


def solution(mesh):
    in_specs = (P(None, ("groups", "blk")), P(None, ("groups", "blk")), P(None, ("groups", "blk")))
    out_specs = P(None, ("groups", "blk"))
    return jax.shard_map(local, mesh=mesh, in_specs=in_specs, out_specs=out_specs, check_vma=False)
```
